32 devices in a mesh: fsdp: 8 (over z, core), cp: 4 (over y, x).
Axes of the slice: x: 2, y: 2, z: 4, core: 2. Of those that a mesh axis runs over, the one named last changes fastest.
Arguments:
- layer_input: bfloat16 [16, 4, 2, 128, 1536], P('fsdp', 'cp'), may hold values from -6 to 6
- cotangent: bfloat16 [16, 4, 2, 128, 1536], P('fsdp', 'cp'), may hold values from -6 to 6
- pairing: int32 [16, 4], P('fsdp'), may hold values from 0 to 3, each once within a row
- routes: int32 [16, 4, 2, 128, 2], P('fsdp', 'cp'), may hold values from 0 to 15, all different within a row; in each aligned block of 256 rows (0 to 255, 256 to 511, ..., all dimensions but the last counted through in order) at most 48 rows name the same one
- first_gain: bfloat16 [1536], P(('fsdp', 'cp')), may hold values from 0.5 to 1.5
- second_gain: bfloat16 [1536], P(('fsdp', 'cp')), may hold values from 0.5 to 1.5
- query_weight: bfloat16 [1536, 1536], P(('fsdp', 'cp')), may hold values from -0.15625 to 0.15625
- key_weight: bfloat16 [1536, 512], P(('fsdp', 'cp')), may hold values from -0.15625 to 0.15625
- value_weight: bfloat16 [1536, 512], P(('fsdp', 'cp')), may hold values from -0.15625 to 0.15625
- out_weight: bfloat16 [1536, 1536], P(('fsdp', 'cp')), may hold values from -1.75 to 1.75
- router_weight: bfloat16 [1536, 16], P(('fsdp', 'cp')), may hold values from -0.109375 to 0.109375
- gate_weight: bfloat16 [16, 1536, 1024], P('cp', 'fsdp'), may hold values from -0.15625 to 0.15625
- up_weight: bfloat16 [16, 1536, 1024], P('cp', 'fsdp'), may hold values from -0.15625 to 0.15625
- down_weight: bfloat16 [16, 1024, 1536], P('cp', 'fsdp'), may hold values from -0.375 to 0.375
Outputs:
- layer_output: bfloat16 [16, 4, 2, 128, 1536], P('fsdp', 'cp')
- input_grad: float32 [16, 4, 2, 128, 1536], P('fsdp', 'cp')
- first_gain_grad: float32 [1536], P(('fsdp', 'cp'))
- second_gain_grad: float32 [1536], P(('fsdp', 'cp'))
- query_grad: float32 [1536, 1536], P(('fsdp', 'cp'))
- key_grad: float32 [1536, 512], P(('fsdp', 'cp'))
- value_grad: float32 [1536, 512], P(('fsdp', 'cp'))
- out_grad: float32 [1536, 1536], P(('fsdp', 'cp'))
- router_grad: float32 [1536, 16], P(('fsdp', 'cp'))
- gate_grad: float32 [16, 1536, 1024], P('cp', 'fsdp')
- up_grad: float32 [16, 1536, 1024], P('cp', 'fsdp')
- down_grad: float32 [16, 1024, 1536], P('cp', 'fsdp')
The draws below stay inside these ranges and needn't reach their ends.
Inputs may be any that keep to these rules, and one draw needn't show every extreme that they name: Each row is a permutation of the indices of cp; index c of cp holds block pairing[s, c] and block 7 - pairing[s, c] of sequence s. `routes`: the two experts of a token differ. Among the 256 tokens that one index of cp holds of one sequence, no expert is named more than 48 times, a bound that some block reaches.
All inputs are finite; a program needn't handle non-finite values.
Results may differ from the reference program's by a relative error of at most 0.018.
Values may be sent and summed in bfloat16 or wider, within the bound.
A program may use at most 384 MiB of HBM per device.

```python
import math
import jax
import jax.numpy as jnp
import numpy as np
from jax import lax

D = 1536
H = 24
KV = 8
HD = 64
FF = 1024
EXPERTS = 16
TOP = 2
BLK = 128
SEQ_LEN = 1024
SEQS = 16
CAP = 48
N_CP = 4


def block_scale(key, extent, shards, least, largest):
    level = 1.0
    for dim, blocks in shards:
        steps = jax.random.uniform(jax.random.fold_in(jax.random.fold_in(key, 6), dim), (blocks,), jnp.float32, least / len(shards), largest / len(shards))
        level = level * jnp.repeat(jnp.exp(steps), extent[dim] // blocks).reshape((-1,) + (1,) * (len(extent) - 1 - dim))
    return level


def assign_block(key, own, number, rows, amount, top, reach, skew):
    ranking = jax.random.permutation(key, amount)
    heavy_load, common = load_shares(amount, rows * top, reach, skew, True), load_shares(amount, rows * top, reach, skew, False)
    places = jnp.arange(amount)

    def named(sizes, offset_by):
        used = int((sizes > 0).sum())
        fixed = max(1, used // 4)
        moved = fixed + (places - fixed + offset_by * (used - fixed)) % max(1, amount - fixed)
        return jnp.zeros((amount,), jnp.int32).at[ranking[jnp.where(places < fixed, places, moved)]].set(jnp.asarray(sizes, jnp.int32))

    sizes = jnp.where(number % 4 == 0, named(heavy_load, number // 4), named(common, number - number // 4 - 1))
    mixed = jax.random.permutation(jax.random.fold_in(own, 3), amount)
    giver, receiver = mixed[0:amount // 2 * 2:2], mixed[1:amount // 2 * 2:2]
    margin = jnp.minimum(sizes[giver] - 1, reach - sizes[receiver]) // 2
    margin = jnp.where((giver == ranking[0]) | (receiver == ranking[0]) | (sizes[receiver] == 0), 0, jnp.maximum(margin, 0))
    moved = jax.random.randint(jax.random.fold_in(own, 4), (amount // 2,), 0, 1 << 20) % (margin + 1)
    sizes = sizes.at[giver].add(-moved).at[receiver].add(moved)
    labels = jnp.searchsorted(jnp.cumsum(sizes), jnp.arange(rows * top), side="right").astype(jnp.int32)
    table = labels.reshape(top, rows).T
    table = table[jax.random.permutation(jax.random.fold_in(own, 1), rows)]
    offset_by = jax.random.randint(jax.random.fold_in(own, 2), (rows, 1), 0, top)
    return jnp.take_along_axis(table, (jnp.arange(top)[None, :] + offset_by) % top, axis=1)


def load_shares(count, total, most, slope, full):
    loads = [(1 << 20) // math.isqrt(standing ** slope) + 1 for standing in range(1, count + 1)]
    largest = most if full else min(most, max(-(-total // count), total * loads[0] // sum(loads)))
    least = 1 if total - largest >= count - 1 else 0
    counts, surplus = [largest] + [least] * (count - 1), total - largest - least * (count - 1)
    while surplus > 0:
        free = [i for i in range(1, count) if counts[i] < largest] or [i for i in range(1, count) if counts[i] < most]
        pool, budget = sum([loads[i] for i in free]), surplus
        for i in free:
            more = min(most - counts[i], max(1, budget * loads[i] // pool), surplus)
            counts[i] = counts[i] + more
            surplus = surplus - more
    return np.array(counts)


def gaussian(stream_key, shape, deviation, reach, cuts=(), kind=jnp.bfloat16):
    level = block_scale(stream_key, shape, cuts, -0.22, 0.18) if cuts else 1.0
    result = jax.random.normal(stream_key, shape, jnp.float32) * deviation * level
    return jnp.minimum(jnp.maximum(result, -reach), reach).astype(kind)


def setup_inputs(seed: int = 0) -> dict:
    splits = jax.random.split(jax.random.key(seed), 15)
    layer_input = gaussian(splits[0], (SEQS, N_CP, 2, BLK, D), 1.0, 6.0, ((0, 8), (1, 4)))
    cotangent = gaussian(splits[1], (SEQS, N_CP, 2, BLK, D), 1.0, 6.0, ((0, 8), (1, 4)))
    pairing = jax.vmap(lambda own: jax.random.permutation(own, N_CP))(jax.random.split(splits[2], SEQS)).reshape((SEQS, N_CP)).astype(jnp.int32)
    routes_keys = jax.random.split(jax.random.fold_in(splits[3], 1), SEQS * N_CP * 2 * BLK // (2 * BLK))
    routes_turns = jax.random.permutation(jax.random.fold_in(splits[3], 3), SEQS * N_CP * 2 * BLK // (2 * BLK))
    routes = jax.vmap(lambda own, number: assign_block(jax.random.fold_in(splits[3], 2), own, number, 2 * BLK, EXPERTS, TOP, CAP, 1))(routes_keys, routes_turns).reshape((SEQS, N_CP, 2, BLK, TOP))
    first_gain = jnp.clip(1.0 + 0.1 * jax.random.normal(splits[4], (D,), jnp.float32), 0.5, 1.5).astype(jnp.bfloat16)
    second_gain = jnp.clip(1.0 + 0.1 * jax.random.normal(splits[5], (D,), jnp.float32), 0.5, 1.5).astype(jnp.bfloat16)
    query_weight = gaussian(splits[6], (D, H * HD), D ** -0.5, 0.15625, ((0, 32),))
    key_weight = gaussian(splits[7], (D, KV * HD), D ** -0.5, 0.15625, ((0, 32),))
    value_weight = gaussian(splits[8], (D, KV * HD), D ** -0.5, 0.15625, ((0, 32),))
    out_weight = gaussian(splits[9], (H * HD, D), (max(1, 8 * H * HD // SEQ_LEN)) ** -0.5, 1.75, ((0, 32),))
    router_weight = gaussian(splits[10], (D, EXPERTS), (2 * D) ** -0.5, 0.109375, ((0, 32),))
    gate_weight = gaussian(splits[11], (EXPERTS, D, FF), D ** -0.5, 0.15625, ((0, 4), (1, 8)))
    up_weight = gaussian(splits[12], (EXPERTS, D, FF), D ** -0.5, 0.15625, ((0, 4), (1, 8)))
    down_weight = gaussian(splits[13], (EXPERTS, FF, D), (FF // 4) ** -0.5, 0.375, ((0, 4), (1, 8)))
    return dict(layer_input=layer_input, cotangent=cotangent, pairing=pairing, routes=routes, first_gain=first_gain, second_gain=second_gain, query_weight=query_weight, key_weight=key_weight, value_weight=value_weight, out_weight=out_weight, router_weight=router_weight, gate_weight=gate_weight, up_weight=up_weight, down_weight=down_weight)


@jax.custom_vjp
def low(v):
    return lax.optimization_barrier(v.astype(jnp.bfloat16)).astype(jnp.float32)

@jax.custom_vjp
def low_back(v):
    return v

def low_keep(v):
    return (low(v), None)

def low_pass(kept, grad):
    return (grad,)

def back_keep(v):
    return (v, None)

def back_low(kept, grad):
    return (low(grad),)
low.defvjp(low_keep, low_pass)
low_back.defvjp(back_keep, back_low)
HIGH = lax.Precision.HIGHEST
EPS = 1e-05
NEG = -1e+30

def matmul(left, right):
    return jnp.dot(left, right, precision=HIGH)

def rms_norm(rows, gain):
    return rows * lax.rsqrt(lax.optimization_barrier(jnp.mean(rows * rows, axis=-1, keepdims=True)) + EPS) * gain

def sequence_forward(params, source, pair_row, route_rows):
    gain_one, gain_two, query_matrix, key_matrix, value_matrix, out_matrix, router_matrix, gate_matrix, up_matrix, down_matrix = params
    group = H // KV
    scale = HD ** (-0.5)
    resid = source.reshape(SEQ_LEN, D)
    blocks = jnp.stack([pair_row, 2 * N_CP - 1 - pair_row], axis=1)
    places = (blocks[:, :, None] * BLK + jnp.arange(BLK, dtype=jnp.int32)[None, None, :]).reshape(SEQ_LEN)
    attn_in = low(rms_norm(resid, gain_one))
    queries = low(low_back(matmul(attn_in, query_matrix)))
    keys = low(low_back(matmul(attn_in, key_matrix)))
    values = low(low_back(matmul(attn_in, value_matrix)))
    span = min(512, SEQ_LEN)
    query_blocks = queries.reshape(SEQ_LEN // span, span, KV, group, HD)
    place_blocks = places.reshape(SEQ_LEN // span, span)
    key_groups = keys.reshape(SEQ_LEN, KV, HD)
    value_groups = values.reshape(SEQ_LEN, KV, HD)

    def attend(operands):
        query_block, place_block = operands
        scores = low_back(jnp.einsum('rkgd,lkd->kgrl', query_block, key_groups, precision=HIGH) * scale)
        allowed = places[None, :] <= place_block[:, None]
        scores = jnp.where(allowed[None, None], scores, NEG)
        peak = lax.optimization_barrier(jnp.max(scores, axis=-1, keepdims=True))
        powers = jnp.exp(scores - peak)
        probs = low(powers / lax.optimization_barrier(jnp.sum(powers, axis=-1, keepdims=True)))
        mixed = jnp.einsum('kgrl,lkd->rkgd', probs, value_groups, precision=HIGH)
        return mixed.reshape(span, H * HD)
    mixed = lax.map(jax.checkpoint(attend), (query_blocks, place_blocks)).reshape(SEQ_LEN, H * HD)
    attn_out = low(low_back(mixed))
    middle = resid + low_back(matmul(attn_out, out_matrix))
    moe_in = low(rms_norm(middle, gain_two))
    logits = matmul(moe_in, router_matrix)
    chosen = route_rows.reshape(SEQ_LEN, 2)
    picks = (chosen[:, :, None] == jnp.arange(EXPERTS, dtype=jnp.int32)[None, None, :]).astype(jnp.float32)
    picked = lax.optimization_barrier(jnp.sum(picks * logits[:, None, :], axis=-1))
    top = lax.optimization_barrier(jnp.max(picked, axis=-1, keepdims=True))
    powers = jnp.exp(picked - top)
    gates = powers / lax.optimization_barrier(jnp.sum(powers, axis=-1, keepdims=True))
    flat = route_rows.reshape(N_CP, 4 * BLK)
    onehot = (flat[:, :, None] == jnp.arange(EXPERTS, dtype=jnp.int32)[None, None, :]).astype(jnp.int32)
    rank = lax.optimization_barrier(jnp.sum((jnp.cumsum(onehot, axis=1) - onehot) * onehot, axis=2))
    device = jnp.arange(N_CP, dtype=jnp.int32)[:, None]
    slots = (flat * (N_CP * CAP) + device * CAP + rank).reshape(2 * SEQ_LEN).astype(jnp.int32)
    routed = low_back(jnp.repeat(moe_in, 2, axis=0))
    buffer = jnp.zeros((EXPERTS * N_CP * CAP, D), jnp.float32).at[slots].add(routed).reshape(EXPERTS, N_CP * CAP, D)
    gate_pre = low_back(jnp.einsum('ecd,edf->ecf', buffer, gate_matrix, precision=HIGH))
    up_pre = low_back(jnp.einsum('ecd,edf->ecf', buffer, up_matrix, precision=HIGH))
    hidden = low(gate_pre * jax.nn.sigmoid(gate_pre) * up_pre)
    produced = low(low_back(jnp.einsum('ecf,efd->ecd', hidden, down_matrix, precision=HIGH)))
    back_rows = produced.reshape(EXPERTS * N_CP * CAP, D)[slots].reshape(SEQ_LEN, 2, D)
    return middle + lax.optimization_barrier(jnp.sum(gates[:, :, None] * back_rows, axis=1))

def reference(layer_input, cotangent, pairing, routes, first_gain, second_gain, query_weight, key_weight, value_weight, out_weight, router_weight, gate_weight, up_weight, down_weight):
    params = jax.tree.map(lambda leaf: leaf.astype(jnp.float32), (first_gain, second_gain, query_weight, key_weight, value_weight, out_weight, router_weight, gate_weight, up_weight, down_weight))
    zeros = jax.tree.map(jnp.zeros_like, params)

    def one_sequence(totals, inputs):
        source, grad_out, pair_row, route_rows = inputs

        def forward(params_now, source_now):
            return sequence_forward(params_now, source_now, pair_row, route_rows)
        final, pullback = jax.vjp(forward, params, source.astype(jnp.float32))
        grads, source_grad = pullback(grad_out.astype(jnp.float32).reshape(final.shape))
        totals = jax.tree.map(jnp.add, totals, grads)
        return (totals, (final.astype(jnp.bfloat16).reshape(source.shape), source_grad))
    totals, (outputs, input_grad) = lax.scan(one_sequence, zeros, (layer_input, cotangent, pairing, routes))
    return (outputs, input_grad, totals[0], totals[1], totals[2], totals[3], totals[4], totals[5], totals[6], totals[7], totals[8], totals[9])
```

```python
import functools

import jax
import jax.numpy as jnp
from jax import lax
from jax.experimental import pallas as pl
from jax.experimental.pallas import tpu as pltpu
from jax.sharding import Mesh, PartitionSpec as P

H = 24
KV = 8
HD = 64
EXPERTS = 16
BLK = 128
CAP = 48
EPS = 1e-05
NEG = -1e30
GROUP = H // KV
SCALE = HD ** (-0.5)
PACK = 2
HIGH = lax.Precision.HIGHEST
F32 = jnp.float32
BF16 = jnp.bfloat16
DENSE = ("hi", "ep", "cp")


def dot(a, b, ca=1, cb=0):
    return lax.dot_general(a, b, (((ca,), (cb,)), ((), ())), preferred_element_type=F32)


def sort_blocks(table, seq, src, dst, which, blocks):
    for b in range(blocks):
        at = table[seq, b]
        dst[pl.ds(b * BLK, BLK), :] = src[at // 2, 0, which, pl.ds((at % 2) * BLK, BLK), :]


def stack_heads(rows, first, scale=None):
    parts = [
        rows[half * BLK : (half + 1) * BLK, (first + i) * HD : (first + i + 1) * HD]
        for half in range(2)
        for i in range(GROUP)
    ]
    out = jnp.concatenate(parts, axis=0)
    return out if scale is None else out * jnp.asarray(scale, out.dtype)


def unstack_heads(low, high):
    rows = []
    for pieces in (low, high):
        heads = [p[i * BLK : (i + 1) * BLK] for p in pieces for i in range(GROUP)]
        rows.append(jnp.concatenate(heads, axis=1))
    return jnp.concatenate(rows, axis=0)


def attend_kernel(table, place, q_ref, kv_ref, o_ref, k_s, v_s, low_bias, high_bias):
    seq = pl.program_id(0)
    blocks = 2 * kv_ref.shape[0]
    half = blocks * BLK // 2
    rows = GROUP * BLK
    at = place[seq]

    @pl.when(pl.program_id(1) == 0)
    def _():
        query = lax.broadcasted_iota(jnp.int32, (BLK, half), 0)
        key = lax.broadcasted_iota(jnp.int32, (BLK, half), 1)
        low_bias[...] = jnp.where(key <= query + at * BLK, 0.0, NEG)
        high_bias[...] = jnp.where(key + half <= query + (blocks - 1 - at) * BLK, 0.0, NEG)

    sort_blocks(table, seq, kv_ref, k_s, 0, blocks)
    sort_blocks(table, seq, kv_ref, v_s, 1, blocks)
    q_all = q_ref[...]
    lows, highs = [], []
    for j in range(PACK):
        k = k_s[:, j * HD : (j + 1) * HD]
        v = v_s[:, j * HD : (j + 1) * HD]
        q = stack_heads(q_all, j * GROUP, SCALE)
        s_low = dot(q[:rows], k[:half], 1, 1) + jnp.concatenate([low_bias[...]] * GROUP, axis=0)
        peak = jnp.max(s_low, axis=-1, keepdims=True)
        e_low = jnp.exp(s_low - peak)
        total = jnp.sum(e_low, axis=-1, keepdims=True)
        lows.append((dot(e_low.astype(BF16), v[:half]) / total).astype(BF16))
        s_one = dot(q[rows:], k[:half], 1, 1)
        s_two = dot(q[rows:], k[half:], 1, 1) + jnp.concatenate([high_bias[...]] * GROUP, axis=0)
        peak = jnp.maximum(
            jnp.max(s_one, axis=-1, keepdims=True), jnp.max(s_two, axis=-1, keepdims=True)
        )
        e_one = jnp.exp(s_one - peak)
        e_two = jnp.exp(s_two - peak)
        total = jnp.sum(e_one, axis=-1, keepdims=True) + jnp.sum(e_two, axis=-1, keepdims=True)
        mixed = dot(e_one.astype(BF16), v[:half]) + dot(e_two.astype(BF16), v[half:])
        highs.append((mixed / total).astype(BF16))
    o_ref[...] = unstack_heads(lows, highs)


def attend_back_kernel(
    sizes, kinds, table, inverse, place, q_ref, kv_ref, g_ref, *refs
):
    n = len(kinds)
    ins, dq_ref, dkv_ref, outs = refs[:n], refs[n], refs[n + 1], refs[n + 2 : 2 * n + 2]
    k_s, v_s, low_bias, high_bias, parts = refs[2 * n + 2 : 2 * n + 7]
    post_sems = refs[2 * n + 7 : 2 * n + 10]
    step_send, step_recv, step_here = refs[2 * n + 10 :]
    cp = sizes[2]
    my_cp = lax.axis_index("cp")
    groups = KV // PACK
    step = pl.program_id(0) * groups + pl.program_id(1)
    last = pl.num_programs(0) * groups - 1
    office = PostOffice(sizes, post_sems)

    @pl.when(step == 0)
    def _():
        office.greet(kinds)
        office.begin(kinds, ins, outs)

    def step_copy(at_seq, at_group, at_step, m):
        columns = pl.ds(pl.multiple_of(at_group * PACK * HD, PACK * HD), PACK * HD)
        to = lax.rem(my_cp + m, cp)
        return mesh_copy(
            parts.at[at_step, to],
            dkv_ref.at[my_cp, at_seq, :, :, columns],
            (step_send, step_recv),
            at_step * (cp - 1) + m - 1,
            {"cp": to},
        )

    def own_copy(at_seq, at_group, at_step):
        columns = pl.ds(pl.multiple_of(at_group * PACK * HD, PACK * HD), PACK * HD)
        return pltpu.make_async_copy(
            parts.at[at_step, my_cp], dkv_ref.at[my_cp, at_seq, :, :, columns], step_here.at[at_step]
        )

    seq = pl.program_id(0)
    blocks = 2 * kv_ref.shape[0]
    half = blocks * BLK // 2
    rows = GROUP * BLK
    at = place[seq]

    @pl.when(pl.program_id(1) == 0)
    def _():
        key = lax.broadcasted_iota(jnp.int32, (half, BLK), 0)
        query = lax.broadcasted_iota(jnp.int32, (half, BLK), 1)
        low_bias[...] = jnp.where(key <= query + at * BLK, 0.0, NEG)
        high_bias[...] = jnp.where(key + half <= query + (blocks - 1 - at) * BLK, 0.0, NEG)

    sort_blocks(table, seq, kv_ref, k_s, 0, blocks)
    sort_blocks(table, seq, kv_ref, v_s, 1, blocks)
    q_all = q_ref[...]
    g_all = g_ref[...]
    lows, highs, dks, dvs = [], [], [], []
    for j in range(PACK):
        k = k_s[:, j * HD : (j + 1) * HD]
        v = v_s[:, j * HD : (j + 1) * HD]
        q = stack_heads(q_all, j * GROUP, SCALE)
        g = stack_heads(g_all, j * GROUP)

        def probs(s_parts):
            peak = jnp.max(s_parts[0], axis=0, keepdims=True)
            for s in s_parts[1:]:
                peak = jnp.maximum(peak, jnp.max(s, axis=0, keepdims=True))
            es = [jnp.exp(s - peak) for s in s_parts]
            total = jnp.sum(es[0], axis=0, keepdims=True)
            for e in es[1:]:
                total = total + jnp.sum(e, axis=0, keepdims=True)
            part = 1.0 / total
            return [e * part for e in es]

        def score_grads(ps, dps):
            inner = jnp.sum(ps[0] * dps[0], axis=0, keepdims=True)
            for p, d in zip(ps[1:], dps[1:]):
                inner = inner + jnp.sum(p * d, axis=0, keepdims=True)
            return [(p * (d - inner)).astype(BF16) for p, d in zip(ps, dps)]

        s_low = dot(k[:half], q[:rows], 1, 1) + jnp.concatenate([low_bias[...]] * GROUP, axis=1)
        (p_low,) = probs([s_low])
        (d_low,) = score_grads([p_low], [dot(v[:half], g[:rows], 1, 1)])
        dv_one = dot(p_low.astype(BF16), g[:rows])
        dk_one = dot(d_low, q[:rows])
        lows.append((dot(d_low, k[:half], 0, 0) * SCALE).astype(BF16))

        s_one = dot(k[:half], q[rows:], 1, 1)
        s_two = dot(k[half:], q[rows:], 1, 1) + jnp.concatenate([high_bias[...]] * GROUP, axis=1)
        p_one, p_two = probs([s_one, s_two])
        d_one, d_two = score_grads(
            [p_one, p_two], [dot(v[:half], g[rows:], 1, 1), dot(v[half:], g[rows:], 1, 1)]
        )
        dv_one = dv_one + dot(p_one.astype(BF16), g[rows:])
        dv_two = dot(p_two.astype(BF16), g[rows:])
        dk_one = dk_one + dot(d_one, q[rows:])
        dk_two = dot(d_two, q[rows:])
        highs.append(
            ((dot(d_one, k[:half], 0, 0) + dot(d_two, k[half:], 0, 0)) * SCALE).astype(BF16)
        )
        dks.append(jnp.concatenate([dk_one, dk_two], axis=0).astype(BF16))
        dvs.append(jnp.concatenate([dv_one, dv_two], axis=0).astype(BF16))
    dq_ref[...] = unstack_heads(lows, highs)
    k_s[...] = jnp.concatenate(dks, axis=1)
    v_s[...] = jnp.concatenate(dvs, axis=1)
    for c in range(cp):
        for h in range(2):
            at_b = pl.ds(inverse[seq, 2 * c + h] * BLK, BLK)
            parts[step, c, 0, h * BLK : (h + 1) * BLK, :] = k_s[at_b, :]
            parts[step, c, 1, h * BLK : (h + 1) * BLK, :] = v_s[at_b, :]
    for m in range(1, cp):
        step_copy(seq, pl.program_id(1), step, m).start()
    own_copy(seq, pl.program_id(1), step).start()

    @pl.when(step == last)
    def _():
        @pl.loop(0, last + 1)
        def _(i):
            at_seq, at_group = i // groups, lax.rem(i, groups)
            for m in range(1, cp):
                step_copy(at_seq, at_group, i, m).wait()
            own_copy(at_seq, at_group, i).wait()

        office.end(kinds, ins, outs)


ATTENTION_COST = pl.CostEstimate(flops=2**34, bytes_accessed=2**24, transcendentals=2**24)


def attention_specs(kv):
    cp, n_seq = kv.shape[:2]
    row = pl.BlockSpec((2 * BLK, PACK * GROUP * HD), lambda s, g, *_: (s, g))
    whole = pl.BlockSpec((cp, 1, 2, 2 * BLK, PACK * HD), lambda s, g, *_: (0, s, 0, 0, g))
    return row, whole, (n_seq, KV // PACK), cp * 2 * BLK


def attend(table, place, q, kv):
    row, whole, grid, keys = attention_specs(kv)
    return pl.pallas_call(
        attend_kernel,
        grid_spec=pltpu.PrefetchScalarGridSpec(
            num_scalar_prefetch=2,
            grid=grid,
            in_specs=[row, whole],
            out_specs=row,
            scratch_shapes=[pltpu.VMEM((keys, PACK * HD), BF16)] * 2
            + [pltpu.VMEM((BLK, keys // 2), F32)] * 2,
        ),
        out_shape=jax.ShapeDtypeStruct(q.shape, BF16),
        compiler_params=pltpu.CompilerParams(
            dimension_semantics=("arbitrary", "arbitrary"), vmem_limit_bytes=56 * 2**20
        ),
        cost_estimate=ATTENTION_COST,
    )(table, place, q, kv)


def attend_back(collective_id, table, inverse, place, q, kv, grad, *jobs):
    row, whole, grid, keys = attention_specs(kv)
    sizes = tuple(lax.axis_size(a) for a in DENSE)
    cp = sizes[2]
    steps = grid[0] * grid[1]
    kinds, arrays, shapes = courier_jobs(sizes, jobs)
    smem = pl.BlockSpec(memory_space=pltpu.SMEM)
    hbm = pl.BlockSpec(memory_space=pl.ANY)
    n = jobs_messages(kinds, *sizes)
    return pl.pallas_call(
        functools.partial(attend_back_kernel, sizes, kinds),
        grid=grid,
        in_specs=[smem, smem, smem, row, whole, row] + [hbm] * len(jobs),
        out_specs=[row, hbm] + [hbm] * len(jobs),
        out_shape=[
            jax.ShapeDtypeStruct(q.shape, BF16),
            jax.ShapeDtypeStruct(kv.shape, BF16),
        ]
        + shapes,
        scratch_shapes=[pltpu.VMEM((keys, PACK * HD), BF16)] * 2
        + [pltpu.VMEM((keys // 2, BLK), F32)] * 2
        + [pltpu.VMEM((steps, cp, 2, 2 * BLK, PACK * HD), BF16)]
        + post_scratch(n, len(jobs))
        + [
            pltpu.SemaphoreType.DMA((steps * (cp - 1),)),
            pltpu.SemaphoreType.DMA((steps * (cp - 1),)),
            pltpu.SemaphoreType.DMA((steps,)),
        ],
        compiler_params=pltpu.CompilerParams(
            dimension_semantics=("arbitrary", "arbitrary"),
            vmem_limit_bytes=56 * 2**20,
            collective_id=collective_id,
            has_side_effects=True,
        ),
        cost_estimate=ATTENTION_COST,
    )(table, inverse, place, q, kv, grad, *arrays)


def tie(x, *others):
    return lax.optimization_barrier((x,) + others)[0]


def mesh_copy(src, dst, sems, at, device):
    send, recv = sems
    return pltpu.make_async_remote_copy(
        src_ref=src, dst_ref=dst, send_sem=send.at[at], recv_sem=recv.at[at],
        device_id=device, device_id_type=pl.DeviceIdType.MESH,
    )


def jobs_messages(kinds, hi, ep, cp):
    f, e = hi * ep, ep * cp
    counts = {
        "gather": f // 2 - 1 + (f // 2) * (cp - 1) + (f // 2) * cp,
        "expert": f - 1, "owners": f - 1, "tokens": e - 1, "peers": cp - 1, "quad": ep - 1,
    }
    return sum(counts[k] for k in kinds)


def post_scratch(n, jobs):
    return [
        pltpu.SemaphoreType.DMA((max(n, 1),)),
        pltpu.SemaphoreType.DMA((max(n, 1),)),
        pltpu.SemaphoreType.DMA((max(jobs, 1),)),
    ]


def plus(a, b, size):
    return lax.rem(a + b, size)


def flip(a, bits):
    out = a
    for bit in range(bits.bit_length()):
        if bits >> bit & 1:
            out = out + (1 << bit) - (1 << (bit + 1)) * lax.rem(a // (1 << bit), 2)
    return out


class PostOffice:
    def __init__(self, sizes, sems):
        self.hi, self.ep, self.cp = sizes
        self.fsdp = self.hi * self.ep
        self.send, self.recv, self.here = sems
        self.my_ep, self.my_cp = lax.axis_index("ep"), lax.axis_index("cp")
        self.me = lax.axis_index("hi") * self.ep + self.my_ep
        self.sibling = flip(self.me, 1)

    def at_fsdp(self, f):
        return {"hi": f // self.ep, "ep": lax.rem(f, self.ep)}

    def greet(self, kinds):
        barrier = pltpu.get_barrier_semaphore()
        partners = [self.at_fsdp(plus(self.me, k, self.fsdp)) for k in range(1, self.fsdp)]
        partners += [{"cp": plus(self.my_cp, k, self.cp)} for k in range(1, self.cp)]
        if "tokens" in kinds:
            partners += [
                {"ep": plus(self.my_ep, a, self.ep), "cp": plus(self.my_cp, b, self.cp)}
                for a in range(1, self.ep)
                for b in range(1, self.cp)
            ]
        for p in partners:
            pl.semaphore_signal(barrier, inc=1, device_id=p, device_id_type=pl.DeviceIdType.MESH)
        pl.semaphore_wait(barrier, len(partners))

    def copies(self, kinds, ins, outs):
        me, my_ep, my_cp, ep, cp, fsdp = (
            self.me, self.my_ep, self.my_cp, self.ep, self.cp, self.fsdp
        )
        away, local = [], []

        def post(src, dst, device):
            away.append(mesh_copy(src, dst, (self.send, self.recv), len(away), device))

        def keep(src, dst):
            local.append(pltpu.make_async_copy(src, dst, self.here.at[len(local)]))

        for kind, x, out in zip(kinds, ins, outs):
            if kind == "expert":
                rows = x.shape[1]
                at = pl.ds(pl.multiple_of(me * rows, rows), rows)
                for k in range(1, fsdp):
                    to = plus(me, k, fsdp)
                    post(x.at[lax.rem(to, ep)], out.at[at], self.at_fsdp(to))
                keep(x.at[my_ep], out.at[at])
            elif kind == "owners":
                rows = out.shape[1]
                for k in range(1, fsdp):
                    to = plus(me, k, fsdp)
                    src = x.at[pl.ds(pl.multiple_of(to * rows, rows), rows)]
                    post(src, out.at[me], self.at_fsdp(to))
                keep(x.at[pl.ds(pl.multiple_of(me * rows, rows), rows)], out.at[me])
            elif kind == "quad":
                for k in range(1, ep):
                    to = plus(my_ep, k, ep)
                    post(x.at[to], out.at[my_ep], {"ep": to})
                keep(x.at[my_ep], out.at[my_ep])
            elif kind == "peers":
                for m in range(1, cp):
                    post(x, out.at[my_cp], {"cp": plus(my_cp, m, cp)})
                keep(x, out.at[my_cp])
        return away, local

    def begin(self, *jobs):
        for group in self.copies(*jobs):
            for c in group:
                c.start()

    def end(self, *jobs):
        for group in self.copies(*jobs):
            for c in group:
                c.wait()

    def gather(self, x, out, first, here):
        me, my_cp, cp, fsdp = self.me, self.my_cp, self.cp, self.fsdp
        sent, across = [], []

        def post(src, dst, device):
            c = mesh_copy(src, dst, (self.send, self.recv), first + len(sent), device)
            c.start()
            sent.append(c)
            return c

        def row(f, c):
            return out.at[f * cp + c]

        def share(f, src):
            for m in range(1, cp):
                across.append((f, m, post(src, row(f, my_cp), {"cp": plus(my_cp, m, cp)})))
            mirrored.append(post(src, row(f, my_cp), self.at_fsdp(self.sibling)))

        mirrored = []
        z = post(x, row(me, my_cp), self.at_fsdp(flip(me, 2)))
        own = pltpu.make_async_copy(x, row(me, my_cp), self.here.at[here])
        own.start()
        share(me, x)
        column = [z]
        for k in range(1, fsdp // 2):
            column[-1].wait_recv()
            if k + 1 < fsdp // 2:
                column.append(post(x, row(me, my_cp), self.at_fsdp(flip(me, 2 * k + 2))))
            f = flip(me, 2 * k)
            share(f, row(f, my_cp))
        yield
        for f, m, c in across:
            c.wait_recv()
            got = row(f, plus(my_cp, cp - m, cp))
            mirrored.append(post(got, got, self.at_fsdp(self.sibling)))
        for c in mirrored:
            c.wait_recv()
        for c in sent:
            c.wait_send()
        own.wait()
        yield


def courier_jobs(sizes, jobs):
    hi, ep, cp = sizes
    shapes = []
    for kind, x in jobs:
        if kind == "gather":
            shape = (hi * ep * cp,) + x.shape
        elif kind == "expert":
            shape = (hi * ep * x.shape[1],) + x.shape[2:]
        elif kind == "owners":
            shape = (hi * ep, x.shape[0] // (hi * ep)) + x.shape[1:]
        elif kind == "peers":
            shape = (cp,) + x.shape
        else:
            shape = x.shape
        shapes.append(jax.ShapeDtypeStruct(shape, x.dtype))
    return [k for k, _ in jobs], [x for _, x in jobs], shapes


def courier_kernel(sizes, kinds, *refs):
    n = len(kinds)
    ins, outs = refs[:n], refs[n : 2 * n]
    office = PostOffice(sizes, refs[2 * n :])
    office.greet(kinds)
    first, here, gathers = jobs_messages([k for k in kinds if k != "gather"], *sizes), 0, []
    here = len([k for k in kinds if k != "gather"])
    for kind, x, out in zip(kinds, ins, outs):
        if kind == "gather":
            gathers.append(office.gather(x, out, first, here))
            first, here = first + jobs_messages(["gather"], *sizes), here + 1
            next(gathers[-1])
    office.begin(kinds, ins, outs)
    for g in gathers:
        next(g)
    office.end(kinds, ins, outs)


def courier(collective_id, *jobs):
    sizes = tuple(lax.axis_size(a) for a in DENSE)
    kinds, arrays, shapes = courier_jobs(sizes, jobs)
    hbm = pl.BlockSpec(memory_space=pl.ANY)
    return pl.pallas_call(
        functools.partial(courier_kernel, sizes, kinds),
        out_shape=shapes,
        in_specs=[hbm] * len(jobs),
        out_specs=[hbm] * len(jobs),
        scratch_shapes=post_scratch(jobs_messages(kinds, *sizes), len(jobs)),
        compiler_params=pltpu.CompilerParams(collective_id=collective_id, has_side_effects=True),
    )(*arrays)


def dense_sum_kernel(sizes, kinds, n_parts, *refs):
    n = len(kinds)
    parts, refs = refs[:n_parts], refs[n_parts:]
    widths = [p.shape[2] for p in parts]
    columns = [pl.ds(sum(widths[:j]), w) for j, w in enumerate(widths)]
    ins, out, outs = refs[:n], refs[n], refs[n + 1 : 2 * n + 1]
    mine, from_core, summed, from_peers, rows_out, from_column = refs[2 * n + 1 : 2 * n + 7]
    office = PostOffice(sizes, refs[2 * n + 7 : 2 * n + 10])
    load_sem, core_sems, peer_sems, column_sems = (
        refs[2 * n + 10],
        refs[2 * n + 11 : 2 * n + 13],
        refs[2 * n + 13 : 2 * n + 15],
        refs[2 * n + 15 : 2 * n + 17],
    )
    cp, columns_n = sizes[2], office.fsdp // 2
    me, my_cp = office.me, office.my_cp
    office.greet(kinds)
    core = lax.rem(me, 2)
    targets = [flip(me, 2 * k) for k in range(columns_n - 1, -1, -1)]
    loads, cores = [], []
    for i, f in enumerate(targets):
        other = flip(f, 1)
        for j, (part, where) in enumerate(zip(parts, columns)):
            c = mesh_copy(
                part.at[pl.ds(other * cp, cp)],
                from_core.at[i, :, :, where],
                core_sems,
                i * n_parts + j,
                office.at_fsdp(office.sibling),
            )
            c.start()
            cores.append(c)
            c = pltpu.make_async_copy(
                part.at[pl.ds(f * cp, cp)], mine.at[i, :, :, where], load_sem.at[i * n_parts + j]
            )
            c.start()
            loads.append(c)
    office.begin(kinds, ins, outs)
    peers = []
    for i in range(columns_n):
        for c in loads[i * n_parts : (i + 1) * n_parts] + cores[i * n_parts : (i + 1) * n_parts]:
            c.wait()
        summed[i] = (mine[i].astype(F32) + from_core[i].astype(F32)).astype(BF16)
        row = []
        for m in range(1, cp):
            to = plus(my_cp, m, cp)
            c = mesh_copy(
                summed.at[i, to], from_peers.at[i, m - 1], peer_sems, i * (cp - 1) + m - 1, {"cp": to}
            )
            c.start()
            row.append(c)
        peers.append(row)
    column = []
    total = None
    for i, f in enumerate(targets):
        total = summed[i, my_cp].astype(F32)
        for m, c in enumerate(peers[i], 1):
            c.wait_recv()
            total = total + from_peers[i, m - 1].astype(F32)
        if i < columns_n - 1:
            rows_out[i] = total.astype(BF16)
            c = mesh_copy(
                rows_out.at[i], from_column.at[i], column_sems, i, office.at_fsdp(f)
            )
            c.start()
            column.append(c)
    for i, c in enumerate(column):
        c.wait_recv()
        total = total + from_column[i].astype(F32)
    out[...] = total
    for c in column + [c for row in peers for c in row]:
        c.wait_send()
    office.end(kinds, ins, outs)


def dense_sum(collective_id, parts, *jobs):
    sizes = tuple(lax.axis_size(a) for a in DENSE)
    hi, ep, cp = sizes
    column = hi * ep // 2
    rows = parts[0].shape[0] // (hi * ep * cp)
    width = sum(p.shape[1] for p in parts)
    kinds, arrays, shapes = courier_jobs(sizes, jobs)
    hbm = pl.BlockSpec(memory_space=pl.ANY)
    vmem = pl.BlockSpec(memory_space=pltpu.VMEM)

    def sems(count):
        return [pltpu.SemaphoreType.DMA((count,))] * 2

    return pl.pallas_call(
        functools.partial(dense_sum_kernel, sizes, kinds, len(parts)),
        out_shape=[jax.ShapeDtypeStruct((rows, width), F32)] + shapes,
        in_specs=[hbm] * (len(parts) + len(jobs)),
        out_specs=[vmem] + [hbm] * len(jobs),
        scratch_shapes=[
            pltpu.VMEM((column, cp, rows, width), BF16),
            pltpu.VMEM((column, cp, rows, width), BF16),
            pltpu.VMEM((column, cp, rows, width), BF16),
            pltpu.VMEM((column, cp - 1, rows, width), BF16),
            pltpu.VMEM((column - 1, rows, width), BF16),
            pltpu.VMEM((column - 1, rows, width), BF16),
        ]
        + post_scratch(jobs_messages(kinds, *sizes), len(jobs))
        + [pltpu.SemaphoreType.DMA((column * len(parts),))]
        + sems(column * len(parts))
        + sems(column * (cp - 1))
        + sems(column - 1),
        compiler_params=pltpu.CompilerParams(
            collective_id=collective_id, has_side_effects=True, vmem_limit_bytes=56 * 2**20
        ),
    )(*(p.reshape(-1, rows, p.shape[1]) for p in parts), *arrays)


def quad(x):
    return lax.all_to_all(x, "ep", split_axis=0, concat_axis=0, tiled=True)


def swap(x):
    hi = lax.axis_size("hi")
    xs = x if isinstance(x, list) else [x] * (hi - 1)
    return [
        lax.ppermute(xs[k - 1], "hi", [(i, (i + k) % hi) for i in range(hi)]) for k in range(1, hi)
    ]


def before(k):
    hi = lax.axis_size("hi")
    return lax.rem(lax.axis_index("hi") - k + hi, hi)


def after(k):
    return lax.rem(lax.axis_index("hi") + k, lax.axis_size("hi"))


def place_pieces(mine, pieces):
    rows = mine.shape[0]
    full = jnp.zeros((rows * lax.axis_size("hi"), mine.shape[1]), mine.dtype)
    full = lax.dynamic_update_slice(full, mine, (before(0) * rows, 0))
    for first, arrays in pieces:
        for k, part in enumerate(arrays, 1):
            full = lax.dynamic_update_slice(full, part, (before(k) * rows + first, 0))
    return full


def half_products(left, right):
    width = left.shape[1] // lax.axis_size("hi")
    parts = [
        dot(lax.dynamic_slice_in_dim(left, after(k) * width, width, axis=1), right, 0, 0)
        for k in range(lax.axis_size("hi"))
    ]
    return parts[0], [p.astype(BF16) for p in parts[1:]]


def small_sum(x):
    n = lax.axis_size("hi") * lax.axis_size("ep") * lax.axis_size("cp")
    rows, k = x.shape[0] // n, x.shape[1]
    flat = x.reshape(n, 1, rows * k)
    got = lax.all_to_all(flat, DENSE, split_axis=0, concat_axis=0, tiled=True)
    return jnp.sum(got, axis=(0, 1)).reshape(rows, k)


def rms_backward(rows, scale, gain, grad_norm):
    weighted = grad_norm * gain
    inner = jnp.mean(weighted * rows, axis=-1, keepdims=True)
    grad_rows = scale * weighted - rows * scale * scale * scale * inner
    return grad_rows, jnp.sum(grad_norm * rows * scale, axis=0)


def with_extra(main, *columns):
    rows = main.shape[0]
    columns = [c.reshape(rows, -1).astype(main.dtype) for c in columns]
    used = sum(c.shape[1] for c in columns)
    return jnp.concatenate([main, *columns, jnp.zeros((rows, -used % 128), main.dtype)], axis=1)


def local(
    layer_input,
    cotangent,
    pairing,
    routes,
    first_gain,
    second_gain,
    query_weight,
    key_weight,
    value_weight,
    out_weight,
    router_weight,
    gate_weight,
    up_weight,
    down_weight,
):
    n_seq = layer_input.shape[0]
    width = layer_input.shape[-1]
    rows = 2 * BLK
    tokens = n_seq * rows
    cp = lax.axis_size("cp")
    here = lax.axis_index("cp")
    blocks = 2 * cp
    n_q, n_kv = H * HD, KV * HD
    n_slots = EXPERTS * n_seq * CAP

    first = with_extra(
        jnp.concatenate([query_weight, key_weight, value_weight], axis=1), first_gain
    )
    second = with_extra(out_weight, router_weight, second_gain)
    second = lax.all_gather(second, DENSE, axis=0, tiled=True)
    first, gate_matrix, down = courier(
        0, ("gather", first), ("expert", gate_weight), ("quad", down_weight)
    )
    first = first.reshape(width, -1)
    down = down.reshape(-1, width)
    n_first = n_q + 2 * n_kv

    chosen = routes.reshape(tokens, 2)
    experts = jnp.arange(EXPERTS, dtype=jnp.int32)
    picks = chosen[:, :, None] == experts[None, None, :]
    named = jnp.any(picks, axis=1).astype(BF16)
    token = jnp.arange(tokens, dtype=jnp.int32)
    earlier = (token[None, :] < token[:, None]) & (token[None, :] // rows == token[:, None] // rows)
    before = dot(earlier.astype(BF16), named)
    rank = jnp.sum(jnp.where(picks, before[:, None, :], 0.0), axis=-1).astype(jnp.int32)
    slots = (chosen * n_seq + (token // rows)[:, None]) * CAP + rank
    slot = jnp.arange(n_slots, dtype=jnp.int32)
    at_slot = [slots[:, r][None, :] == slot[:, None] for r in range(2)]
    place_rows = (at_slot[0] | at_slot[1]).astype(BF16)
    take_rows = [(slots[:, r][:, None] == slot[None, :]).astype(BF16) for r in range(2)]

    def exchange(x):
        x = x.reshape(EXPERTS, n_seq * CAP, -1)
        x = lax.all_to_all(x, ("cp", "ep"), split_axis=0, concat_axis=0, tiled=True)
        return x.reshape(n_slots, -1)

    def exchange_scalar(x):
        x = x.reshape(EXPERTS, 1, n_seq * CAP)
        x = lax.all_to_all(x, ("cp", "ep"), split_axis=0, concat_axis=0, tiled=True)
        return x.reshape(n_slots)

    grad_rows = dot(place_rows, cotangent.reshape(tokens, width)).astype(BF16)
    qkv_matrix = first[:, :n_first]
    gain_one = first[:, n_first].astype(F32)
    out_matrix = second[:, :width]
    router_matrix = second[:, width : width + EXPERTS]
    gain_two = second[:, width + EXPERTS].astype(F32)

    resid = layer_input.reshape(tokens, width).astype(F32)
    scale_one = lax.rsqrt(jnp.mean(resid * resid, axis=-1, keepdims=True) + EPS)
    attn_in = (resid * scale_one * gain_one).astype(BF16)
    qkv = dot(attn_in, qkv_matrix).astype(BF16)
    queries = qkv[:, :n_q]
    kv = qkv[:, n_q:].reshape(n_seq, rows, 2, n_kv).transpose(0, 2, 1, 3)
    kv_all, up_matrix = courier(1, ("peers", kv), ("expert", up_weight))
    ids = jnp.stack([pairing, blocks - 1 - pairing], axis=2).reshape(n_seq, blocks)
    order = jnp.arange(blocks, dtype=jnp.int32)
    table = jnp.sum(jnp.where(ids[:, :, None] == order, order[None, :, None], 0), axis=1)
    place = lax.dynamic_index_in_dim(pairing, here, axis=1, keepdims=False)
    grad_rows = exchange(tie(grad_rows, kv_all))
    attn_out = attend(table, place, queries, kv_all)
    attn_out = tie(attn_out, grad_rows)
    middle = resid + dot(attn_out, out_matrix)
    scale_two = lax.rsqrt(jnp.mean(middle * middle, axis=-1, keepdims=True) + EPS)
    moe_in = (middle * scale_two * gain_two).astype(BF16)

    rows_out = dot(place_rows, moe_in).astype(BF16)
    down_piece = swap(down)
    arrived = exchange(rows_out)
    down_matrix = place_pieces(down, [(0, down_piece)])
    gate_pre = dot(arrived, gate_matrix)
    up_pre = dot(arrived, up_matrix)
    sigmoid_gate = jax.nn.sigmoid(gate_pre)
    swish = gate_pre * sigmoid_gate
    hidden = (swish * up_pre).astype(BF16)
    produced = dot(hidden, down_matrix).astype(BF16)
    hidden_grad = dot(grad_rows, down_matrix, 1, 1)
    gate_inner = exchange_scalar(jnp.sum(hidden_grad * hidden.astype(F32), axis=1))
    gate_pre_grad = hidden_grad * up_pre * sigmoid_gate * (1.0 + gate_pre * (1.0 - sigmoid_gate))
    gate_pre_grad = gate_pre_grad.astype(BF16)
    up_pre_grad = (hidden_grad * swish).astype(BF16)
    grad_back = dot(gate_pre_grad, gate_matrix, 1, 1) + dot(up_pre_grad, up_matrix, 1, 1)
    grad_back = grad_back.astype(BF16)

    logits = dot(moe_in, router_matrix)
    pick_f = picks.astype(F32)
    picked = jnp.sum(pick_f * logits[:, None, :], axis=-1)
    powers = jnp.exp(picked - jnp.max(picked, axis=-1, keepdims=True))
    gates = powers / jnp.sum(powers, axis=-1, keepdims=True)
    gate_slot = jnp.sum(
        sum(jnp.where(at_slot[r], gates[:, r][None, :], 0.0) for r in range(2)), axis=1
    )
    gate_slot = exchange_scalar(tie(gate_slot, arrived))[:, None]

    arrived_gated = (arrived.astype(F32) * gate_slot).astype(BF16)
    gate_part = dot(arrived_gated, gate_pre_grad, 0, 0).astype(BF16)
    up_part = dot(arrived_gated, up_pre_grad, 0, 0).astype(BF16)
    down_own, down_sent = half_products(
        hidden, (grad_rows.astype(F32) * gate_slot).astype(BF16)
    )
    down_sent = swap(down_sent)
    grad_returned, gate_part, up_part, down_own = lax.optimization_barrier(
        (exchange(grad_back), gate_part, up_part, down_own)
    )

    returned = exchange(tie(produced, grad_returned))
    back = [dot(take_rows[r], returned) for r in range(2)]
    final = middle + gates[:, :1] * back[0] + gates[:, 1:] * back[1]
    layer_output = final.astype(BF16)
    grad_final = cotangent.reshape(tokens, width).astype(F32)
    gate_inner = jnp.stack(
        [jnp.sum(jnp.where(a, gate_inner[:, None], 0.0), axis=0) for a in at_slot], axis=1
    )
    pair_grad = gates * (gate_inner - jnp.sum(gates * gate_inner, axis=-1, keepdims=True))
    logit_grad = jnp.sum(pick_f * pair_grad[:, :, None], axis=1)
    moe_in_grad = jnp.dot(logit_grad, router_matrix.astype(F32).T, precision=HIGH)
    for r in range(2):
        moe_in_grad = moe_in_grad + gates[:, r : r + 1] * dot(take_rows[r], grad_returned)
    router_part = jnp.dot(moe_in.astype(F32).T, logit_grad, precision=HIGH)
    middle_norm_grad, gain_two_grad = rms_backward(middle, scale_two, gain_two, moe_in_grad)
    middle_grad = grad_final + middle_norm_grad
    branch_grad = middle_grad.astype(BF16)
    out_part = dot(attn_out, branch_grad, 0, 0).astype(BF16)
    router_sum = small_sum(tie(router_part, returned))
    attn_out_grad = dot(branch_grad, out_matrix, 1, 1).astype(BF16)
    attn_out_grad = tie(attn_out_grad, out_part)
    query_grad, kv_grad, gate_parts = attend_back(
        2, table, ids, place, queries, kv_all, attn_out_grad, ("owners", gate_part)
    )
    kv_grad = tie(kv_grad, returned, *down_sent)
    kv_grad = jnp.sum(kv_grad.astype(F32), axis=0).astype(BF16)
    kv_grad = kv_grad.transpose(0, 2, 1, 3).reshape(tokens, 2 * n_kv)
    qkv_grad = jnp.concatenate([query_grad, kv_grad], axis=1)
    first_part = dot(attn_in, qkv_grad, 0, 0).astype(BF16)
    first_sum, up_parts = dense_sum(
        3, [first_part, out_part], ("owners", up_part)
    )
    attn_in_grad = dot(qkv_grad, qkv_matrix, 1, 1)
    resid_norm_grad, gain_one_grad = rms_backward(resid, scale_one, gain_one, attn_in_grad)
    input_grad = middle_grad + resid_norm_grad
    down_sum = tie(down_own, query_grad, returned) + sum(d.astype(F32) for d in down_sent)
    down_sum = quad(down_sum.astype(BF16).reshape(down_weight.shape)).astype(F32)

    def own_sum(parts):
        halves = parts.reshape((-1,) + gate_weight.shape)
        return jnp.sum(halves.astype(F32), axis=0)

    gain_sum = small_sum(jnp.stack([gain_one_grad, gain_two_grad], axis=1))
    return (
        layer_output.reshape(layer_input.shape),
        input_grad.reshape(layer_input.shape),
        gain_sum[:, 0],
        gain_sum[:, 1],
        first_sum[:, :n_q],
        first_sum[:, n_q : n_q + n_kv],
        first_sum[:, n_q + n_kv : n_first],
        first_sum[:, n_first:],
        router_sum,
        own_sum(gate_parts),
        own_sum(up_parts),
        down_sum,
    )


def solution(mesh):
    fsdp, cp = mesh.shape["fsdp"], mesh.shape["cp"]
    ep = EXPERTS // cp
    finer = Mesh(mesh.devices.reshape(fsdp // ep, ep, cp), DENSE)
    rows = ("hi", "ep")
    block = P(rows, "cp", None, None, None)
    dense, vector, expert = P(DENSE, None), P(DENSE), P("cp", rows, None)
    in_specs = (block, block, P(rows, None), block) + (vector,) * 2 + (dense,) * 5 + (expert,) * 3
    out_specs = (block,) * 2 + (vector,) * 2 + (dense,) * 5 + (expert,) * 3
    return jax.shard_map(
        local, mesh=finer, in_specs=in_specs, out_specs=out_specs, check_vma=False
    )
```

```python
import functools

import jax
import jax.numpy as jnp
from jax import lax
from jax.experimental import pallas as pl
from jax.experimental.pallas import tpu as pltpu
from jax.sharding import Mesh, PartitionSpec as P

H = 24
KV = 8
HD = 64
EXPERTS = 16
BLK = 128
CAP = 48
EPS = 1e-05
NEG = -1e30
GROUP = H // KV
SCALE = HD ** (-0.5)
PACK = 2
HIGH = lax.Precision.HIGHEST
F32 = jnp.float32
BF16 = jnp.bfloat16
DENSE = ("hi", "ep", "cp")


def dot(a, b, ca=1, cb=0):
    return lax.dot_general(a, b, (((ca,), (cb,)), ((), ())), preferred_element_type=F32)


def sort_blocks(table, seq, src, dst, which, blocks):
    for b in range(blocks):
        at = table[seq, b]
        dst[pl.ds(b * BLK, BLK), :] = src[at // 2, 0, which, pl.ds((at % 2) * BLK, BLK), :]


def stack_heads(rows, first, scale=None):
    parts = [
        rows[half * BLK : (half + 1) * BLK, (first + i) * HD : (first + i + 1) * HD]
        for half in range(2)
        for i in range(GROUP)
    ]
    out = jnp.concatenate(parts, axis=0)
    return out if scale is None else out * jnp.asarray(scale, out.dtype)


def unstack_heads(low, high):
    rows = []
    for pieces in (low, high):
        heads = [p[i * BLK : (i + 1) * BLK] for p in pieces for i in range(GROUP)]
        rows.append(jnp.concatenate(heads, axis=1))
    return jnp.concatenate(rows, axis=0)


def attend_group(q_all, k_all, v_all, low_bias, high_bias):
    half = k_all.shape[0] // 2
    rows = GROUP * BLK
    lows, highs = [], []
    for j in range(PACK):
        k = k_all[:, j * HD : (j + 1) * HD]
        v = v_all[:, j * HD : (j + 1) * HD]
        q = stack_heads(q_all, j * GROUP, SCALE)
        s_low = dot(q[:rows], k[:half], 1, 1) + jnp.concatenate([low_bias] * GROUP, axis=0)
        peak = jnp.max(s_low, axis=-1, keepdims=True)
        e_low = jnp.exp(s_low - peak)
        total = jnp.sum(e_low, axis=-1, keepdims=True)
        lows.append((dot(e_low.astype(BF16), v[:half]) / total).astype(BF16))
        s_one = dot(q[rows:], k[:half], 1, 1)
        s_two = dot(q[rows:], k[half:], 1, 1) + jnp.concatenate([high_bias] * GROUP, axis=0)
        peak = jnp.maximum(
            jnp.max(s_one, axis=-1, keepdims=True), jnp.max(s_two, axis=-1, keepdims=True)
        )
        e_one = jnp.exp(s_one - peak)
        e_two = jnp.exp(s_two - peak)
        total = jnp.sum(e_one, axis=-1, keepdims=True) + jnp.sum(e_two, axis=-1, keepdims=True)
        mixed = dot(e_one.astype(BF16), v[:half]) + dot(e_two.astype(BF16), v[half:])
        highs.append((mixed / total).astype(BF16))
    return unstack_heads(lows, highs)


def query_bias(at, blocks):
    half = blocks * BLK // 2
    query = lax.broadcasted_iota(jnp.int32, (BLK, half), 0)
    key = lax.broadcasted_iota(jnp.int32, (BLK, half), 1)
    low = jnp.where(key <= query + at * BLK, 0.0, NEG)
    high = jnp.where(key + half <= query + (blocks - 1 - at) * BLK, 0.0, NEG)
    return low, high


def attend_kernel(table, place, q_ref, kv_ref, o_ref, k_s, v_s, low_bias, high_bias):
    seq = pl.program_id(0)
    blocks = 2 * kv_ref.shape[0]

    @pl.when(pl.program_id(1) == 0)
    def _():
        low_bias[...], high_bias[...] = query_bias(place[seq], blocks)

    sort_blocks(table, seq, kv_ref, k_s, 0, blocks)
    sort_blocks(table, seq, kv_ref, v_s, 1, blocks)
    o_ref[...] = attend_group(q_ref[...], k_s[...], v_s[...], low_bias[...], high_bias[...])


def attend_back_kernel(
    sizes, kinds, table, inverse, place, q_ref, kv_ref, g_ref, *refs
):
    n = len(kinds)
    ins, dq_ref, dkv_ref, outs = refs[:n], refs[n], refs[n + 1], refs[n + 2 : 2 * n + 2]
    k_s, v_s, low_bias, high_bias, parts = refs[2 * n + 2 : 2 * n + 7]
    post_sems = refs[2 * n + 7 : 2 * n + 10]
    step_send, step_recv, step_here = refs[2 * n + 10 :]
    cp = sizes[2]
    my_cp = lax.axis_index("cp")
    groups = KV // PACK
    step = pl.program_id(0) * groups + pl.program_id(1)
    last = pl.num_programs(0) * groups - 1
    office = PostOffice(sizes, post_sems)

    @pl.when(step == 0)
    def _():
        office.greet(kinds)
        office.begin(kinds, ins, outs)

    def step_copy(at_seq, at_group, at_step, m):
        columns = pl.ds(pl.multiple_of(at_group * PACK * HD, PACK * HD), PACK * HD)
        to = lax.rem(my_cp + m, cp)
        return mesh_copy(
            parts.at[at_step, to],
            dkv_ref.at[my_cp, at_seq, :, :, columns],
            (step_send, step_recv),
            at_step * (cp - 1) + m - 1,
            {"cp": to},
        )

    def own_copy(at_seq, at_group, at_step):
        columns = pl.ds(pl.multiple_of(at_group * PACK * HD, PACK * HD), PACK * HD)
        return pltpu.make_async_copy(
            parts.at[at_step, my_cp], dkv_ref.at[my_cp, at_seq, :, :, columns], step_here.at[at_step]
        )

    seq = pl.program_id(0)
    blocks = 2 * kv_ref.shape[0]
    half = blocks * BLK // 2
    rows = GROUP * BLK
    at = place[seq]

    @pl.when(pl.program_id(1) == 0)
    def _():
        key = lax.broadcasted_iota(jnp.int32, (half, BLK), 0)
        query = lax.broadcasted_iota(jnp.int32, (half, BLK), 1)
        low_bias[...] = jnp.where(key <= query + at * BLK, 0.0, NEG)
        high_bias[...] = jnp.where(key + half <= query + (blocks - 1 - at) * BLK, 0.0, NEG)

    sort_blocks(table, seq, kv_ref, k_s, 0, blocks)
    sort_blocks(table, seq, kv_ref, v_s, 1, blocks)
    q_all = q_ref[...]
    g_all = g_ref[...]
    lows, highs, dks, dvs = [], [], [], []
    for j in range(PACK):
        k = k_s[:, j * HD : (j + 1) * HD]
        v = v_s[:, j * HD : (j + 1) * HD]
        q = stack_heads(q_all, j * GROUP, SCALE)
        g = stack_heads(g_all, j * GROUP)

        def probs(s_parts):
            peak = jnp.max(s_parts[0], axis=0, keepdims=True)
            for s in s_parts[1:]:
                peak = jnp.maximum(peak, jnp.max(s, axis=0, keepdims=True))
            es = [jnp.exp(s - peak) for s in s_parts]
            total = jnp.sum(es[0], axis=0, keepdims=True)
            for e in es[1:]:
                total = total + jnp.sum(e, axis=0, keepdims=True)
            part = 1.0 / total
            return [e * part for e in es]

        def score_grads(ps, dps):
            inner = jnp.sum(ps[0] * dps[0], axis=0, keepdims=True)
            for p, d in zip(ps[1:], dps[1:]):
                inner = inner + jnp.sum(p * d, axis=0, keepdims=True)
            return [(p * (d - inner)).astype(BF16) for p, d in zip(ps, dps)]

        s_low = dot(k[:half], q[:rows], 1, 1) + jnp.concatenate([low_bias[...]] * GROUP, axis=1)
        (p_low,) = probs([s_low])
        (d_low,) = score_grads([p_low], [dot(v[:half], g[:rows], 1, 1)])
        dv_one = dot(p_low.astype(BF16), g[:rows])
        dk_one = dot(d_low, q[:rows])
        lows.append((dot(d_low, k[:half], 0, 0) * SCALE).astype(BF16))

        s_one = dot(k[:half], q[rows:], 1, 1)
        s_two = dot(k[half:], q[rows:], 1, 1) + jnp.concatenate([high_bias[...]] * GROUP, axis=1)
        p_one, p_two = probs([s_one, s_two])
        d_one, d_two = score_grads(
            [p_one, p_two], [dot(v[:half], g[rows:], 1, 1), dot(v[half:], g[rows:], 1, 1)]
        )
        dv_one = dv_one + dot(p_one.astype(BF16), g[rows:])
        dv_two = dot(p_two.astype(BF16), g[rows:])
        dk_one = dk_one + dot(d_one, q[rows:])
        dk_two = dot(d_two, q[rows:])
        highs.append(
            ((dot(d_one, k[:half], 0, 0) + dot(d_two, k[half:], 0, 0)) * SCALE).astype(BF16)
        )
        dks.append(jnp.concatenate([dk_one, dk_two], axis=0).astype(BF16))
        dvs.append(jnp.concatenate([dv_one, dv_two], axis=0).astype(BF16))
    dq_ref[...] = unstack_heads(lows, highs)
    k_s[...] = jnp.concatenate(dks, axis=1)
    v_s[...] = jnp.concatenate(dvs, axis=1)
    for c in range(cp):
        for h in range(2):
            at_b = pl.ds(inverse[seq, 2 * c + h] * BLK, BLK)
            parts[step, c, 0, h * BLK : (h + 1) * BLK, :] = k_s[at_b, :]
            parts[step, c, 1, h * BLK : (h + 1) * BLK, :] = v_s[at_b, :]
    for m in range(1, cp):
        step_copy(seq, pl.program_id(1), step, m).start()
    own_copy(seq, pl.program_id(1), step).start()

    @pl.when(step == last)
    def _():
        @pl.loop(0, last + 1)
        def _(i):
            at_seq, at_group = i // groups, lax.rem(i, groups)
            for m in range(1, cp):
                step_copy(at_seq, at_group, i, m).wait()
            own_copy(at_seq, at_group, i).wait()

        office.end(kinds, ins, outs)


ATTENTION_COST = pl.CostEstimate(flops=2**34, bytes_accessed=2**24, transcendentals=2**24)


def attention_specs(kv):
    cp, n_seq = kv.shape[:2]
    row = pl.BlockSpec((2 * BLK, PACK * GROUP * HD), lambda s, g, *_: (s, g))
    whole = pl.BlockSpec((cp, 1, 2, 2 * BLK, PACK * HD), lambda s, g, *_: (0, s, 0, 0, g))
    return row, whole, (n_seq, KV // PACK), cp * 2 * BLK


def attend(table, place, q, kv):
    row, whole, grid, keys = attention_specs(kv)
    return pl.pallas_call(
        attend_kernel,
        grid_spec=pltpu.PrefetchScalarGridSpec(
            num_scalar_prefetch=2,
            grid=grid,
            in_specs=[row, whole],
            out_specs=row,
            scratch_shapes=[pltpu.VMEM((keys, PACK * HD), BF16)] * 2
            + [pltpu.VMEM((BLK, keys // 2), F32)] * 2,
        ),
        out_shape=jax.ShapeDtypeStruct(q.shape, BF16),
        compiler_params=pltpu.CompilerParams(
            dimension_semantics=("arbitrary", "arbitrary"), vmem_limit_bytes=56 * 2**20
        ),
        cost_estimate=ATTENTION_COST,
    )(table, place, q, kv)


def attend_back(collective_id, table, inverse, place, q, kv, grad, *jobs):
    row, whole, grid, keys = attention_specs(kv)
    sizes = tuple(lax.axis_size(a) for a in DENSE)
    cp = sizes[2]
    steps = grid[0] * grid[1]
    kinds, arrays, shapes = courier_jobs(sizes, jobs)
    smem = pl.BlockSpec(memory_space=pltpu.SMEM)
    hbm = pl.BlockSpec(memory_space=pl.ANY)
    n = jobs_messages(kinds, *sizes)
    return pl.pallas_call(
        functools.partial(attend_back_kernel, sizes, kinds),
        grid=grid,
        in_specs=[smem, smem, smem, row, whole, row] + [hbm] * len(jobs),
        out_specs=[row, hbm] + [hbm] * len(jobs),
        out_shape=[
            jax.ShapeDtypeStruct(q.shape, BF16),
            jax.ShapeDtypeStruct(kv.shape, BF16),
        ]
        + shapes,
        scratch_shapes=[pltpu.VMEM((keys, PACK * HD), BF16)] * 2
        + [pltpu.VMEM((keys // 2, BLK), F32)] * 2
        + [pltpu.VMEM((steps, cp, 2, 2 * BLK, PACK * HD), BF16)]
        + post_scratch(n, len(jobs))
        + [
            pltpu.SemaphoreType.DMA((steps * (cp - 1),)),
            pltpu.SemaphoreType.DMA((steps * (cp - 1),)),
            pltpu.SemaphoreType.DMA((steps,)),
        ],
        compiler_params=pltpu.CompilerParams(
            dimension_semantics=("arbitrary", "arbitrary"),
            vmem_limit_bytes=56 * 2**20,
            collective_id=collective_id,
            has_side_effects=True,
        ),
        cost_estimate=ATTENTION_COST,
    )(table, inverse, place, q, kv, grad, *arrays)


def tie(x, *others):
    return lax.optimization_barrier((x,) + others)[0]


def mesh_copy(src, dst, sems, at, device):
    send, recv = sems
    return pltpu.make_async_remote_copy(
        src_ref=src, dst_ref=dst, send_sem=send.at[at], recv_sem=recv.at[at],
        device_id=device, device_id_type=pl.DeviceIdType.MESH,
    )


def jobs_messages(kinds, hi, ep, cp):
    f, e = hi * ep, ep * cp
    counts = {
        "gather": f // 2 - 1 + (f // 2) * (cp - 1) + (f // 2) * cp,
        "expert": f - 1, "owners": f - 1, "tokens": e - 1, "peers": cp - 1, "quad": ep - 1,
    }
    return sum(counts[k] for k in kinds)


def post_scratch(n, jobs):
    return [
        pltpu.SemaphoreType.DMA((max(n, 1),)),
        pltpu.SemaphoreType.DMA((max(n, 1),)),
        pltpu.SemaphoreType.DMA((max(jobs, 1),)),
    ]


def plus(a, b, size):
    return lax.rem(a + b, size)


def flip(a, bits):
    out = a
    for bit in range(bits.bit_length()):
        if bits >> bit & 1:
            out = out + (1 << bit) - (1 << (bit + 1)) * lax.rem(a // (1 << bit), 2)
    return out


class PostOffice:
    def __init__(self, sizes, sems):
        self.hi, self.ep, self.cp = sizes
        self.fsdp = self.hi * self.ep
        self.send, self.recv, self.here = sems
        self.my_ep, self.my_cp = lax.axis_index("ep"), lax.axis_index("cp")
        self.me = lax.axis_index("hi") * self.ep + self.my_ep
        self.sibling = flip(self.me, 1)

    def at_fsdp(self, f):
        return {"hi": f // self.ep, "ep": lax.rem(f, self.ep)}

    def greet(self, kinds):
        barrier = pltpu.get_barrier_semaphore()
        partners = [self.at_fsdp(plus(self.me, k, self.fsdp)) for k in range(1, self.fsdp)]
        partners += [{"cp": plus(self.my_cp, k, self.cp)} for k in range(1, self.cp)]
        if "tokens" in kinds:
            partners += [
                {"ep": plus(self.my_ep, a, self.ep), "cp": plus(self.my_cp, b, self.cp)}
                for a in range(1, self.ep)
                for b in range(1, self.cp)
            ]
        for p in partners:
            pl.semaphore_signal(barrier, inc=1, device_id=p, device_id_type=pl.DeviceIdType.MESH)
        pl.semaphore_wait(barrier, len(partners))

    def copies(self, kinds, ins, outs):
        me, my_ep, my_cp, ep, cp, fsdp = (
            self.me, self.my_ep, self.my_cp, self.ep, self.cp, self.fsdp
        )
        away, local = [], []

        def post(src, dst, device):
            away.append(mesh_copy(src, dst, (self.send, self.recv), len(away), device))

        def keep(src, dst):
            local.append(pltpu.make_async_copy(src, dst, self.here.at[len(local)]))

        for kind, x, out in zip(kinds, ins, outs):
            if kind == "expert":
                rows = x.shape[1]
                at = pl.ds(pl.multiple_of(me * rows, rows), rows)
                for k in range(1, fsdp):
                    to = plus(me, k, fsdp)
                    post(x.at[lax.rem(to, ep)], out.at[at], self.at_fsdp(to))
                keep(x.at[my_ep], out.at[at])
            elif kind == "owners":
                rows = out.shape[1]
                for k in range(1, fsdp):
                    to = plus(me, k, fsdp)
                    src = x.at[pl.ds(pl.multiple_of(to * rows, rows), rows)]
                    post(src, out.at[me], self.at_fsdp(to))
                keep(x.at[pl.ds(pl.multiple_of(me * rows, rows), rows)], out.at[me])
            elif kind == "quad":
                for k in range(1, ep):
                    to = plus(my_ep, k, ep)
                    post(x.at[to], out.at[my_ep], {"ep": to})
                keep(x.at[my_ep], out.at[my_ep])
            elif kind == "peers":
                for m in range(1, cp):
                    post(x, out.at[my_cp], {"cp": plus(my_cp, m, cp)})
                keep(x, out.at[my_cp])
            elif kind == "tokens":
                for a in range(ep):
                    for b in range(cp):
                        if a or b:
                            to_ep, to_cp = plus(my_ep, a, ep), plus(my_cp, b, cp)
                            post(
                                x.at[to_cp * ep + to_ep],
                                out.at[my_cp * ep + my_ep],
                                {"ep": to_ep, "cp": to_cp},
                            )
                keep(x.at[my_cp * ep + my_ep], out.at[my_cp * ep + my_ep])
        return away, local

    def begin(self, *jobs):
        for group in self.copies(*jobs):
            for c in group:
                c.start()

    def end(self, *jobs):
        for group in self.copies(*jobs):
            for c in group:
                c.wait()

    def gather(self, x, out, first, here):
        me, my_cp, cp, fsdp = self.me, self.my_cp, self.cp, self.fsdp
        sent, across = [], []

        def post(src, dst, device):
            c = mesh_copy(src, dst, (self.send, self.recv), first + len(sent), device)
            c.start()
            sent.append(c)
            return c

        def row(f, c):
            return out.at[f * cp + c]

        def share(f, src):
            for m in range(1, cp):
                across.append((f, m, post(src, row(f, my_cp), {"cp": plus(my_cp, m, cp)})))
            mirrored.append(post(src, row(f, my_cp), self.at_fsdp(self.sibling)))

        mirrored = []
        z = post(x, row(me, my_cp), self.at_fsdp(flip(me, 2)))
        own = pltpu.make_async_copy(x, row(me, my_cp), self.here.at[here])
        own.start()
        share(me, x)
        column = [z]
        for k in range(1, fsdp // 2):
            column[-1].wait_recv()
            if k + 1 < fsdp // 2:
                column.append(post(x, row(me, my_cp), self.at_fsdp(flip(me, 2 * k + 2))))
            f = flip(me, 2 * k)
            share(f, row(f, my_cp))
        yield
        for f, m, c in across:
            c.wait_recv()
            got = row(f, plus(my_cp, cp - m, cp))
            mirrored.append(post(got, got, self.at_fsdp(self.sibling)))
        for c in mirrored:
            c.wait_recv()
        for c in sent:
            c.wait_send()
        own.wait()
        yield


def courier_jobs(sizes, jobs):
    hi, ep, cp = sizes
    shapes = []
    for kind, x in jobs:
        if kind == "gather":
            shape = (hi * ep * cp,) + x.shape
        elif kind == "expert":
            shape = (hi * ep * x.shape[1],) + x.shape[2:]
        elif kind == "owners":
            shape = (hi * ep, x.shape[0] // (hi * ep)) + x.shape[1:]
        elif kind == "peers":
            shape = (cp,) + x.shape
        else:
            shape = x.shape
        shapes.append(jax.ShapeDtypeStruct(shape, x.dtype))
    return [k for k, _ in jobs], [x for _, x in jobs], shapes


def courier_kernel(sizes, kinds, *refs):
    n = len(kinds)
    ins, outs = refs[:n], refs[n : 2 * n]
    office = PostOffice(sizes, refs[2 * n :])
    office.greet(kinds)
    first, here, gathers = jobs_messages([k for k in kinds if k != "gather"], *sizes), 0, []
    here = len([k for k in kinds if k != "gather"])
    for kind, x, out in zip(kinds, ins, outs):
        if kind == "gather":
            gathers.append(office.gather(x, out, first, here))
            first, here = first + jobs_messages(["gather"], *sizes), here + 1
            next(gathers[-1])
    office.begin(kinds, ins, outs)
    for g in gathers:
        next(g)
    office.end(kinds, ins, outs)


def courier(collective_id, *jobs):
    sizes = tuple(lax.axis_size(a) for a in DENSE)
    kinds, arrays, shapes = courier_jobs(sizes, jobs)
    hbm = pl.BlockSpec(memory_space=pl.ANY)
    return pl.pallas_call(
        functools.partial(courier_kernel, sizes, kinds),
        out_shape=shapes,
        in_specs=[hbm] * len(jobs),
        out_specs=[hbm] * len(jobs),
        scratch_shapes=post_scratch(jobs_messages(kinds, *sizes), len(jobs)),
        compiler_params=pltpu.CompilerParams(collective_id=collective_id, has_side_effects=True),
    )(*arrays)


def front_kernel(sizes, kinds, table, place, x_ref, shard_ref, *refs):
    n = len(kinds)
    ins = refs[:n]
    a_ref, q_ref, o_ref, kv_ref, w_ref = refs[n : n + 5]
    outs = refs[n + 5 : 2 * n + 5]
    rest = refs[2 * n + 5 :]
    w_all, kv_mine, k_s, v_s, low_bias, high_bias = rest[:6]
    office = PostOffice(sizes, rest[6:9])
    kv_send, kv_recv, kv_here = rest[9:12]
    kv_bufs = rest[12:]
    n_seq, cp, my_cp = len(kv_bufs), sizes[2], office.my_cp
    rows = 2 * BLK
    wide = KV * HD
    office.greet(kinds)
    gather = office.gather(shard_ref, w_all, jobs_messages(kinds, *sizes), n)
    next(gather)
    office.begin(kinds, ins, outs)
    x = x_ref[...].astype(F32)
    x = x * lax.rsqrt(jnp.mean(x * x, axis=-1, keepdims=True) + EPS)
    next(gather)
    depth = x.shape[1]
    keep_w = pltpu.make_async_copy(w_all, w_ref, kv_here.at[2 * n_seq])
    keep_w.start()
    last = pl.ds(H * HD + 2 * wide, 128)
    gain = w_all[:, :, last].astype(F32).reshape(depth, 128).T[:1]
    a_ref[...] = (x * gain).astype(BF16)

    def project(first):
        return dot(a_ref[...], w_all[:, :, pl.ds(first, wide)].reshape(depth, wide)).astype(BF16)

    for part in range(2):
        piece = project(H * HD + part * wide)
        for s in range(n_seq):
            kv_mine[s, part] = piece[s * rows : (s + 1) * rows]
    copies = []
    for s in range(n_seq):
        group = [
            mesh_copy(
                kv_mine.at[s],
                kv_bufs[s].at[my_cp],
                (kv_send, kv_recv),
                s * (cp - 1) + m - 1,
                {"cp": plus(my_cp, m, cp)},
            )
            for m in range(1, cp)
        ]
        group.append(pltpu.make_async_copy(kv_mine.at[s], kv_bufs[s].at[my_cp], kv_here.at[s]))
        for c in group:
            c.start()
        copies.append(group)

    @pl.loop(0, H * HD // wide)
    def _(t):
        first = pl.multiple_of(t * wide, wide)
        q_ref[:, pl.ds(first, wide)] = project(first)

    keeps = []
    for s in range(n_seq):
        for c in copies[s]:
            c.wait()
        keep = pltpu.make_async_copy(kv_bufs[s], kv_ref.at[:, s], kv_here.at[n_seq + s])
        keep.start()
        keeps.append(keep)
        for b in range(2 * cp):
            at = table[s, b]
            to = pl.ds(b * BLK, BLK)
            source = pl.ds((at % 2) * BLK, BLK)
            k_s[to, :] = kv_bufs[s][at // 2, 0, source, :]
            v_s[to, :] = kv_bufs[s][at // 2, 1, source, :]
        low_bias[...], high_bias[...] = query_bias(place[s], 2 * cp)

        @pl.loop(0, KV // PACK)
        def _(g, s=s):
            head = pl.ds(pl.multiple_of(g * PACK * HD, PACK * HD), PACK * HD)
            group = PACK * GROUP * HD
            heads = pl.ds(pl.multiple_of(g * group, group), group)
            at = pl.ds(s * rows, rows)
            o_ref[at, heads] = attend_group(
                q_ref[at, heads], k_s[:, head], v_s[:, head], low_bias[...], high_bias[...]
            )

    for c in keeps + [keep_w]:
        c.wait()
    office.end(kinds, ins, outs)


def front(collective_id, table, place, x, shard, *jobs):
    sizes = tuple(lax.axis_size(a) for a in DENSE)
    hi, ep, cp = sizes
    n_seq = table.shape[0]
    kinds, arrays, shapes = courier_jobs(sizes, jobs)
    rows, wide = 2 * BLK, KV * HD
    whole = (hi * ep * cp,) + shard.shape
    hbm = pl.BlockSpec(memory_space=pl.ANY)
    vmem = pl.BlockSpec(memory_space=pltpu.VMEM)
    smem = pl.BlockSpec(memory_space=pltpu.SMEM)
    keys = cp * rows
    row_shape = jax.ShapeDtypeStruct(x.shape, BF16)
    return pl.pallas_call(
        functools.partial(front_kernel, sizes, kinds),
        in_specs=[smem, smem, vmem, hbm] + [hbm] * len(jobs),
        out_specs=[vmem] * 3 + [hbm] * 2 + [hbm] * len(jobs),
        out_shape=[row_shape] * 3
        + [
            jax.ShapeDtypeStruct((cp, n_seq, 2, rows, wide), BF16),
            jax.ShapeDtypeStruct(whole, BF16),
        ]
        + shapes,
        scratch_shapes=[
            pltpu.VMEM(whole, BF16),
            pltpu.VMEM((n_seq, 2, rows, wide), BF16),
            pltpu.VMEM((keys, wide), BF16),
            pltpu.VMEM((keys, wide), BF16),
            pltpu.VMEM((BLK, keys // 2), F32),
            pltpu.VMEM((BLK, keys // 2), F32),
        ]
        + post_scratch(jobs_messages(kinds + ["gather"], *sizes), len(jobs) + 1)
        + [
            pltpu.SemaphoreType.DMA((n_seq * (cp - 1),)),
            pltpu.SemaphoreType.DMA((n_seq * (cp - 1),)),
            pltpu.SemaphoreType.DMA((2 * n_seq + 1,)),
        ]
        + [pltpu.VMEM((cp, 2, rows, wide), BF16)] * n_seq,
        compiler_params=pltpu.CompilerParams(
            collective_id=collective_id, has_side_effects=True, vmem_limit_bytes=58 * 2**20
        ),
        cost_estimate=ATTENTION_COST,
    )(table, place, x, shard, *arrays)


def dense_sum_kernel(sizes, kinds, n_parts, *refs):
    n = len(kinds)
    parts, refs = refs[:n_parts], refs[n_parts:]
    widths = [p.shape[2] for p in parts]
    columns = [pl.ds(sum(widths[:j]), w) for j, w in enumerate(widths)]
    ins, out, outs = refs[:n], refs[n], refs[n + 1 : 2 * n + 1]
    mine, from_core, summed, from_peers, rows_out, from_column = refs[2 * n + 1 : 2 * n + 7]
    office = PostOffice(sizes, refs[2 * n + 7 : 2 * n + 10])
    load_sem, core_sems, peer_sems, column_sems = (
        refs[2 * n + 10],
        refs[2 * n + 11 : 2 * n + 13],
        refs[2 * n + 13 : 2 * n + 15],
        refs[2 * n + 15 : 2 * n + 17],
    )
    cp, columns_n = sizes[2], office.fsdp // 2
    me, my_cp = office.me, office.my_cp
    office.greet(kinds)
    core = lax.rem(me, 2)
    targets = [flip(me, 2 * k) for k in range(columns_n - 1, -1, -1)]
    loads, cores = [], []
    for i, f in enumerate(targets):
        other = flip(f, 1)
        for j, (part, where) in enumerate(zip(parts, columns)):
            c = mesh_copy(
                part.at[pl.ds(other * cp, cp)],
                from_core.at[i, :, :, where],
                core_sems,
                i * n_parts + j,
                office.at_fsdp(office.sibling),
            )
            c.start()
            cores.append(c)
            c = pltpu.make_async_copy(
                part.at[pl.ds(f * cp, cp)], mine.at[i, :, :, where], load_sem.at[i * n_parts + j]
            )
            c.start()
            loads.append(c)
    office.begin(kinds, ins, outs)
    peers = []
    for i in range(columns_n):
        for c in loads[i * n_parts : (i + 1) * n_parts] + cores[i * n_parts : (i + 1) * n_parts]:
            c.wait()
        summed[i] = (mine[i].astype(F32) + from_core[i].astype(F32)).astype(BF16)
        row = []
        for m in range(1, cp):
            to = plus(my_cp, m, cp)
            c = mesh_copy(
                summed.at[i, to], from_peers.at[i, m - 1], peer_sems, i * (cp - 1) + m - 1, {"cp": to}
            )
            c.start()
            row.append(c)
        peers.append(row)
    column = []
    total = None
    for i, f in enumerate(targets):
        total = summed[i, my_cp].astype(F32)
        for m, c in enumerate(peers[i], 1):
            c.wait_recv()
            total = total + from_peers[i, m - 1].astype(F32)
        if i < columns_n - 1:
            rows_out[i] = total.astype(BF16)
            c = mesh_copy(
                rows_out.at[i], from_column.at[i], column_sems, i, office.at_fsdp(f)
            )
            c.start()
            column.append(c)
    for i, c in enumerate(column):
        c.wait_recv()
        total = total + from_column[i].astype(F32)
    out[...] = total
    for c in column + [c for row in peers for c in row]:
        c.wait_send()
    office.end(kinds, ins, outs)


def dense_sum(collective_id, parts, *jobs):
    sizes = tuple(lax.axis_size(a) for a in DENSE)
    hi, ep, cp = sizes
    column = hi * ep // 2
    rows = parts[0].shape[0] // (hi * ep * cp)
    width = sum(p.shape[1] for p in parts)
    kinds, arrays, shapes = courier_jobs(sizes, jobs)
    hbm = pl.BlockSpec(memory_space=pl.ANY)
    vmem = pl.BlockSpec(memory_space=pltpu.VMEM)

    def sems(count):
        return [pltpu.SemaphoreType.DMA((count,))] * 2

    return pl.pallas_call(
        functools.partial(dense_sum_kernel, sizes, kinds, len(parts)),
        out_shape=[jax.ShapeDtypeStruct((rows, width), F32)] + shapes,
        in_specs=[hbm] * (len(parts) + len(jobs)),
        out_specs=[vmem] + [hbm] * len(jobs),
        scratch_shapes=[
            pltpu.VMEM((column, cp, rows, width), BF16),
            pltpu.VMEM((column, cp, rows, width), BF16),
            pltpu.VMEM((column, cp, rows, width), BF16),
            pltpu.VMEM((column, cp - 1, rows, width), BF16),
            pltpu.VMEM((column - 1, rows, width), BF16),
            pltpu.VMEM((column - 1, rows, width), BF16),
        ]
        + post_scratch(jobs_messages(kinds, *sizes), len(jobs))
        + [pltpu.SemaphoreType.DMA((column * len(parts),))]
        + sems(column * len(parts))
        + sems(column * (cp - 1))
        + sems(column - 1),
        compiler_params=pltpu.CompilerParams(
            collective_id=collective_id, has_side_effects=True, vmem_limit_bytes=56 * 2**20
        ),
    )(*(p.reshape(-1, rows, p.shape[1]) for p in parts), *arrays)


def swap(x):
    hi = lax.axis_size("hi")
    xs = x if isinstance(x, list) else [x] * (hi - 1)
    return [
        lax.ppermute(xs[k - 1], "hi", [(i, (i + k) % hi) for i in range(hi)]) for k in range(1, hi)
    ]


def after(k):
    return lax.rem(lax.axis_index("hi") + k, lax.axis_size("hi"))


def half_rows(x):
    rows = x.shape[0] // lax.axis_size("hi")
    parts = [
        lax.dynamic_slice_in_dim(x, after(k) * rows, rows, axis=0)
        for k in range(lax.axis_size("hi"))
    ]
    return parts[0], parts[1:]


def expert_kernel(
    sizes,
    group,
    x_hbm,
    dy_hbm,
    gate_hbm,
    up_hbm,
    down_hbm,
    scale_ref,
    back_ref,
    inner_ref,
    e_ref,
    gate_out,
    up_out,
    down_out,
    x_s,
    dy_s,
    gate_w,
    up_w,
    down_w,
    hidden_s,
    dg_s,
    du_s,
    back_s,
    inner_s,
    e_s,
    load_sem,
    weight_sem,
    send,
    recv,
    out_sem,
):
    _, ep, cp = sizes
    n, cap, width = x_hbm.shape
    depth = hidden_s.shape[1]
    me = lax.axis_index("cp") * ep + lax.axis_index("ep")

    def source(k):
        return lax.rem(me + 1 + k, n)

    def device(at):
        return {"cp": at // ep, "ep": lax.rem(at, ep)}

    barrier = pltpu.get_barrier_semaphore()
    for k in range(n - 1):
        pl.semaphore_signal(
            barrier, inc=1, device_id=device(source(k)), device_id_type=pl.DeviceIdType.MESH
        )
    weights = [
        pltpu.make_async_copy(src, dst, weight_sem.at[i])
        for i, (src, dst) in enumerate(
            ((gate_hbm, gate_w), (up_hbm, up_w), (down_hbm, down_w))
        )
    ]
    loads = []
    for c in weights[:2]:
        c.start()
    for k in range(n):
        pair = [
            pltpu.make_async_copy(src.at[source(k)], dst.at[k], load_sem.at[2 * k + i])
            for i, (src, dst) in enumerate(((x_hbm, x_s), (dy_hbm, dy_s)))
        ]
        for c in pair:
            c.start()
        loads.append(pair)
    weights[2].start()
    for pair in loads:
        for c in pair:
            c.wait()
    for c in weights:
        c.wait()
    pl.semaphore_wait(barrier, n - 1)

    def away(k, src, dst, lane):
        return pltpu.make_async_remote_copy(
            src_ref=src.at[k],
            dst_ref=dst.at[me],
            send_sem=send.at[2 * k + lane],
            recv_sem=recv.at[2 * k + lane],
            device_id=device(source(k)),
            device_id_type=pl.DeviceIdType.MESH,
        )

    def here(src, dst, lane):
        return pltpu.make_async_copy(src.at[n - 1], dst.at[me], out_sem.at[lane])

    def keep_e(k):
        return pltpu.make_async_copy(e_s.at[k], e_ref.at[source(k)], out_sem.at[2 + k])

    tile = group * cap
    chunk = min(512, depth)

    @pl.loop(0, n // group)
    def _(t):
        first = pl.multiple_of(t * tile, tile)
        at = pl.ds(first, tile)
        k0 = t * group
        x = x_s[pl.ds(k0, group)].reshape(tile, width)
        dy = dy_s[pl.ds(k0, group)].reshape(tile, width)
        inner = jnp.zeros((tile, 1), F32)
        for f in range(0, depth, chunk):
            cols = slice(f, f + chunk)
            gate_pre = dot(x, gate_w[:, cols])
            up_pre = dot(x, up_w[:, cols])
            sigmoid_gate = jax.nn.sigmoid(gate_pre)
            swish = gate_pre * sigmoid_gate
            hidden = (swish * up_pre).astype(BF16)
            hidden_s[at, cols] = hidden
            hidden_grad = dot(dy, down_w[cols, :], 1, 1)
            inner = inner + jnp.sum(hidden_grad * hidden.astype(F32), axis=1, keepdims=True)
            slope = sigmoid_gate * (1.0 + gate_pre * (1.0 - sigmoid_gate))
            dg_s[at, cols] = (hidden_grad * up_pre * slope).astype(BF16)
            du_s[at, cols] = (hidden_grad * swish).astype(BF16)
        high = inner.astype(BF16)
        rest = inner - high.astype(F32)
        middle = rest.astype(BF16)
        low = (rest - middle.astype(F32)).astype(BF16)
        lane = lax.broadcasted_iota(jnp.int32, (tile, 128), 1)
        spread = jnp.where(
            lane == 0,
            high.astype(F32),
            jnp.where(lane == 1, middle.astype(F32), jnp.where(lane == 2, low.astype(F32), 0.0)),
        )
        inner_s[pl.ds(k0, group)] = spread.astype(BF16).reshape(group, cap, 128)
        for d in range(0, width, 512):
            cols = slice(d, d + 512)
            back = dot(dg_s[at, :], gate_w[cols, :], 1, 1) + dot(du_s[at, :], up_w[cols, :], 1, 1)
            back_s[pl.ds(k0, group), :, cols] = back.astype(BF16).reshape(group, cap, 512)
        for i in range(group):
            k = k0 + i

            @pl.when(k < n - 1)
            def _():
                away(k, back_s, back_ref, 0).start()
                away(k, inner_s, inner_ref, 1).start()

        for d in range(0, width, 512):
            cols = slice(d, d + 512)
            e = dot(hidden_s[at, :], down_w[:, cols])
            e_s[pl.ds(k0, group), :, cols] = e.astype(BF16).reshape(group, cap, 512)
        for i in range(group):
            keep_e(k0 + i).start()

    here(back_s, back_ref, 0).start()
    here(inner_s, inner_ref, 1).start()
    for k in range(n):
        gate = scale_ref[source(k)]
        x_s[k] = (x_s[k].astype(F32) * gate).astype(BF16)
        dy_s[k] = (dy_s[k].astype(F32) * gate).astype(BF16)

    @pl.loop(0, width // 256)
    def _(d):
        cols = pl.ds(pl.multiple_of(d * 256, 256), 256)
        x = x_s[:, :, cols].reshape(n * cap, 256)
        gate_out[cols, :] = dot(x, dg_s[...], 0, 0).astype(BF16)
        up_out[cols, :] = dot(x, du_s[...], 0, 0).astype(BF16)

    @pl.loop(0, depth // 256)
    def _(f):
        cols = pl.ds(pl.multiple_of(f * 256, 256), 256)
        down_out[cols, :] = dot(
            hidden_s[:, cols], dy_s[...].reshape(n * cap, width), 0, 0
        ).astype(BF16)

    here(back_s, back_ref, 0).wait()
    here(inner_s, inner_ref, 1).wait()
    for k in range(n):
        keep_e(k).wait()
    for k in range(n - 1):
        away(k, back_s, back_ref, 0).wait()
        away(k, inner_s, inner_ref, 1).wait()


def expert(collective_id, x, dy, gate, up, down, scale):
    sizes = tuple(lax.axis_size(a) for a in DENSE)
    n, cap, width = x.shape
    depth = gate.shape[1]
    hbm = pl.BlockSpec(memory_space=pl.ANY)
    vmem = pl.BlockSpec(memory_space=pltpu.VMEM)
    rows = pltpu.VMEM(x.shape, BF16)
    tall = pltpu.VMEM((n * cap, depth), BF16)

    def sems(count):
        return pltpu.SemaphoreType.DMA((count,))

    return pl.pallas_call(
        functools.partial(expert_kernel, sizes, 4),
        in_specs=[hbm] * 5 + [vmem],
        out_specs=[hbm] * 3 + [vmem] * 3,
        out_shape=[
            jax.ShapeDtypeStruct(x.shape, BF16),
            jax.ShapeDtypeStruct((n, cap, 128), BF16),
            jax.ShapeDtypeStruct(x.shape, BF16),
            jax.ShapeDtypeStruct(gate.shape, BF16),
            jax.ShapeDtypeStruct(up.shape, BF16),
            jax.ShapeDtypeStruct(down.shape, BF16),
        ],
        scratch_shapes=[
            rows,
            rows,
            pltpu.VMEM(gate.shape, BF16),
            pltpu.VMEM(up.shape, BF16),
            pltpu.VMEM(down.shape, BF16),
            tall,
            tall,
            tall,
            rows,
            pltpu.VMEM((n, cap, 128), BF16),
            rows,
            sems(2 * n),
            sems(3),
            sems(2 * n),
            sems(2 * n),
            sems(2 + n),
        ],
        compiler_params=pltpu.CompilerParams(
            collective_id=collective_id, has_side_effects=True, vmem_limit_bytes=62 * 2**20
        ),
        cost_estimate=ATTENTION_COST,
    )(x, dy, gate, up, down, scale)


def rms_backward(rows, scale, gain, grad_norm):
    weighted = grad_norm * gain
    inner = jnp.mean(weighted * rows, axis=-1, keepdims=True)
    grad_rows = scale * weighted - rows * scale * scale * scale * inner
    return grad_rows, jnp.sum(grad_norm * rows * scale, axis=0)


def with_extra(main, *columns):
    rows = main.shape[0]
    columns = [c.reshape(rows, -1).astype(main.dtype) for c in columns]
    used = sum(c.shape[1] for c in columns)
    return jnp.concatenate([main, *columns, jnp.zeros((rows, -used % 128), main.dtype)], axis=1)


def local(
    layer_input,
    cotangent,
    pairing,
    routes,
    first_gain,
    second_gain,
    query_weight,
    key_weight,
    value_weight,
    out_weight,
    router_weight,
    gate_weight,
    up_weight,
    down_weight,
):
    n_seq = layer_input.shape[0]
    width = layer_input.shape[-1]
    rows = 2 * BLK
    tokens = n_seq * rows
    cp = lax.axis_size("cp")
    here = lax.axis_index("cp")
    blocks = 2 * cp
    n_q, n_kv = H * HD, KV * HD
    n_slots = EXPERTS * n_seq * CAP

    first = with_extra(
        jnp.concatenate([query_weight, key_weight, value_weight], axis=1), first_gain
    )
    second = with_extra(out_weight, router_weight, second_gain)
    second = lax.all_gather(second, DENSE, axis=0, tiled=True)
    n_first = n_q + 2 * n_kv

    chosen = routes.reshape(tokens, 2)
    experts = jnp.arange(EXPERTS, dtype=jnp.int32)
    picks = chosen[:, :, None] == experts[None, None, :]
    named = jnp.any(picks, axis=1).astype(BF16)
    token = jnp.arange(tokens, dtype=jnp.int32)
    earlier = (token[None, :] < token[:, None]) & (token[None, :] // rows == token[:, None] // rows)
    before = dot(earlier.astype(BF16), named)
    rank = jnp.sum(jnp.where(picks, before[:, None, :], 0.0), axis=-1).astype(jnp.int32)
    slots = (chosen * n_seq + (token // rows)[:, None]) * CAP + rank
    slot = jnp.arange(n_slots, dtype=jnp.int32)
    at_slot = [slots[:, r][None, :] == slot[:, None] for r in range(2)]
    place_rows = (at_slot[0] | at_slot[1]).astype(BF16)
    take_rows = [(slots[:, r][:, None] == slot[None, :]).astype(BF16) for r in range(2)]

    def exchange(x):
        x = x.reshape(EXPERTS, n_seq * CAP, -1)
        x = lax.all_to_all(x, ("cp", "ep"), split_axis=0, concat_axis=0, tiled=True)
        return x.reshape(n_slots, -1)

    def exchange_scalar(x):
        x = x.reshape(EXPERTS, 1, n_seq * CAP)
        x = lax.all_to_all(x, ("cp", "ep"), split_axis=0, concat_axis=0, tiled=True)
        return x.reshape(n_slots)

    out_matrix = second[:, :width]
    router_matrix = second[:, width : width + EXPERTS]
    gain_two = second[:, width + EXPERTS].astype(F32)

    grad_rows = dot(place_rows, cotangent.reshape(tokens, width)).astype(BF16)
    resid = layer_input.reshape(tokens, width).astype(F32)
    scale_one = lax.rsqrt(jnp.mean(resid * resid, axis=-1, keepdims=True) + EPS)
    ids = jnp.stack([pairing, blocks - 1 - pairing], axis=2).reshape(n_seq, blocks)
    order = jnp.arange(blocks, dtype=jnp.int32)
    table = jnp.sum(jnp.where(ids[:, :, None] == order, order[None, :, None], 0), axis=1)
    place = lax.dynamic_index_in_dim(pairing, here, axis=1, keepdims=False)
    weights = [("expert", w) for w in (gate_weight, up_weight, down_weight)]
    if first.shape[0] % 16 == 0:
        (
            attn_in,
            queries,
            attn_out,
            kv_all,
            first,
            gate_matrix,
            up_matrix,
            down_matrix,
            grad_rows,
        ) = front(
            0,
            table,
            place,
            layer_input.reshape(tokens, width),
            first,
            *weights,
            ("tokens", grad_rows.reshape(EXPERTS, n_seq * CAP, width)),
        )
        grad_rows = grad_rows.reshape(n_slots, width)
        first = first.reshape(width, -1)
        qkv_matrix = first[:, :n_first]
        gain_one = first[:, n_first].astype(F32)
    else:
        first, gate_matrix, down_matrix = courier(0, ("gather", first), weights[0], weights[2])
        first = first.reshape(width, -1)
        qkv_matrix = first[:, :n_first]
        gain_one = first[:, n_first].astype(F32)
        attn_in = (resid * scale_one * gain_one).astype(BF16)
        qkv = dot(attn_in, qkv_matrix).astype(BF16)
        queries = qkv[:, :n_q]
        kv = qkv[:, n_q:].reshape(n_seq, rows, 2, n_kv).transpose(0, 2, 1, 3)
        kv_all, up_matrix = courier(1, ("peers", kv), weights[1])
        grad_rows = exchange(tie(grad_rows, kv_all))
        attn_out = tie(attend(table, place, queries, kv_all), grad_rows)
    middle = resid + dot(attn_out, out_matrix)
    scale_two = lax.rsqrt(jnp.mean(middle * middle, axis=-1, keepdims=True) + EPS)
    moe_in = (middle * scale_two * gain_two).astype(BF16)

    rows_out = dot(place_rows, moe_in).astype(BF16)
    arrived = exchange(rows_out)
    logits = dot(moe_in, router_matrix)
    pick_f = picks.astype(F32)
    picked = jnp.sum(pick_f * logits[:, None, :], axis=-1)
    powers = jnp.exp(picked - jnp.max(picked, axis=-1, keepdims=True))
    gates = powers / jnp.sum(powers, axis=-1, keepdims=True)
    gate_slot = jnp.sum(
        sum(jnp.where(at_slot[r], gates[:, r][None, :], 0.0) for r in range(2)), axis=1
    )
    gate_slot = exchange_scalar(tie(gate_slot, arrived))
    shape = (EXPERTS, n_seq * CAP, width)
    grad_returned, inner, produced, gate_part, up_part, down_part = expert(
        4,
        arrived.reshape(shape),
        grad_rows.reshape(shape),
        gate_matrix,
        up_matrix,
        down_matrix,
        gate_slot.reshape(EXPERTS, -1, 1),
    )
    grad_returned = grad_returned.reshape(n_slots, width)
    gate_inner = jnp.sum(inner[:, :, :3].astype(F32), axis=2).reshape(n_slots)
    down_own, down_sent = half_rows(down_part)
    down_sent = swap(down_sent)

    returned = exchange(tie(produced, grad_returned))
    back = [dot(take_rows[r], returned) for r in range(2)]
    final = middle + gates[:, :1] * back[0] + gates[:, 1:] * back[1]
    layer_output = final.astype(BF16)
    grad_final = cotangent.reshape(tokens, width).astype(F32)
    gate_inner = jnp.stack(
        [jnp.sum(jnp.where(a, gate_inner[:, None], 0.0), axis=0) for a in at_slot], axis=1
    )
    pair_grad = gates * (gate_inner - jnp.sum(gates * gate_inner, axis=-1, keepdims=True))
    logit_grad = jnp.sum(pick_f * pair_grad[:, :, None], axis=1)
    moe_in_grad = jnp.dot(logit_grad, router_matrix.astype(F32).T, precision=HIGH)
    for r in range(2):
        moe_in_grad = moe_in_grad + gates[:, r : r + 1] * dot(take_rows[r], grad_returned)
    router_part = jnp.dot(moe_in.astype(F32).T, logit_grad, precision=HIGH)
    middle_norm_grad, gain_two_grad = rms_backward(middle, scale_two, gain_two, moe_in_grad)
    middle_grad = grad_final + middle_norm_grad
    branch_grad = middle_grad.astype(BF16)
    out_part = dot(attn_out, branch_grad, 0, 0).astype(BF16)
    attn_out_grad = dot(branch_grad, out_matrix, 1, 1).astype(BF16)
    attn_out_grad = tie(attn_out_grad, out_part)
    query_grad, kv_grad, gate_parts = attend_back(
        2, table, ids, place, queries, kv_all, attn_out_grad, ("owners", gate_part)
    )
    kv_grad = tie(kv_grad, returned, *down_sent)
    kv_grad = jnp.sum(kv_grad.astype(F32), axis=0).astype(BF16)
    kv_grad = kv_grad.transpose(0, 2, 1, 3).reshape(tokens, 2 * n_kv)
    qkv_grad = jnp.concatenate([query_grad, kv_grad], axis=1)
    first_part = dot(attn_in, qkv_grad, 0, 0).astype(BF16)
    attn_in_grad = dot(qkv_grad, qkv_matrix, 1, 1)
    resid_norm_grad, gain_one_grad = rms_backward(resid, scale_one, gain_one, attn_in_grad)
    input_grad = middle_grad + resid_norm_grad
    down_sum = tie(down_own, query_grad, returned).astype(F32) + sum(d.astype(F32) for d in down_sent)
    down_sum = down_sum.astype(BF16).reshape(down_weight.shape)

    def own_sum(parts):
        halves = parts.reshape((-1,) + gate_weight.shape)
        return jnp.sum(halves.astype(F32), axis=0)

    small_part = jnp.concatenate(
        [router_part, gain_one_grad[:, None], gain_two_grad[:, None]], axis=1
    ).astype(BF16)
    small_part = jnp.pad(small_part, ((0, 0), (0, -small_part.shape[1] % 128)))
    dense, up_parts, down_sum = dense_sum(
        3, [first_part, out_part, small_part], ("owners", up_part), ("quad", down_sum)
    )
    at_small = n_first + width
    return (
        layer_output.reshape(layer_input.shape),
        input_grad.reshape(layer_input.shape),
        dense[:, at_small + EXPERTS],
        dense[:, at_small + EXPERTS + 1],
        dense[:, :n_q],
        dense[:, n_q : n_q + n_kv],
        dense[:, n_q + n_kv : n_first],
        dense[:, n_first:at_small],
        dense[:, at_small : at_small + EXPERTS],
        own_sum(gate_parts),
        own_sum(up_parts),
        down_sum.astype(F32),
    )


def solution(mesh):
    fsdp, cp = mesh.shape["fsdp"], mesh.shape["cp"]
    ep = EXPERTS // cp
    finer = Mesh(mesh.devices.reshape(fsdp // ep, ep, cp), DENSE)
    rows = ("hi", "ep")
    block = P(rows, "cp", None, None, None)
    dense, vector, expert = P(DENSE, None), P(DENSE), P("cp", rows, None)
    in_specs = (block, block, P(rows, None), block) + (vector,) * 2 + (dense,) * 5 + (expert,) * 3
    out_specs = (block,) * 2 + (vector,) * 2 + (dense,) * 5 + (expert,) * 3
    return jax.shard_map(
        local, mesh=finer, in_specs=in_specs, out_specs=out_specs, check_vma=False
    )
```

```python
import functools

import jax
import jax.numpy as jnp
from jax import lax
from jax.experimental import pallas as pl
from jax.experimental.pallas import tpu as pltpu
from jax.sharding import Mesh, PartitionSpec as P

H = 24
KV = 8
HD = 64
EXPERTS = 16
BLK = 128
CAP = 48
EPS = 1e-05
NEG = -1e30
GROUP = H // KV
SCALE = HD ** (-0.5)
PACK = 2
HIGH = lax.Precision.HIGHEST
F32 = jnp.float32
BF16 = jnp.bfloat16
DENSE = ("hi", "ep", "cp")


def dot(a, b, ca=1, cb=0):
    return lax.dot_general(a, b, (((ca,), (cb,)), ((), ())), preferred_element_type=F32)


def sort_blocks(table, seq, src, dst, which, blocks):
    for b in range(blocks):
        at = table[seq, b]
        dst[pl.ds(b * BLK, BLK), :] = src[at // 2, 0, which, pl.ds((at % 2) * BLK, BLK), :]


def stack_heads(rows, first, scale=None):
    parts = [
        rows[half * BLK : (half + 1) * BLK, (first + i) * HD : (first + i + 1) * HD]
        for half in range(2)
        for i in range(GROUP)
    ]
    out = jnp.concatenate(parts, axis=0)
    return out if scale is None else out * jnp.asarray(scale, out.dtype)


def unstack_heads(low, high):
    rows = []
    for pieces in (low, high):
        heads = [p[i * BLK : (i + 1) * BLK] for p in pieces for i in range(GROUP)]
        rows.append(jnp.concatenate(heads, axis=1))
    return jnp.concatenate(rows, axis=0)


def attend_group(q_all, k_all, v_all, low_bias, high_bias):
    half = k_all.shape[0] // 2
    rows = GROUP * BLK
    lows, highs = [], []
    for j in range(PACK):
        k = k_all[:, j * HD : (j + 1) * HD]
        v = v_all[:, j * HD : (j + 1) * HD]
        q = stack_heads(q_all, j * GROUP, SCALE)
        s_low = dot(q[:rows], k[:half], 1, 1) + jnp.concatenate([low_bias] * GROUP, axis=0)
        peak = jnp.max(s_low, axis=-1, keepdims=True)
        e_low = jnp.exp(s_low - peak)
        total = jnp.sum(e_low, axis=-1, keepdims=True)
        lows.append((dot(e_low.astype(BF16), v[:half]) / total).astype(BF16))
        s_one = dot(q[rows:], k[:half], 1, 1)
        s_two = dot(q[rows:], k[half:], 1, 1) + jnp.concatenate([high_bias] * GROUP, axis=0)
        peak = jnp.maximum(
            jnp.max(s_one, axis=-1, keepdims=True), jnp.max(s_two, axis=-1, keepdims=True)
        )
        e_one = jnp.exp(s_one - peak)
        e_two = jnp.exp(s_two - peak)
        total = jnp.sum(e_one, axis=-1, keepdims=True) + jnp.sum(e_two, axis=-1, keepdims=True)
        mixed = dot(e_one.astype(BF16), v[:half]) + dot(e_two.astype(BF16), v[half:])
        highs.append((mixed / total).astype(BF16))
    return unstack_heads(lows, highs)


def query_bias(at, blocks):
    half = blocks * BLK // 2
    query = lax.broadcasted_iota(jnp.int32, (BLK, half), 0)
    key = lax.broadcasted_iota(jnp.int32, (BLK, half), 1)
    low = jnp.where(key <= query + at * BLK, 0.0, NEG)
    high = jnp.where(key + half <= query + (blocks - 1 - at) * BLK, 0.0, NEG)
    return low, high


def attend_kernel(table, place, q_ref, kv_ref, o_ref, k_s, v_s, low_bias, high_bias):
    seq = pl.program_id(0)
    blocks = 2 * kv_ref.shape[0]

    @pl.when(pl.program_id(1) == 0)
    def _():
        low_bias[...], high_bias[...] = query_bias(place[seq], blocks)

    sort_blocks(table, seq, kv_ref, k_s, 0, blocks)
    sort_blocks(table, seq, kv_ref, v_s, 1, blocks)
    o_ref[...] = attend_group(q_ref[...], k_s[...], v_s[...], low_bias[...], high_bias[...])


def attend_back_kernel(
    sizes, kinds, table, inverse, place, q_ref, kv_ref, g_ref, *refs
):
    n = len(kinds)
    ins, dq_ref, dkv_ref, outs = refs[:n], refs[n], refs[n + 1], refs[n + 2 : 2 * n + 2]
    k_s, v_s, low_bias, high_bias, parts = refs[2 * n + 2 : 2 * n + 7]
    post_sems = refs[2 * n + 7 : 2 * n + 10]
    step_send, step_recv, step_here = refs[2 * n + 10 :]
    cp = sizes[2]
    my_cp = lax.axis_index("cp")
    groups = KV // PACK
    step = pl.program_id(0) * groups + pl.program_id(1)
    last = pl.num_programs(0) * groups - 1
    office = PostOffice(sizes, post_sems)

    @pl.when(step == 0)
    def _():
        office.greet(kinds)
        office.begin(kinds, ins, outs)

    def step_copy(at_seq, at_group, at_step, m):
        columns = pl.ds(pl.multiple_of(at_group * PACK * HD, PACK * HD), PACK * HD)
        to = lax.rem(my_cp + m, cp)
        return mesh_copy(
            parts.at[at_step, to],
            dkv_ref.at[my_cp, at_seq, :, :, columns],
            (step_send, step_recv),
            at_step * (cp - 1) + m - 1,
            {"cp": to},
        )

    def own_copy(at_seq, at_group, at_step):
        columns = pl.ds(pl.multiple_of(at_group * PACK * HD, PACK * HD), PACK * HD)
        return pltpu.make_async_copy(
            parts.at[at_step, my_cp], dkv_ref.at[my_cp, at_seq, :, :, columns], step_here.at[at_step]
        )

    seq = pl.program_id(0)
    blocks = 2 * kv_ref.shape[0]
    half = blocks * BLK // 2
    rows = GROUP * BLK
    at = place[seq]

    @pl.when(pl.program_id(1) == 0)
    def _():
        key = lax.broadcasted_iota(jnp.int32, (half, BLK), 0)
        query = lax.broadcasted_iota(jnp.int32, (half, BLK), 1)
        low_bias[...] = jnp.where(key <= query + at * BLK, 0.0, NEG)
        high_bias[...] = jnp.where(key + half <= query + (blocks - 1 - at) * BLK, 0.0, NEG)

    sort_blocks(table, seq, kv_ref, k_s, 0, blocks)
    sort_blocks(table, seq, kv_ref, v_s, 1, blocks)
    q_all = q_ref[...]
    g_all = g_ref[...]
    lows, highs, dks, dvs = [], [], [], []
    for j in range(PACK):
        k = k_s[:, j * HD : (j + 1) * HD]
        v = v_s[:, j * HD : (j + 1) * HD]
        q = stack_heads(q_all, j * GROUP, SCALE)
        g = stack_heads(g_all, j * GROUP)

        def probs(s_parts):
            peak = jnp.max(s_parts[0], axis=0, keepdims=True)
            for s in s_parts[1:]:
                peak = jnp.maximum(peak, jnp.max(s, axis=0, keepdims=True))
            es = [jnp.exp(s - peak) for s in s_parts]
            total = jnp.sum(es[0], axis=0, keepdims=True)
            for e in es[1:]:
                total = total + jnp.sum(e, axis=0, keepdims=True)
            part = 1.0 / total
            return [e * part for e in es]

        def score_grads(ps, dps):
            inner = jnp.sum(ps[0] * dps[0], axis=0, keepdims=True)
            for p, d in zip(ps[1:], dps[1:]):
                inner = inner + jnp.sum(p * d, axis=0, keepdims=True)
            return [(p * (d - inner)).astype(BF16) for p, d in zip(ps, dps)]

        s_low = dot(k[:half], q[:rows], 1, 1) + jnp.concatenate([low_bias[...]] * GROUP, axis=1)
        (p_low,) = probs([s_low])
        (d_low,) = score_grads([p_low], [dot(v[:half], g[:rows], 1, 1)])
        dv_one = dot(p_low.astype(BF16), g[:rows])
        dk_one = dot(d_low, q[:rows])
        lows.append((dot(d_low, k[:half], 0, 0) * SCALE).astype(BF16))

        s_one = dot(k[:half], q[rows:], 1, 1)
        s_two = dot(k[half:], q[rows:], 1, 1) + jnp.concatenate([high_bias[...]] * GROUP, axis=1)
        p_one, p_two = probs([s_one, s_two])
        d_one, d_two = score_grads(
            [p_one, p_two], [dot(v[:half], g[rows:], 1, 1), dot(v[half:], g[rows:], 1, 1)]
        )
        dv_one = dv_one + dot(p_one.astype(BF16), g[rows:])
        dv_two = dot(p_two.astype(BF16), g[rows:])
        dk_one = dk_one + dot(d_one, q[rows:])
        dk_two = dot(d_two, q[rows:])
        highs.append(
            ((dot(d_one, k[:half], 0, 0) + dot(d_two, k[half:], 0, 0)) * SCALE).astype(BF16)
        )
        dks.append(jnp.concatenate([dk_one, dk_two], axis=0).astype(BF16))
        dvs.append(jnp.concatenate([dv_one, dv_two], axis=0).astype(BF16))
    dq_ref[...] = unstack_heads(lows, highs)
    k_s[...] = jnp.concatenate(dks, axis=1)
    v_s[...] = jnp.concatenate(dvs, axis=1)
    for c in range(cp):
        for h in range(2):
            at_b = pl.ds(inverse[seq, 2 * c + h] * BLK, BLK)
            parts[step, c, 0, h * BLK : (h + 1) * BLK, :] = k_s[at_b, :]
            parts[step, c, 1, h * BLK : (h + 1) * BLK, :] = v_s[at_b, :]
    for m in range(1, cp):
        step_copy(seq, pl.program_id(1), step, m).start()
    own_copy(seq, pl.program_id(1), step).start()

    @pl.when(step == last)
    def _():
        @pl.loop(0, last + 1)
        def _(i):
            at_seq, at_group = i // groups, lax.rem(i, groups)
            for m in range(1, cp):
                step_copy(at_seq, at_group, i, m).wait()
            own_copy(at_seq, at_group, i).wait()

        office.end(kinds, ins, outs)


ATTENTION_COST = pl.CostEstimate(flops=2**34, bytes_accessed=2**24, transcendentals=2**24)


def attention_specs(kv):
    cp, n_seq = kv.shape[:2]
    row = pl.BlockSpec((2 * BLK, PACK * GROUP * HD), lambda s, g, *_: (s, g))
    whole = pl.BlockSpec((cp, 1, 2, 2 * BLK, PACK * HD), lambda s, g, *_: (0, s, 0, 0, g))
    return row, whole, (n_seq, KV // PACK), cp * 2 * BLK


def attend(table, place, q, kv):
    row, whole, grid, keys = attention_specs(kv)
    return pl.pallas_call(
        attend_kernel,
        grid_spec=pltpu.PrefetchScalarGridSpec(
            num_scalar_prefetch=2,
            grid=grid,
            in_specs=[row, whole],
            out_specs=row,
            scratch_shapes=[pltpu.VMEM((keys, PACK * HD), BF16)] * 2
            + [pltpu.VMEM((BLK, keys // 2), F32)] * 2,
        ),
        out_shape=jax.ShapeDtypeStruct(q.shape, BF16),
        compiler_params=pltpu.CompilerParams(
            dimension_semantics=("arbitrary", "arbitrary"), vmem_limit_bytes=56 * 2**20
        ),
        cost_estimate=ATTENTION_COST,
    )(table, place, q, kv)


def attend_back(collective_id, table, inverse, place, q, kv, grad, *jobs):
    row, whole, grid, keys = attention_specs(kv)
    sizes = tuple(lax.axis_size(a) for a in DENSE)
    cp = sizes[2]
    steps = grid[0] * grid[1]
    kinds, arrays, shapes = courier_jobs(sizes, jobs)
    smem = pl.BlockSpec(memory_space=pltpu.SMEM)
    hbm = pl.BlockSpec(memory_space=pl.ANY)
    n = jobs_messages(kinds, *sizes)
    return pl.pallas_call(
        functools.partial(attend_back_kernel, sizes, kinds),
        grid=grid,
        in_specs=[smem, smem, smem, row, whole, row] + [hbm] * len(jobs),
        out_specs=[row, hbm] + [hbm] * len(jobs),
        out_shape=[
            jax.ShapeDtypeStruct(q.shape, BF16),
            jax.ShapeDtypeStruct(kv.shape, BF16),
        ]
        + shapes,
        scratch_shapes=[pltpu.VMEM((keys, PACK * HD), BF16)] * 2
        + [pltpu.VMEM((keys // 2, BLK), F32)] * 2
        + [pltpu.VMEM((steps, cp, 2, 2 * BLK, PACK * HD), BF16)]
        + post_scratch(n, len(jobs))
        + [
            pltpu.SemaphoreType.DMA((steps * (cp - 1),)),
            pltpu.SemaphoreType.DMA((steps * (cp - 1),)),
            pltpu.SemaphoreType.DMA((steps,)),
        ],
        compiler_params=pltpu.CompilerParams(
            dimension_semantics=("arbitrary", "arbitrary"),
            vmem_limit_bytes=56 * 2**20,
            collective_id=collective_id,
            has_side_effects=True,
        ),
        cost_estimate=ATTENTION_COST,
    )(table, inverse, place, q, kv, grad, *arrays)


def tie(x, *others):
    return lax.optimization_barrier((x,) + others)[0]


def mesh_copy(src, dst, sems, at, device):
    send, recv = sems
    return pltpu.make_async_remote_copy(
        src_ref=src, dst_ref=dst, send_sem=send.at[at], recv_sem=recv.at[at],
        device_id=device, device_id_type=pl.DeviceIdType.MESH,
    )


def jobs_messages(kinds, hi, ep, cp):
    f, e = hi * ep, ep * cp
    counts = {
        "gather": f // 2 - 1 + (f // 2) * (cp - 1) + (f // 2) * cp,
        "expert": f - 1, "owners": f - 1, "tokens": e - 1, "peers": cp - 1, "quad": ep - 1,
    }
    return sum(counts[k] for k in kinds)


def post_scratch(n, jobs):
    return [
        pltpu.SemaphoreType.DMA((max(n, 1),)),
        pltpu.SemaphoreType.DMA((max(n, 1),)),
        pltpu.SemaphoreType.DMA((max(jobs, 1),)),
    ]


def plus(a, b, size):
    return lax.rem(a + b, size)


def flip(a, bits):
    out = a
    for bit in range(bits.bit_length()):
        if bits >> bit & 1:
            out = out + (1 << bit) - (1 << (bit + 1)) * lax.rem(a // (1 << bit), 2)
    return out


class PostOffice:
    def __init__(self, sizes, sems):
        self.hi, self.ep, self.cp = sizes
        self.fsdp = self.hi * self.ep
        self.send, self.recv, self.here = sems
        self.my_ep, self.my_cp = lax.axis_index("ep"), lax.axis_index("cp")
        self.me = lax.axis_index("hi") * self.ep + self.my_ep
        self.sibling = flip(self.me, 1)

    def at_fsdp(self, f):
        return {"hi": f // self.ep, "ep": lax.rem(f, self.ep)}

    def greet(self, kinds):
        barrier = pltpu.get_barrier_semaphore()
        partners = [self.at_fsdp(plus(self.me, k, self.fsdp)) for k in range(1, self.fsdp)]
        partners += [{"cp": plus(self.my_cp, k, self.cp)} for k in range(1, self.cp)]
        if "tokens" in kinds:
            partners += [
                {"ep": plus(self.my_ep, a, self.ep), "cp": plus(self.my_cp, b, self.cp)}
                for a in range(1, self.ep)
                for b in range(1, self.cp)
            ]
        for p in partners:
            pl.semaphore_signal(barrier, inc=1, device_id=p, device_id_type=pl.DeviceIdType.MESH)
        pl.semaphore_wait(barrier, len(partners))

    def copies(self, kinds, ins, outs, only=None):
        me, my_ep, my_cp, ep, cp, fsdp = (
            self.me, self.my_ep, self.my_cp, self.ep, self.cp, self.fsdp
        )
        away, local, count = [], [], {"away": 0, "here": 0}

        def post(src, dst, device):
            if only is None or job in only:
                away.append(mesh_copy(src, dst, (self.send, self.recv), count["away"], device))
            count["away"] += 1

        def keep(src, dst):
            if only is None or job in only:
                local.append(pltpu.make_async_copy(src, dst, self.here.at[count["here"]]))
            count["here"] += 1

        for job, (kind, x, out) in enumerate(zip(kinds, ins, outs)):
            if kind == "expert":
                rows = x.shape[1]
                at = pl.ds(pl.multiple_of(me * rows, rows), rows)
                for k in range(1, fsdp):
                    to = plus(me, k, fsdp)
                    post(x.at[lax.rem(to, ep)], out.at[at], self.at_fsdp(to))
                keep(x.at[my_ep], out.at[at])
            elif kind == "owners":
                rows = out.shape[1]
                for k in range(1, fsdp):
                    to = plus(me, k, fsdp)
                    src = x.at[pl.ds(pl.multiple_of(to * rows, rows), rows)]
                    post(src, out.at[me], self.at_fsdp(to))
                keep(x.at[pl.ds(pl.multiple_of(me * rows, rows), rows)], out.at[me])
            elif kind == "quad":
                for k in range(1, ep):
                    to = plus(my_ep, k, ep)
                    post(x.at[to], out.at[my_ep], {"ep": to})
                keep(x.at[my_ep], out.at[my_ep])
            elif kind == "peers":
                for m in range(1, cp):
                    post(x, out.at[my_cp], {"cp": plus(my_cp, m, cp)})
                keep(x, out.at[my_cp])
            elif kind == "tokens":
                for a in range(ep):
                    for b in range(cp):
                        if a or b:
                            to_ep, to_cp = plus(my_ep, a, ep), plus(my_cp, b, cp)
                            post(
                                x.at[to_cp * ep + to_ep],
                                out.at[my_cp * ep + my_ep],
                                {"ep": to_ep, "cp": to_cp},
                            )
                keep(x.at[my_cp * ep + my_ep], out.at[my_cp * ep + my_ep])
        return away, local

    def begin(self, *jobs):
        for group in self.copies(*jobs):
            for c in group:
                c.start()

    def end(self, *jobs):
        for group in self.copies(*jobs):
            for c in group:
                c.wait()

    def gather(self, x, out, first, here):
        me, my_cp, cp, fsdp = self.me, self.my_cp, self.cp, self.fsdp
        sent, across, mirrored = [], [], []

        def post(src, dst, device):
            c = mesh_copy(src, dst, (self.send, self.recv), first + len(sent), device)
            c.start()
            sent.append(c)
            return c

        def row(f, c):
            return out.at[f * cp + c]

        def share(f, src):
            for m in range(1, cp):
                across.append((f, m, post(src, row(f, my_cp), {"cp": plus(my_cp, m, cp)})))
            mirrored.append(post(src, row(f, my_cp), self.at_fsdp(self.sibling)))

        z = post(x, row(me, my_cp), self.at_fsdp(flip(me, 2)))
        own = pltpu.make_async_copy(x, row(me, my_cp), self.here.at[here])
        own.start()
        share(me, x)
        for k in range(1, fsdp // 2):
            yield
            z.wait_recv()
            if k + 1 < fsdp // 2:
                z = post(x, row(me, my_cp), self.at_fsdp(flip(me, 2 * k + 2)))
            f = flip(me, 2 * k)
            share(f, row(f, my_cp))
        yield
        for f, m, c in across:
            c.wait_recv()
            got = row(f, plus(my_cp, cp - m, cp))
            mirrored.append(post(got, got, self.at_fsdp(self.sibling)))
        for c in mirrored:
            c.wait_recv()
        for c in sent:
            c.wait_send()
        own.wait()

    def column_steps(self):
        return self.fsdp // 2


def steps(generator, count):
    for _ in range(count):
        next(generator, None)


def courier_jobs(sizes, jobs):
    hi, ep, cp = sizes
    shapes = []
    for kind, x in jobs:
        if kind == "gather":
            shape = (hi * ep * cp,) + x.shape
        elif kind == "expert":
            shape = (hi * ep * x.shape[1],) + x.shape[2:]
        elif kind == "owners":
            shape = (hi * ep, x.shape[0] // (hi * ep)) + x.shape[1:]
        elif kind == "peers":
            shape = (cp,) + x.shape
        else:
            shape = x.shape
        shapes.append(jax.ShapeDtypeStruct(shape, x.dtype))
    return [k for k, _ in jobs], [x for _, x in jobs], shapes


def courier_kernel(sizes, kinds, *refs):
    n = len(kinds)
    ins, outs = refs[:n], refs[n : 2 * n]
    office = PostOffice(sizes, refs[2 * n :])
    office.greet(kinds)
    first, here, gathers = jobs_messages([k for k in kinds if k != "gather"], *sizes), 0, []
    here = len([k for k in kinds if k != "gather"])
    for kind, x, out in zip(kinds, ins, outs):
        if kind == "gather":
            gathers.append(office.gather(x, out, first, here))
            first, here = first + jobs_messages(["gather"], *sizes), here + 1
            steps(gathers[-1], office.column_steps())
    office.begin(kinds, ins, outs)
    for g in gathers:
        steps(g, 1)
    office.end(kinds, ins, outs)


def courier(collective_id, *jobs):
    sizes = tuple(lax.axis_size(a) for a in DENSE)
    kinds, arrays, shapes = courier_jobs(sizes, jobs)
    hbm = pl.BlockSpec(memory_space=pl.ANY)
    return pl.pallas_call(
        functools.partial(courier_kernel, sizes, kinds),
        out_shape=shapes,
        in_specs=[hbm] * len(jobs),
        out_specs=[hbm] * len(jobs),
        scratch_shapes=post_scratch(jobs_messages(kinds, *sizes), len(jobs)),
        compiler_params=pltpu.CompilerParams(collective_id=collective_id, has_side_effects=True),
    )(*arrays)


def three_parts(x):
    high = x.astype(BF16).astype(F32)
    middle = (x - high).astype(BF16).astype(F32)
    low = x - high - middle
    lane = lax.broadcasted_iota(jnp.int32, (x.shape[0], 128), 1)
    out = jnp.where(lane == 0, high, jnp.where(lane == 1, middle, jnp.where(lane == 2, low, 0.0)))
    return out.astype(BF16)


STAGES = ((0, 3), (), (1, 2), ())


def front_kernel(sizes, kinds, table, place, x_ref, routes_ref, slots_ref, shard_ref, shard2_ref, *refs):
    n = len(kinds)
    ins, refs = refs[:n], refs[n:]
    a_ref, q_ref, o_ref, middle_ref, b_ref, gates_ref = refs[:6]
    kv_ref, w_ref, w2_ref, rows_ref, rows_gate_ref = refs[6:11]
    outs, rest = refs[11 : n + 11], refs[n + 11 :]
    w_all, w2_all, kv_mine, k_s, v_s, low_bias, high_bias, send_s, gate_s = rest[:9]
    office = PostOffice(sizes, rest[9:12])
    kv_send, kv_recv, kv_here, row_send, row_recv = rest[12:17]
    kv_bufs = rest[17:]
    _, ep, cp = sizes
    n_seq, my_cp = len(kv_bufs), office.my_cp
    rows = 2 * BLK
    wide = KV * HD
    office.greet(kinds)
    base = jobs_messages(kinds, *sizes)

    def begin(stage):
        if STAGES[stage]:
            office.begin(kinds, ins, outs, STAGES[stage])

    gather = office.gather(shard_ref, w_all, base, n)
    gather2 = office.gather(shard2_ref, w2_all, base + jobs_messages(["gather"], *sizes), n + 1)
    steps(gather, office.column_steps())
    begin(0)
    x = x_ref[...].astype(F32)
    x = x * lax.rsqrt(jnp.mean(x * x, axis=-1, keepdims=True) + EPS)
    steps(gather, 1)
    begin(1)
    steps(gather2, 1)
    depth = x.shape[1]
    keep_w = pltpu.make_async_copy(w_all, w_ref, kv_here.at[2 * n_seq])
    keep_w.start()

    def column(w, first):
        return w[:, :, pl.ds(first, 128)].reshape(depth, 128)

    gain = column(w_all, H * HD + 2 * wide).astype(F32).T[:1]
    a_ref[...] = (x * gain).astype(BF16)

    def project(first):
        return dot(a_ref[...], w_all[:, :, pl.ds(first, wide)].reshape(depth, wide)).astype(BF16)

    for part in range(2):
        piece = project(H * HD + part * wide)
        for s in range(n_seq):
            kv_mine[s, part] = piece[s * rows : (s + 1) * rows]
    copies = []
    for s in range(n_seq):
        group = [
            mesh_copy(
                kv_mine.at[s],
                kv_bufs[s].at[my_cp],
                (kv_send, kv_recv),
                s * (cp - 1) + m - 1,
                {"cp": plus(my_cp, m, cp)},
            )
            for m in range(1, cp)
        ]
        group.append(pltpu.make_async_copy(kv_mine.at[s], kv_bufs[s].at[my_cp], kv_here.at[s]))
        for c in group:
            c.start()
        copies.append(group)
    steps(gather2, 1)

    @pl.loop(0, H * HD // wide)
    def _(t):
        first = pl.multiple_of(t * wide, wide)
        q_ref[:, pl.ds(first, wide)] = project(first)

    steps(gather2, 1)
    keeps = []
    for s in range(n_seq):
        for c in copies[s]:
            c.wait()
        keep = pltpu.make_async_copy(kv_bufs[s], kv_ref.at[:, s], kv_here.at[n_seq + s])
        keep.start()
        keeps.append(keep)
        for b in range(2 * cp):
            at = table[s, b]
            to = pl.ds(b * BLK, BLK)
            source = pl.ds((at % 2) * BLK, BLK)
            k_s[to, :] = kv_bufs[s][at // 2, 0, source, :]
            v_s[to, :] = kv_bufs[s][at // 2, 1, source, :]
        if s == n_seq - 1:
            begin(2)
        low_bias[...], high_bias[...] = query_bias(place[s], 2 * cp)

        @pl.loop(0, KV // PACK)
        def _(g, s=s):
            head = pl.ds(pl.multiple_of(g * PACK * HD, PACK * HD), PACK * HD)
            group = PACK * GROUP * HD
            heads = pl.ds(pl.multiple_of(g * group, group), group)
            at = pl.ds(s * rows, rows)
            o_ref[at, heads] = attend_group(
                q_ref[at, heads], k_s[:, head], v_s[:, head], low_bias[...], high_bias[...]
            )

        steps(gather2, 1)

    begin(3)
    steps(gather2, office.column_steps())
    keep_w2 = pltpu.make_async_copy(w2_all, w2_ref, kv_here.at[2 * n_seq + 1])
    keep_w2.start()

    @pl.loop(0, depth // wide)
    def _(t):
        cols = pl.ds(pl.multiple_of(t * wide, wide), wide)
        out = dot(o_ref[...], w2_all[:, :, cols].reshape(H * HD, wide))
        middle_ref[:, cols] = x_ref[:, cols].astype(F32) + out

    middle = middle_ref[...]
    last = column(w2_all, depth)
    gain = last.astype(F32).T[EXPERTS : EXPERTS + 1]
    b_ref[...] = (
        middle * lax.rsqrt(jnp.mean(middle * middle, axis=-1, keepdims=True) + EPS) * gain
    ).astype(BF16)
    logits = dot(b_ref[...], last)
    lane = lax.broadcasted_iota(jnp.int32, logits.shape, 1)
    picked = [
        jnp.sum(jnp.where(lane == routes_ref[:, r : r + 1], logits, 0.0), axis=1, keepdims=True)
        for r in range(2)
    ]
    top = jnp.maximum(picked[0], picked[1])
    powers = [jnp.exp(p - top) for p in picked]
    gates = [p / (powers[0] + powers[1]) for p in powers]
    both = jnp.where(lane == 0, gates[0], jnp.where(lane == 1, gates[1], 0.0))
    gates_ref[...] = both
    gate_rows = both.T[:2]
    count = EXPERTS
    cap = send_s.shape[1]
    mine = my_cp * ep + office.my_ep

    def away(k, lane):
        to = lax.rem(mine + 1 + k, count)
        src, dst = ((send_s, rows_ref), (gate_s, rows_gate_ref))[lane]
        return mesh_copy(
            src.at[k],
            dst.at[mine],
            (row_send, row_recv),
            2 * k + lane,
            {"cp": to // ep, "ep": lax.rem(to, ep)},
        )

    @pl.loop(0, count)
    def _(k):
        first = lax.rem(mine + 1 + k, count) * cap
        ids = lax.broadcasted_iota(jnp.int32, (cap, slots_ref.shape[1]), 0) + first
        at = [slots_ref[r : r + 1, :] == ids for r in range(2)]
        chosen = jnp.where(at[0] | at[1], 1.0, 0.0).astype(BF16)
        send_s[k] = dot(chosen, b_ref[...]).astype(BF16)
        gate = sum(jnp.where(at[r], gate_rows[r : r + 1], 0.0) for r in range(2))
        gate_s[k] = three_parts(jnp.sum(gate, axis=1, keepdims=True))

        @pl.when(k < count - 1)
        def _():
            away(k, 0).start()
            away(k, 1).start()

    own = [
        pltpu.make_async_copy(src.at[count - 1], dst.at[mine], kv_here.at[2 * n_seq + 2 + i])
        for i, (src, dst) in enumerate(((send_s, rows_ref), (gate_s, rows_gate_ref)))
    ]
    for c in own:
        c.start()
    for c in own + keeps + [keep_w, keep_w2]:
        c.wait()
    for k in range(count - 1):
        away(k, 0).wait()
        away(k, 1).wait()
    office.end(kinds, ins, outs)


def front(collective_id, table, place, x, routes, slots, shard, shard2, *jobs):
    sizes = tuple(lax.axis_size(a) for a in DENSE)
    hi, ep, cp = sizes
    n_seq = table.shape[0]
    kinds, arrays, shapes = courier_jobs(sizes, jobs)
    rows, wide = 2 * BLK, KV * HD
    whole, whole2 = ((hi * ep * cp,) + s.shape for s in (shard, shard2))
    hbm = pl.BlockSpec(memory_space=pl.ANY)
    vmem = pl.BlockSpec(memory_space=pltpu.VMEM)
    smem = pl.BlockSpec(memory_space=pltpu.SMEM)
    keys = cp * rows
    tokens, width = x.shape
    sent = (EXPERTS, n_seq * CAP, width)
    sent_gate = (EXPERTS, n_seq * CAP, 128)

    def sems(count):
        return pltpu.SemaphoreType.DMA((count,))

    return pl.pallas_call(
        functools.partial(front_kernel, sizes, kinds),
        in_specs=[smem, smem, vmem, vmem, vmem, hbm, hbm] + [hbm] * len(jobs),
        out_specs=[vmem] * 6 + [hbm] * 5 + [hbm] * len(jobs),
        out_shape=[jax.ShapeDtypeStruct(x.shape, BF16)] * 3
        + [
            jax.ShapeDtypeStruct(x.shape, F32),
            jax.ShapeDtypeStruct(x.shape, BF16),
            jax.ShapeDtypeStruct((tokens, 128), F32),
            jax.ShapeDtypeStruct((cp, n_seq, 2, rows, wide), BF16),
            jax.ShapeDtypeStruct(whole, BF16),
            jax.ShapeDtypeStruct(whole2, BF16),
            jax.ShapeDtypeStruct(sent, BF16),
            jax.ShapeDtypeStruct(sent_gate, BF16),
        ]
        + shapes,
        scratch_shapes=[
            pltpu.VMEM(whole, BF16),
            pltpu.VMEM(whole2, BF16),
            pltpu.VMEM((n_seq, 2, rows, wide), BF16),
            pltpu.VMEM((keys, wide), BF16),
            pltpu.VMEM((keys, wide), BF16),
            pltpu.VMEM((BLK, keys // 2), F32),
            pltpu.VMEM((BLK, keys // 2), F32),
            pltpu.VMEM(sent, BF16),
            pltpu.VMEM(sent_gate, BF16),
        ]
        + post_scratch(jobs_messages(kinds + ["gather"] * 2, *sizes), len(jobs) + 2)
        + [
            sems(n_seq * (cp - 1)),
            sems(n_seq * (cp - 1)),
            sems(2 * n_seq + 4),
            sems(2 * EXPERTS),
            sems(2 * EXPERTS),
        ]
        + [pltpu.VMEM((cp, 2, rows, wide), BF16)] * n_seq,
        compiler_params=pltpu.CompilerParams(
            collective_id=collective_id, has_side_effects=True, vmem_limit_bytes=60 * 2**20
        ),
        cost_estimate=ATTENTION_COST,
    )(table, place, x, routes, slots, shard, shard2, *arrays)


STAGE_SUM = 0


def dense_sum_kernel(sizes, kinds, n_parts, slots_ref, gates_ref, returned_hbm, middle_hbm, *refs):
    n = len(kinds)
    parts, refs = refs[:n_parts], refs[n_parts:]
    widths = [p.shape[2] for p in parts]
    columns = [pl.ds(sum(widths[:j]), w) for j, w in enumerate(widths)]
    ins, out, final_ref, outs, rest = (
        refs[:n], refs[n], refs[n + 1], refs[n + 2 : 2 * n + 2], refs[2 * n + 2 :]
    )
    mine, from_core, summed, from_peers, rows_out, from_column, returned_s, middle_s = rest[:8]
    office = PostOffice(sizes, rest[8:11])
    load_sem, combine_sem = rest[11:13]
    core_sems, peer_sems, column_sems = rest[13:15], rest[15:17], rest[17:19]
    cp, columns_n = sizes[2], office.fsdp // 2
    me, my_cp = office.me, office.my_cp
    office.greet(kinds)
    core = lax.rem(me, 2)
    targets = [flip(me, 2 * k) for k in range(columns_n - 1, -1, -1)]
    loads, cores = [], []
    for i, f in enumerate(targets):
        other = flip(f, 1)
        for j, (part, where) in enumerate(zip(parts, columns)):
            c = mesh_copy(
                part.at[pl.ds(other * cp, cp)],
                from_core.at[i, :, :, where],
                core_sems,
                i * n_parts + j,
                office.at_fsdp(office.sibling),
            )
            c.start()
            cores.append(c)
            c = pltpu.make_async_copy(
                part.at[pl.ds(f * cp, cp)], mine.at[i, :, :, where], load_sem.at[i * n_parts + j]
            )
            c.start()
            loads.append(c)
    fetch = [
        pltpu.make_async_copy(src, dst, combine_sem.at[i])
        for i, (src, dst) in enumerate(((returned_hbm, returned_s), (middle_hbm, middle_s)))
    ]
    for c in fetch:
        c.start()
    peers = []
    for i in range(columns_n):
        for c in loads[i * n_parts : (i + 1) * n_parts] + cores[i * n_parts : (i + 1) * n_parts]:
            c.wait()
        summed[i] = (mine[i].astype(F32) + from_core[i].astype(F32)).astype(BF16)
        row = []
        for m in range(1, cp):
            to = plus(my_cp, m, cp)
            c = mesh_copy(
                summed.at[i, to], from_peers.at[i, m - 1], peer_sems, i * (cp - 1) + m - 1, {"cp": to}
            )
            c.start()
            row.append(c)
        peers.append(row)
        if i == STAGE_SUM:
            office.begin(kinds, ins, outs)
    for c in fetch:
        c.wait()
    tokens, width = middle_s.shape
    slot = lax.broadcasted_iota(jnp.int32, (tokens, returned_s.shape[0]), 1)
    takes = [(slots_ref[:, r : r + 1] == slot).astype(F32).astype(BF16) for r in range(2)]
    for d in range(0, width, 512):
        cols = slice(d, d + 512)
        final = middle_s[:, cols]
        for r in range(2):
            final = final + gates_ref[:, r : r + 1] * dot(takes[r], returned_s[:, cols])
        final_ref[:, cols] = final.astype(BF16)
    column = []
    total = None
    for i, f in enumerate(targets):
        total = summed[i, my_cp].astype(F32)
        for m, c in enumerate(peers[i], 1):
            c.wait_recv()
            total = total + from_peers[i, m - 1].astype(F32)
        if i < columns_n - 1:
            rows_out[i] = total.astype(BF16)
            c = mesh_copy(
                rows_out.at[i], from_column.at[i], column_sems, i, office.at_fsdp(f)
            )
            c.start()
            column.append(c)
    for i, c in enumerate(column):
        c.wait_recv()
        total = total + from_column[i].astype(F32)
    out[...] = total
    for c in column + [c for row in peers for c in row]:
        c.wait_send()
    office.end(kinds, ins, outs)


def dense_sum(collective_id, parts, slots, gates, returned, middle, *jobs):
    sizes = tuple(lax.axis_size(a) for a in DENSE)
    hi, ep, cp = sizes
    column = hi * ep // 2
    rows = parts[0].shape[0] // (hi * ep * cp)
    width = sum(p.shape[1] for p in parts)
    kinds, arrays, shapes = courier_jobs(sizes, jobs)
    hbm = pl.BlockSpec(memory_space=pl.ANY)
    vmem = pl.BlockSpec(memory_space=pltpu.VMEM)

    def sems(count):
        return [pltpu.SemaphoreType.DMA((count,))] * 2

    return pl.pallas_call(
        functools.partial(dense_sum_kernel, sizes, kinds, len(parts)),
        out_shape=[
            jax.ShapeDtypeStruct((rows, width), F32),
            jax.ShapeDtypeStruct(middle.shape, BF16),
        ]
        + shapes,
        in_specs=[vmem] * 2 + [hbm] * (2 + len(parts) + len(jobs)),
        out_specs=[vmem] * 2 + [hbm] * len(jobs),
        scratch_shapes=[
            pltpu.VMEM((column, cp, rows, width), BF16),
            pltpu.VMEM((column, cp, rows, width), BF16),
            pltpu.VMEM((column, cp, rows, width), BF16),
            pltpu.VMEM((column, cp - 1, rows, width), BF16),
            pltpu.VMEM((column - 1, rows, width), BF16),
            pltpu.VMEM((column - 1, rows, width), BF16),
            pltpu.VMEM(returned.shape, BF16),
            pltpu.VMEM(middle.shape, F32),
        ]
        + post_scratch(jobs_messages(kinds, *sizes), len(jobs))
        + [pltpu.SemaphoreType.DMA((column * len(parts),)), pltpu.SemaphoreType.DMA((2,))]
        + sems(column * len(parts))
        + sems(column * (cp - 1))
        + sems(column - 1),
        compiler_params=pltpu.CompilerParams(
            collective_id=collective_id, has_side_effects=True, vmem_limit_bytes=56 * 2**20
        ),
    )(slots, gates, returned, middle, *(p.reshape(-1, rows, p.shape[1]) for p in parts), *arrays)


def swap(x):
    hi = lax.axis_size("hi")
    xs = x if isinstance(x, list) else [x] * (hi - 1)
    return [
        lax.ppermute(xs[k - 1], "hi", [(i, (i + k) % hi) for i in range(hi)]) for k in range(1, hi)
    ]


def after(k):
    return lax.rem(lax.axis_index("hi") + k, lax.axis_size("hi"))


def half_rows(x):
    rows = x.shape[0] // lax.axis_size("hi")
    parts = [
        lax.dynamic_slice_in_dim(x, after(k) * rows, rows, axis=0)
        for k in range(lax.axis_size("hi"))
    ]
    return parts[0], parts[1:]


def expert_kernel(
    sizes,
    group,
    x_hbm,
    dy_hbm,
    gate_hbm,
    up_hbm,
    down_hbm,
    scale_ref,
    back_ref,
    inner_ref,
    e_ref,
    gate_out,
    up_out,
    down_out,
    x_s,
    dy_s,
    gate_w,
    up_w,
    down_w,
    hidden_s,
    dg_s,
    du_s,
    back_s,
    inner_s,
    e_s,
    load_sem,
    weight_sem,
    send,
    recv,
    out_sem,
):
    _, ep, cp = sizes
    n, cap, width = x_hbm.shape
    depth = hidden_s.shape[1]
    me = lax.axis_index("cp") * ep + lax.axis_index("ep")

    def source(k):
        return lax.rem(me + 1 + k, n)

    def device(at):
        return {"cp": at // ep, "ep": lax.rem(at, ep)}

    barrier = pltpu.get_barrier_semaphore()
    for k in range(n - 1):
        pl.semaphore_signal(
            barrier, inc=1, device_id=device(source(k)), device_id_type=pl.DeviceIdType.MESH
        )
    weights = [
        pltpu.make_async_copy(src, dst, weight_sem.at[i])
        for i, (src, dst) in enumerate(
            ((gate_hbm, gate_w), (up_hbm, up_w), (down_hbm, down_w))
        )
    ]
    loads = []
    for c in weights[:2]:
        c.start()
    for k in range(n):
        pair = [
            pltpu.make_async_copy(src.at[source(k)], dst.at[k], load_sem.at[2 * k + i])
            for i, (src, dst) in enumerate(((x_hbm, x_s), (dy_hbm, dy_s)))
        ]
        for c in pair:
            c.start()
        loads.append(pair)
    weights[2].start()
    for pair in loads:
        for c in pair:
            c.wait()
    for c in weights:
        c.wait()
    pl.semaphore_wait(barrier, n - 1)

    def away(k, src, dst, lane):
        return pltpu.make_async_remote_copy(
            src_ref=src.at[k],
            dst_ref=dst.at[me],
            send_sem=send.at[2 * k + lane],
            recv_sem=recv.at[2 * k + lane],
            device_id=device(source(k)),
            device_id_type=pl.DeviceIdType.MESH,
        )

    def here(src, dst, lane):
        return pltpu.make_async_copy(src.at[n - 1], dst.at[me], out_sem.at[lane])

    def keep_e(k):
        return pltpu.make_async_copy(e_s.at[k], e_ref.at[source(k)], out_sem.at[2 + k])

    tile = group * cap
    chunk = min(512, depth)

    @pl.loop(0, n // group)
    def _(t):
        first = pl.multiple_of(t * tile, tile)
        at = pl.ds(first, tile)
        k0 = t * group
        x = x_s[pl.ds(k0, group)].reshape(tile, width)
        dy = dy_s[pl.ds(k0, group)].reshape(tile, width)
        inner = jnp.zeros((tile, 1), F32)
        for f in range(0, depth, chunk):
            cols = slice(f, f + chunk)
            gate_pre = dot(x, gate_w[:, cols])
            up_pre = dot(x, up_w[:, cols])
            sigmoid_gate = jax.nn.sigmoid(gate_pre)
            swish = gate_pre * sigmoid_gate
            hidden = (swish * up_pre).astype(BF16)
            hidden_s[at, cols] = hidden
            hidden_grad = dot(dy, down_w[cols, :], 1, 1)
            inner = inner + jnp.sum(hidden_grad * hidden.astype(F32), axis=1, keepdims=True)
            slope = sigmoid_gate * (1.0 + gate_pre * (1.0 - sigmoid_gate))
            dg_s[at, cols] = (hidden_grad * up_pre * slope).astype(BF16)
            du_s[at, cols] = (hidden_grad * swish).astype(BF16)
        inner_s[pl.ds(k0, group)] = three_parts(inner).reshape(group, cap, 128)
        for d in range(0, width, 512):
            cols = slice(d, d + 512)
            back = dot(dg_s[at, :], gate_w[cols, :], 1, 1) + dot(du_s[at, :], up_w[cols, :], 1, 1)
            back_s[pl.ds(k0, group), :, cols] = back.astype(BF16).reshape(group, cap, 512)
        for i in range(group):
            k = k0 + i

            @pl.when(k < n - 1)
            def _():
                away(k, back_s, back_ref, 0).start()
                away(k, inner_s, inner_ref, 1).start()

        for d in range(0, width, 512):
            cols = slice(d, d + 512)
            e = dot(hidden_s[at, :], down_w[:, cols])
            e_s[pl.ds(k0, group), :, cols] = e.astype(BF16).reshape(group, cap, 512)
        for i in range(group):
            keep_e(k0 + i).start()

    here(back_s, back_ref, 0).start()
    here(inner_s, inner_ref, 1).start()
    for k in range(n):
        lanes = lax.broadcasted_iota(jnp.int32, (cap, 128), 1)
        gate = jnp.sum(
            jnp.where(lanes < 3, scale_ref[source(k)].astype(F32), 0.0), axis=1, keepdims=True
        )
        x_s[k] = (x_s[k].astype(F32) * gate).astype(BF16)
        dy_s[k] = (dy_s[k].astype(F32) * gate).astype(BF16)

    @pl.loop(0, width // 256)
    def _(d):
        cols = pl.ds(pl.multiple_of(d * 256, 256), 256)
        x = x_s[:, :, cols].reshape(n * cap, 256)
        gate_out[cols, :] = dot(x, dg_s[...], 0, 0).astype(BF16)
        up_out[cols, :] = dot(x, du_s[...], 0, 0).astype(BF16)

    @pl.loop(0, depth // 256)
    def _(f):
        cols = pl.ds(pl.multiple_of(f * 256, 256), 256)
        down_out[cols, :] = dot(
            hidden_s[:, cols], dy_s[...].reshape(n * cap, width), 0, 0
        ).astype(BF16)

    here(back_s, back_ref, 0).wait()
    here(inner_s, inner_ref, 1).wait()
    for k in range(n):
        keep_e(k).wait()
    for k in range(n - 1):
        away(k, back_s, back_ref, 0).wait()
        away(k, inner_s, inner_ref, 1).wait()


def expert(collective_id, x, dy, gate, up, down, scale):
    sizes = tuple(lax.axis_size(a) for a in DENSE)
    n, cap, width = x.shape
    depth = gate.shape[1]
    hbm = pl.BlockSpec(memory_space=pl.ANY)
    vmem = pl.BlockSpec(memory_space=pltpu.VMEM)
    rows = pltpu.VMEM(x.shape, BF16)
    tall = pltpu.VMEM((n * cap, depth), BF16)

    def sems(count):
        return pltpu.SemaphoreType.DMA((count,))

    return pl.pallas_call(
        functools.partial(expert_kernel, sizes, 4),
        in_specs=[hbm] * 5 + [vmem],
        out_specs=[hbm] * 3 + [vmem] * 3,
        out_shape=[
            jax.ShapeDtypeStruct(x.shape, BF16),
            jax.ShapeDtypeStruct((n, cap, 128), BF16),
            jax.ShapeDtypeStruct(x.shape, BF16),
            jax.ShapeDtypeStruct(gate.shape, BF16),
            jax.ShapeDtypeStruct(up.shape, BF16),
            jax.ShapeDtypeStruct(down.shape, BF16),
        ],
        scratch_shapes=[
            rows,
            rows,
            pltpu.VMEM(gate.shape, BF16),
            pltpu.VMEM(up.shape, BF16),
            pltpu.VMEM(down.shape, BF16),
            tall,
            tall,
            tall,
            rows,
            pltpu.VMEM((n, cap, 128), BF16),
            rows,
            sems(2 * n),
            sems(3),
            sems(2 * n),
            sems(2 * n),
            sems(2 + n),
        ],
        compiler_params=pltpu.CompilerParams(
            collective_id=collective_id, has_side_effects=True, vmem_limit_bytes=62 * 2**20
        ),
        cost_estimate=ATTENTION_COST,
    )(x, dy, gate, up, down, scale)


def rms_backward(rows, scale, gain, grad_norm):
    weighted = grad_norm * gain
    inner = jnp.mean(weighted * rows, axis=-1, keepdims=True)
    grad_rows = scale * weighted - rows * scale * scale * scale * inner
    return grad_rows, jnp.sum(grad_norm * rows * scale, axis=0)


def with_extra(main, *columns):
    rows = main.shape[0]
    columns = [c.reshape(rows, -1).astype(main.dtype) for c in columns]
    used = sum(c.shape[1] for c in columns)
    return jnp.concatenate([main, *columns, jnp.zeros((rows, -used % 128), main.dtype)], axis=1)


def local(
    layer_input,
    cotangent,
    pairing,
    routes,
    first_gain,
    second_gain,
    query_weight,
    key_weight,
    value_weight,
    out_weight,
    router_weight,
    gate_weight,
    up_weight,
    down_weight,
):
    n_seq = layer_input.shape[0]
    width = layer_input.shape[-1]
    rows = 2 * BLK
    tokens = n_seq * rows
    cp = lax.axis_size("cp")
    here = lax.axis_index("cp")
    blocks = 2 * cp
    n_q, n_kv = H * HD, KV * HD
    n_slots = EXPERTS * n_seq * CAP

    first = with_extra(
        jnp.concatenate([query_weight, key_weight, value_weight], axis=1), first_gain
    )
    second = with_extra(out_weight, router_weight, second_gain)
    n_first = n_q + 2 * n_kv

    chosen = routes.reshape(tokens, 2)
    experts = jnp.arange(EXPERTS, dtype=jnp.int32)
    picks = chosen[:, :, None] == experts[None, None, :]
    named = jnp.any(picks, axis=1).astype(BF16)
    token = jnp.arange(tokens, dtype=jnp.int32)
    earlier = (token[None, :] < token[:, None]) & (token[None, :] // rows == token[:, None] // rows)
    before = dot(earlier.astype(BF16), named)
    rank = jnp.sum(jnp.where(picks, before[:, None, :], 0.0), axis=-1).astype(jnp.int32)
    slots = (chosen * n_seq + (token // rows)[:, None]) * CAP + rank
    slot = jnp.arange(n_slots, dtype=jnp.int32)
    at_slot = [slots[:, r][None, :] == slot[:, None] for r in range(2)]
    place_rows = (at_slot[0] | at_slot[1]).astype(BF16)
    take_rows = [(slots[:, r][:, None] == slot[None, :]).astype(BF16) for r in range(2)]

    def exchange(x):
        x = x.reshape(EXPERTS, n_seq * CAP, -1)
        x = lax.all_to_all(x, ("cp", "ep"), split_axis=0, concat_axis=0, tiled=True)
        return x.reshape(n_slots, -1)

    def exchange_scalar(x):
        x = x.reshape(EXPERTS, 1, n_seq * CAP)
        x = lax.all_to_all(x, ("cp", "ep"), split_axis=0, concat_axis=0, tiled=True)
        return x.reshape(n_slots)

    grad_rows = dot(place_rows, cotangent.reshape(tokens, width)).astype(BF16)
    resid = layer_input.reshape(tokens, width).astype(F32)
    scale_one = lax.rsqrt(jnp.mean(resid * resid, axis=-1, keepdims=True) + EPS)
    ids = jnp.stack([pairing, blocks - 1 - pairing], axis=2).reshape(n_seq, blocks)
    order = jnp.arange(blocks, dtype=jnp.int32)
    table = jnp.sum(jnp.where(ids[:, :, None] == order, order[None, :, None], 0), axis=1)
    place = lax.dynamic_index_in_dim(pairing, here, axis=1, keepdims=False)
    pick_f = picks.astype(F32)
    weights = [("expert", w) for w in (gate_weight, up_weight, down_weight)]
    if first.shape[0] % 16 == 0:
        (
            attn_in,
            queries,
            attn_out,
            middle,
            moe_in,
            gates,
            kv_all,
            first,
            second,
            arrived,
            arrived_gate,
            gate_matrix,
            up_matrix,
            down_matrix,
            grad_rows,
        ) = front(
            0,
            table,
            place,
            layer_input.reshape(tokens, width),
            chosen,
            slots.T,
            first,
            second,
            *weights,
            ("tokens", grad_rows.reshape(EXPERTS, n_seq * CAP, width)),
        )
        gates = gates[:, :2]
        first = first.reshape(width, -1)
        second = second.reshape(n_q, -1)
    else:
        second = lax.all_gather(second, DENSE, axis=0, tiled=True)
        first, gate_matrix, down_matrix = courier(0, ("gather", first), weights[0], weights[2])
        first = first.reshape(width, -1)
        attn_in = (resid * scale_one * first[:, n_first].astype(F32)).astype(BF16)
        qkv = dot(attn_in, first[:, :n_first]).astype(BF16)
        queries = qkv[:, :n_q]
        kv = qkv[:, n_q:].reshape(n_seq, rows, 2, n_kv).transpose(0, 2, 1, 3)
        kv_all, up_matrix = courier(1, ("peers", kv), weights[1])
        grad_rows = exchange(tie(grad_rows, kv_all))
        attn_out = tie(attend(table, place, queries, kv_all), grad_rows)
        middle = resid + dot(attn_out, second[:, :width])
        scale_two = lax.rsqrt(jnp.mean(middle * middle, axis=-1, keepdims=True) + EPS)
        moe_in = (middle * scale_two * second[:, width + EXPERTS].astype(F32)).astype(BF16)
        logits = dot(moe_in, second[:, width : width + EXPERTS])
        picked = jnp.sum(pick_f * logits[:, None, :], axis=-1)
        powers = jnp.exp(picked - jnp.max(picked, axis=-1, keepdims=True))
        gates = powers / jnp.sum(powers, axis=-1, keepdims=True)
        gate_slot = jnp.sum(
            sum(jnp.where(at_slot[r], gates[:, r][None, :], 0.0) for r in range(2)), axis=1
        )
        arrived = exchange(dot(place_rows, moe_in).astype(BF16))
        rest, lanes = exchange_scalar(tie(gate_slot, arrived)), []
        for _ in range(3):
            lanes.append(lax.reduce_precision(rest, 8, 7))
            rest = rest - lanes[-1]
        arrived_gate = jnp.pad(jnp.stack(lanes, axis=1).astype(BF16), ((0, 0), (0, 125)))
    qkv_matrix = first[:, :n_first]
    gain_one = first[:, n_first].astype(F32)
    out_matrix = second[:, :width]
    router_matrix = second[:, width : width + EXPERTS]
    gain_two = second[:, width + EXPERTS].astype(F32)
    scale_two = lax.rsqrt(jnp.mean(middle * middle, axis=-1, keepdims=True) + EPS)

    shape = (EXPERTS, n_seq * CAP, width)
    grad_returned, inner, produced, gate_part, up_part, down_part = expert(
        4,
        arrived.reshape(shape),
        grad_rows.reshape(shape),
        gate_matrix,
        up_matrix,
        down_matrix,
        arrived_gate.reshape(EXPERTS, -1, 128),
    )
    grad_returned = grad_returned.reshape(n_slots, width)
    gate_inner = jnp.sum(inner[:, :, :3].astype(F32), axis=2).reshape(n_slots)
    down_own, down_sent = half_rows(down_part)
    down_sent = swap(down_sent)

    returned = exchange(tie(produced, grad_returned))
    grad_final = cotangent.reshape(tokens, width).astype(F32)
    gate_inner = jnp.stack(
        [jnp.sum(jnp.where(a, gate_inner[:, None], 0.0), axis=0) for a in at_slot], axis=1
    )
    pair_grad = gates * (gate_inner - jnp.sum(gates * gate_inner, axis=-1, keepdims=True))
    logit_grad = jnp.sum(pick_f * pair_grad[:, :, None], axis=1)
    moe_in_grad = jnp.dot(logit_grad, router_matrix.astype(F32).T, precision=HIGH)
    for r in range(2):
        moe_in_grad = moe_in_grad + gates[:, r : r + 1] * dot(take_rows[r], grad_returned)
    router_part = jnp.dot(moe_in.astype(F32).T, logit_grad, precision=HIGH)
    middle_norm_grad, gain_two_grad = rms_backward(middle, scale_two, gain_two, moe_in_grad)
    middle_grad = grad_final + middle_norm_grad
    branch_grad = middle_grad.astype(BF16)
    out_part = dot(attn_out, branch_grad, 0, 0).astype(BF16)
    attn_out_grad = dot(branch_grad, out_matrix, 1, 1).astype(BF16)
    attn_out_grad = tie(attn_out_grad, out_part)
    query_grad, kv_grad, gate_parts = attend_back(
        2, table, ids, place, queries, kv_all, attn_out_grad, ("owners", gate_part)
    )
    kv_grad = tie(kv_grad, returned, *down_sent)
    kv_grad = jnp.sum(kv_grad.astype(F32), axis=0).astype(BF16)
    kv_grad = kv_grad.transpose(0, 2, 1, 3).reshape(tokens, 2 * n_kv)
    qkv_grad = jnp.concatenate([query_grad, kv_grad], axis=1)
    first_part = dot(attn_in, qkv_grad, 0, 0).astype(BF16)
    attn_in_grad = dot(qkv_grad, qkv_matrix, 1, 1)
    resid_norm_grad, gain_one_grad = rms_backward(resid, scale_one, gain_one, attn_in_grad)
    input_grad = middle_grad + resid_norm_grad
    down_sum = tie(down_own, query_grad, returned).astype(F32) + sum(d.astype(F32) for d in down_sent)
    down_sum = down_sum.astype(BF16).reshape(down_weight.shape)

    def own_sum(parts):
        halves = parts.reshape((-1,) + gate_weight.shape)
        return jnp.sum(halves.astype(F32), axis=0)

    small_part = jnp.concatenate(
        [router_part, gain_one_grad[:, None], gain_two_grad[:, None]], axis=1
    ).astype(BF16)
    small_part = jnp.pad(small_part, ((0, 0), (0, -small_part.shape[1] % 128)))
    dense, layer_output, up_parts, down_sum = dense_sum(
        3,
        [first_part, out_part, small_part],
        slots,
        gates,
        returned,
        middle,
        ("owners", up_part),
        ("quad", down_sum),
    )
    at_small = n_first + width
    return (
        layer_output.reshape(layer_input.shape),
        input_grad.reshape(layer_input.shape),
        dense[:, at_small + EXPERTS],
        dense[:, at_small + EXPERTS + 1],
        dense[:, :n_q],
        dense[:, n_q : n_q + n_kv],
        dense[:, n_q + n_kv : n_first],
        dense[:, n_first:at_small],
        dense[:, at_small : at_small + EXPERTS],
        own_sum(gate_parts),
        own_sum(up_parts),
        down_sum.astype(F32),
    )


def solution(mesh):
    fsdp, cp = mesh.shape["fsdp"], mesh.shape["cp"]
    ep = EXPERTS // cp
    finer = Mesh(mesh.devices.reshape(fsdp // ep, ep, cp), DENSE)
    rows = ("hi", "ep")
    block = P(rows, "cp", None, None, None)
    dense, vector, expert = P(DENSE, None), P(DENSE), P("cp", rows, None)
    in_specs = (block, block, P(rows, None), block) + (vector,) * 2 + (dense,) * 5 + (expert,) * 3
    out_specs = (block,) * 2 + (vector,) * 2 + (dense,) * 5 + (expert,) * 3
    return jax.shard_map(
        local, mesh=finer, in_specs=in_specs, out_specs=out_specs, check_vma=False
    )
```

```python
import functools

import jax
import jax.numpy as jnp
from jax import lax
from jax.experimental import pallas as pl
from jax.experimental.pallas import tpu as pltpu
from jax.sharding import Mesh, PartitionSpec as P

H = 24
KV = 8
HD = 64
EXPERTS = 16
BLK = 128
CAP = 48
EPS = 1e-05
NEG = -1e30
GROUP = H // KV
SCALE = HD ** (-0.5)
PACK = 2
HIGH = lax.Precision.HIGHEST
F32 = jnp.float32
BF16 = jnp.bfloat16
DENSE = ("hi", "ep", "cp")


def dot(a, b, ca=1, cb=0):
    return lax.dot_general(a, b, (((ca,), (cb,)), ((), ())), preferred_element_type=F32)


def sort_blocks(table, seq, src, dst, which, blocks):
    for b in range(blocks):
        at = table[seq, b]
        dst[pl.ds(b * BLK, BLK), :] = src[at // 2, 0, which, pl.ds((at % 2) * BLK, BLK), :]


def stack_heads(rows, first, scale=None):
    parts = [
        rows[half * BLK : (half + 1) * BLK, (first + i) * HD : (first + i + 1) * HD]
        for half in range(2)
        for i in range(GROUP)
    ]
    out = jnp.concatenate(parts, axis=0)
    return out if scale is None else out * jnp.asarray(scale, out.dtype)


def unstack_heads(low, high):
    rows = []
    for pieces in (low, high):
        heads = [p[i * BLK : (i + 1) * BLK] for p in pieces for i in range(GROUP)]
        rows.append(jnp.concatenate(heads, axis=1))
    return jnp.concatenate(rows, axis=0)


def attend_group(q_all, k_all, v_all, low_bias, high_bias):
    half = k_all.shape[0] // 2
    rows = GROUP * BLK
    lows, highs = [], []
    for j in range(PACK):
        k = k_all[:, j * HD : (j + 1) * HD]
        v = v_all[:, j * HD : (j + 1) * HD]
        q = stack_heads(q_all, j * GROUP, SCALE)
        s_low = dot(q[:rows], k[:half], 1, 1) + jnp.concatenate([low_bias] * GROUP, axis=0)
        peak = jnp.max(s_low, axis=-1, keepdims=True)
        e_low = jnp.exp(s_low - peak)
        total = jnp.sum(e_low, axis=-1, keepdims=True)
        lows.append((dot(e_low.astype(BF16), v[:half]) / total).astype(BF16))
        s_one = dot(q[rows:], k[:half], 1, 1)
        s_two = dot(q[rows:], k[half:], 1, 1) + jnp.concatenate([high_bias] * GROUP, axis=0)
        peak = jnp.maximum(
            jnp.max(s_one, axis=-1, keepdims=True), jnp.max(s_two, axis=-1, keepdims=True)
        )
        e_one = jnp.exp(s_one - peak)
        e_two = jnp.exp(s_two - peak)
        total = jnp.sum(e_one, axis=-1, keepdims=True) + jnp.sum(e_two, axis=-1, keepdims=True)
        mixed = dot(e_one.astype(BF16), v[:half]) + dot(e_two.astype(BF16), v[half:])
        highs.append((mixed / total).astype(BF16))
    return unstack_heads(lows, highs)


def query_bias(at, blocks):
    half = blocks * BLK // 2
    query = lax.broadcasted_iota(jnp.int32, (BLK, half), 0)
    key = lax.broadcasted_iota(jnp.int32, (BLK, half), 1)
    low = jnp.where(key <= query + at * BLK, 0.0, NEG)
    high = jnp.where(key + half <= query + (blocks - 1 - at) * BLK, 0.0, NEG)
    return low, high


def attend_kernel(table, place, q_ref, kv_ref, o_ref, k_s, v_s, low_bias, high_bias):
    seq = pl.program_id(0)
    blocks = 2 * kv_ref.shape[0]

    @pl.when(pl.program_id(1) == 0)
    def _():
        low_bias[...], high_bias[...] = query_bias(place[seq], blocks)

    sort_blocks(table, seq, kv_ref, k_s, 0, blocks)
    sort_blocks(table, seq, kv_ref, v_s, 1, blocks)
    o_ref[...] = attend_group(q_ref[...], k_s[...], v_s[...], low_bias[...], high_bias[...])


def attend_back_kernel(
    sizes, kinds, table, inverse, place, q_ref, kv_ref, g_ref, *refs
):
    n = len(kinds)
    ins, dq_ref, dkv_ref, outs = refs[:n], refs[n], refs[n + 1], refs[n + 2 : 2 * n + 2]
    k_s, v_s, low_bias, high_bias, parts = refs[2 * n + 2 : 2 * n + 7]
    post_sems = refs[2 * n + 7 : 2 * n + 10]
    step_send, step_recv, step_here = refs[2 * n + 10 :]
    cp = sizes[2]
    my_cp = lax.axis_index("cp")
    groups = KV // PACK
    step = pl.program_id(0) * groups + pl.program_id(1)
    last = pl.num_programs(0) * groups - 1
    office = PostOffice(sizes, post_sems)

    @pl.when(step == 0)
    def _():
        office.greet(kinds)
        office.begin(kinds, ins, outs)

    def step_copy(at_seq, at_group, at_step, m):
        columns = pl.ds(pl.multiple_of(at_group * PACK * HD, PACK * HD), PACK * HD)
        to = lax.rem(my_cp + m, cp)
        return mesh_copy(
            parts.at[at_step, to],
            dkv_ref.at[my_cp, at_seq, :, :, columns],
            (step_send, step_recv),
            at_step * (cp - 1) + m - 1,
            {"cp": to},
        )

    def own_copy(at_seq, at_group, at_step):
        columns = pl.ds(pl.multiple_of(at_group * PACK * HD, PACK * HD), PACK * HD)
        return pltpu.make_async_copy(
            parts.at[at_step, my_cp], dkv_ref.at[my_cp, at_seq, :, :, columns], step_here.at[at_step]
        )

    seq = pl.program_id(0)
    blocks = 2 * kv_ref.shape[0]
    half = blocks * BLK // 2
    rows = GROUP * BLK
    at = place[seq]

    @pl.when(pl.program_id(1) == 0)
    def _():
        key = lax.broadcasted_iota(jnp.int32, (half, BLK), 0)
        query = lax.broadcasted_iota(jnp.int32, (half, BLK), 1)
        low_bias[...] = jnp.where(key <= query + at * BLK, 0.0, NEG)
        high_bias[...] = jnp.where(key + half <= query + (blocks - 1 - at) * BLK, 0.0, NEG)

    sort_blocks(table, seq, kv_ref, k_s, 0, blocks)
    sort_blocks(table, seq, kv_ref, v_s, 1, blocks)
    q_all = q_ref[...]
    g_all = g_ref[...]
    lows, highs, dks, dvs = [], [], [], []
    for j in range(PACK):
        k = k_s[:, j * HD : (j + 1) * HD]
        v = v_s[:, j * HD : (j + 1) * HD]
        q = stack_heads(q_all, j * GROUP, SCALE)
        g = stack_heads(g_all, j * GROUP)

        def probs(s_parts):
            peak = jnp.max(s_parts[0], axis=0, keepdims=True)
            for s in s_parts[1:]:
                peak = jnp.maximum(peak, jnp.max(s, axis=0, keepdims=True))
            es = [jnp.exp(s - peak) for s in s_parts]
            total = jnp.sum(es[0], axis=0, keepdims=True)
            for e in es[1:]:
                total = total + jnp.sum(e, axis=0, keepdims=True)
            part = 1.0 / total
            return [e * part for e in es]

        def score_grads(ps, dps):
            inner = jnp.sum(ps[0] * dps[0], axis=0, keepdims=True)
            for p, d in zip(ps[1:], dps[1:]):
                inner = inner + jnp.sum(p * d, axis=0, keepdims=True)
            return [(p * (d - inner)).astype(BF16) for p, d in zip(ps, dps)]

        s_low = dot(k[:half], q[:rows], 1, 1) + jnp.concatenate([low_bias[...]] * GROUP, axis=1)
        (p_low,) = probs([s_low])
        (d_low,) = score_grads([p_low], [dot(v[:half], g[:rows], 1, 1)])
        dv_one = dot(p_low.astype(BF16), g[:rows])
        dk_one = dot(d_low, q[:rows])
        lows.append((dot(d_low, k[:half], 0, 0) * SCALE).astype(BF16))

        s_one = dot(k[:half], q[rows:], 1, 1)
        s_two = dot(k[half:], q[rows:], 1, 1) + jnp.concatenate([high_bias[...]] * GROUP, axis=1)
        p_one, p_two = probs([s_one, s_two])
        d_one, d_two = score_grads(
            [p_one, p_two], [dot(v[:half], g[rows:], 1, 1), dot(v[half:], g[rows:], 1, 1)]
        )
        dv_one = dv_one + dot(p_one.astype(BF16), g[rows:])
        dv_two = dot(p_two.astype(BF16), g[rows:])
        dk_one = dk_one + dot(d_one, q[rows:])
        dk_two = dot(d_two, q[rows:])
        highs.append(
            ((dot(d_one, k[:half], 0, 0) + dot(d_two, k[half:], 0, 0)) * SCALE).astype(BF16)
        )
        dks.append(jnp.concatenate([dk_one, dk_two], axis=0).astype(BF16))
        dvs.append(jnp.concatenate([dv_one, dv_two], axis=0).astype(BF16))
    dq_ref[...] = unstack_heads(lows, highs)
    k_s[...] = jnp.concatenate(dks, axis=1)
    v_s[...] = jnp.concatenate(dvs, axis=1)
    for c in range(cp):
        for h in range(2):
            at_b = pl.ds(inverse[seq, 2 * c + h] * BLK, BLK)
            parts[step, c, 0, h * BLK : (h + 1) * BLK, :] = k_s[at_b, :]
            parts[step, c, 1, h * BLK : (h + 1) * BLK, :] = v_s[at_b, :]
    for m in range(1, cp):
        step_copy(seq, pl.program_id(1), step, m).start()
    own_copy(seq, pl.program_id(1), step).start()

    @pl.when(step == last)
    def _():
        @pl.loop(0, last + 1)
        def _(i):
            at_seq, at_group = i // groups, lax.rem(i, groups)
            for m in range(1, cp):
                step_copy(at_seq, at_group, i, m).wait()
            own_copy(at_seq, at_group, i).wait()

        office.end(kinds, ins, outs)


ATTENTION_COST = pl.CostEstimate(flops=2**34, bytes_accessed=2**24, transcendentals=2**24)


def attention_specs(kv):
    cp, n_seq = kv.shape[:2]
    row = pl.BlockSpec((2 * BLK, PACK * GROUP * HD), lambda s, g, *_: (s, g))
    whole = pl.BlockSpec((cp, 1, 2, 2 * BLK, PACK * HD), lambda s, g, *_: (0, s, 0, 0, g))
    return row, whole, (n_seq, KV // PACK), cp * 2 * BLK


def attend(table, place, q, kv):
    row, whole, grid, keys = attention_specs(kv)
    return pl.pallas_call(
        attend_kernel,
        grid_spec=pltpu.PrefetchScalarGridSpec(
            num_scalar_prefetch=2,
            grid=grid,
            in_specs=[row, whole],
            out_specs=row,
            scratch_shapes=[pltpu.VMEM((keys, PACK * HD), BF16)] * 2
            + [pltpu.VMEM((BLK, keys // 2), F32)] * 2,
        ),
        out_shape=jax.ShapeDtypeStruct(q.shape, BF16),
        compiler_params=pltpu.CompilerParams(
            dimension_semantics=("arbitrary", "arbitrary"), vmem_limit_bytes=56 * 2**20
        ),
        cost_estimate=ATTENTION_COST,
    )(table, place, q, kv)


def attend_back(collective_id, table, inverse, place, q, kv, grad, *jobs):
    row, whole, grid, keys = attention_specs(kv)
    sizes = tuple(lax.axis_size(a) for a in DENSE)
    cp = sizes[2]
    steps = grid[0] * grid[1]
    kinds, arrays, shapes = courier_jobs(sizes, jobs)
    smem = pl.BlockSpec(memory_space=pltpu.SMEM)
    hbm = pl.BlockSpec(memory_space=pl.ANY)
    n = jobs_messages(kinds, *sizes)
    return pl.pallas_call(
        functools.partial(attend_back_kernel, sizes, kinds),
        grid=grid,
        in_specs=[smem, smem, smem, row, whole, row] + [hbm] * len(jobs),
        out_specs=[row, hbm] + [hbm] * len(jobs),
        out_shape=[
            jax.ShapeDtypeStruct(q.shape, BF16),
            jax.ShapeDtypeStruct(kv.shape, BF16),
        ]
        + shapes,
        scratch_shapes=[pltpu.VMEM((keys, PACK * HD), BF16)] * 2
        + [pltpu.VMEM((keys // 2, BLK), F32)] * 2
        + [pltpu.VMEM((steps, cp, 2, 2 * BLK, PACK * HD), BF16)]
        + post_scratch(n, len(jobs))
        + [
            pltpu.SemaphoreType.DMA((steps * (cp - 1),)),
            pltpu.SemaphoreType.DMA((steps * (cp - 1),)),
            pltpu.SemaphoreType.DMA((steps,)),
        ],
        compiler_params=pltpu.CompilerParams(
            dimension_semantics=("arbitrary", "arbitrary"),
            vmem_limit_bytes=56 * 2**20,
            collective_id=collective_id,
            has_side_effects=True,
        ),
        cost_estimate=ATTENTION_COST,
    )(table, inverse, place, q, kv, grad, *arrays)


def tie(x, *others):
    return lax.optimization_barrier((x,) + others)[0]


def mesh_copy(src, dst, sems, at, device):
    send, recv = sems
    return pltpu.make_async_remote_copy(
        src_ref=src, dst_ref=dst, send_sem=send.at[at], recv_sem=recv.at[at],
        device_id=device, device_id_type=pl.DeviceIdType.MESH,
    )


def jobs_messages(kinds, hi, ep, cp):
    f, e = hi * ep, ep * cp
    counts = {
        "gather": f // 2 - 1 + (f // 2) * (cp - 1) + (f // 2) * cp,
        "expert": f - 1, "owners": f - 1, "tokens": e - 1, "peers": cp - 1, "quad": ep - 1,
    }
    return sum(counts[k] for k in kinds)


def post_scratch(n, jobs):
    return [
        pltpu.SemaphoreType.DMA((max(n, 1),)),
        pltpu.SemaphoreType.DMA((max(n, 1),)),
        pltpu.SemaphoreType.DMA((max(jobs, 1),)),
    ]


def plus(a, b, size):
    return lax.rem(a + b, size)


def flip(a, bits):
    out = a
    for bit in range(bits.bit_length()):
        if bits >> bit & 1:
            out = out + (1 << bit) - (1 << (bit + 1)) * lax.rem(a // (1 << bit), 2)
    return out


def partner(me, k, n):
    return lax.rem(me + lax.rem((k + 1) * 5, n), n)


class PostOffice:
    def __init__(self, sizes, sems):
        self.hi, self.ep, self.cp = sizes
        self.fsdp = self.hi * self.ep
        self.send, self.recv, self.here = sems
        self.my_ep, self.my_cp = lax.axis_index("ep"), lax.axis_index("cp")
        self.me = lax.axis_index("hi") * self.ep + self.my_ep
        self.sibling = flip(self.me, 1)

    def at_fsdp(self, f):
        return {"hi": f // self.ep, "ep": lax.rem(f, self.ep)}

    def greet(self, kinds):
        barrier = pltpu.get_barrier_semaphore()
        partners = [self.at_fsdp(plus(self.me, k, self.fsdp)) for k in range(1, self.fsdp)]
        partners += [{"cp": plus(self.my_cp, k, self.cp)} for k in range(1, self.cp)]
        if "tokens" in kinds:
            partners += [
                {"ep": plus(self.my_ep, a, self.ep), "cp": plus(self.my_cp, b, self.cp)}
                for a in range(1, self.ep)
                for b in range(1, self.cp)
            ]
        for p in partners:
            pl.semaphore_signal(barrier, inc=1, device_id=p, device_id_type=pl.DeviceIdType.MESH)
        pl.semaphore_wait(barrier, len(partners))

    def copies(self, kinds, ins, outs, only=None):
        me, my_ep, my_cp, ep, cp, fsdp = (
            self.me, self.my_ep, self.my_cp, self.ep, self.cp, self.fsdp
        )
        away, local, count = [], [], {"away": 0, "here": 0}

        def post(src, dst, device):
            if only is None or job in only:
                away.append(mesh_copy(src, dst, (self.send, self.recv), count["away"], device))
            count["away"] += 1

        def keep(src, dst):
            if only is None or job in only:
                local.append(pltpu.make_async_copy(src, dst, self.here.at[count["here"]]))
            count["here"] += 1

        for job, (kind, x, out) in enumerate(zip(kinds, ins, outs)):
            if kind == "expert":
                rows = x.shape[1]
                at = pl.ds(pl.multiple_of(me * rows, rows), rows)
                for k in range(1, fsdp):
                    to = plus(me, k, fsdp)
                    post(x.at[lax.rem(to, ep)], out.at[at], self.at_fsdp(to))
                keep(x.at[my_ep], out.at[at])
            elif kind == "owners":
                rows = out.shape[1]
                for k in range(1, fsdp):
                    to = plus(me, k, fsdp)
                    src = x.at[pl.ds(pl.multiple_of(to * rows, rows), rows)]
                    post(src, out.at[me], self.at_fsdp(to))
                keep(x.at[pl.ds(pl.multiple_of(me * rows, rows), rows)], out.at[me])
            elif kind == "quad":
                for k in range(1, ep):
                    to = plus(my_ep, k, ep)
                    post(x.at[to], out.at[my_ep], {"ep": to})
                keep(x.at[my_ep], out.at[my_ep])
            elif kind == "peers":
                for m in range(1, cp):
                    post(x, out.at[my_cp], {"cp": plus(my_cp, m, cp)})
                keep(x, out.at[my_cp])
            elif kind == "tokens":
                mine = my_cp * ep + my_ep
                for k in range(ep * cp - 1):
                    to = partner(mine, k, ep * cp)
                    post(x.at[to], out.at[mine], {"ep": lax.rem(to, ep), "cp": to // ep})
                keep(x.at[my_cp * ep + my_ep], out.at[my_cp * ep + my_ep])
        return away, local

    def begin(self, *jobs):
        for group in self.copies(*jobs):
            for c in group:
                c.start()

    def end(self, *jobs):
        for group in self.copies(*jobs):
            for c in group:
                c.wait()

    def gather(self, x, out, first, here):
        me, my_cp, cp, fsdp = self.me, self.my_cp, self.cp, self.fsdp
        sent, across, mirrored = [], [], []

        def post(src, dst, device):
            c = mesh_copy(src, dst, (self.send, self.recv), first + len(sent), device)
            c.start()
            sent.append(c)
            return c

        def row(f, c):
            return out.at[f * cp + c]

        def share(f, src):
            for m in range(1, cp):
                across.append((f, m, post(src, row(f, my_cp), {"cp": plus(my_cp, m, cp)})))
            mirrored.append(post(src, row(f, my_cp), self.at_fsdp(self.sibling)))

        z = post(x, row(me, my_cp), self.at_fsdp(flip(me, 2)))
        own = pltpu.make_async_copy(x, row(me, my_cp), self.here.at[here])
        own.start()
        share(me, x)
        for k in range(1, fsdp // 2):
            yield
            z.wait_recv()
            if k + 1 < fsdp // 2:
                z = post(x, row(me, my_cp), self.at_fsdp(flip(me, 2 * k + 2)))
            f = flip(me, 2 * k)
            share(f, row(f, my_cp))
        yield
        for f, m, c in across:
            c.wait_recv()
            got = row(f, plus(my_cp, cp - m, cp))
            mirrored.append(post(got, got, self.at_fsdp(self.sibling)))
        for c in mirrored:
            c.wait_recv()
        for c in sent:
            c.wait_send()
        own.wait()

    def column_steps(self):
        return self.fsdp // 2


def steps(generator, count):
    for _ in range(count):
        next(generator, None)


def courier_jobs(sizes, jobs):
    hi, ep, cp = sizes
    shapes = []
    for kind, x in jobs:
        if kind == "gather":
            shape = (hi * ep * cp,) + x.shape
        elif kind == "expert":
            shape = (hi * ep * x.shape[1],) + x.shape[2:]
        elif kind == "owners":
            shape = (hi * ep, x.shape[0] // (hi * ep)) + x.shape[1:]
        elif kind == "peers":
            shape = (cp,) + x.shape
        else:
            shape = x.shape
        shapes.append(jax.ShapeDtypeStruct(shape, x.dtype))
    return [k for k, _ in jobs], [x for _, x in jobs], shapes


def courier_kernel(sizes, kinds, *refs):
    n = len(kinds)
    ins, outs = refs[:n], refs[n : 2 * n]
    office = PostOffice(sizes, refs[2 * n :])
    office.greet(kinds)
    first, here, gathers = jobs_messages([k for k in kinds if k != "gather"], *sizes), 0, []
    here = len([k for k in kinds if k != "gather"])
    for kind, x, out in zip(kinds, ins, outs):
        if kind == "gather":
            gathers.append(office.gather(x, out, first, here))
            first, here = first + jobs_messages(["gather"], *sizes), here + 1
            steps(gathers[-1], office.column_steps())
    office.begin(kinds, ins, outs)
    for g in gathers:
        steps(g, 1)
    office.end(kinds, ins, outs)


def courier(collective_id, *jobs):
    sizes = tuple(lax.axis_size(a) for a in DENSE)
    kinds, arrays, shapes = courier_jobs(sizes, jobs)
    hbm = pl.BlockSpec(memory_space=pl.ANY)
    return pl.pallas_call(
        functools.partial(courier_kernel, sizes, kinds),
        out_shape=shapes,
        in_specs=[hbm] * len(jobs),
        out_specs=[hbm] * len(jobs),
        scratch_shapes=post_scratch(jobs_messages(kinds, *sizes), len(jobs)),
        compiler_params=pltpu.CompilerParams(collective_id=collective_id, has_side_effects=True),
    )(*arrays)


def three_parts(x):
    high = x.astype(BF16).astype(F32)
    middle = (x - high).astype(BF16).astype(F32)
    low = x - high - middle
    lane = lax.broadcasted_iota(jnp.int32, (x.shape[0], 128), 1)
    out = jnp.where(lane == 0, high, jnp.where(lane == 1, middle, jnp.where(lane == 2, low, 0.0)))
    return out.astype(BF16)


STAGES = ((0, 3), (), (1, 2), ())


def front_kernel(sizes, kinds, table, place, x_ref, routes_ref, slots_ref, shard_ref, shard2_ref, *refs):
    n = len(kinds)
    ins, refs = refs[:n], refs[n:]
    a_ref, q_ref, o_ref, middle_ref, b_ref, gates_ref = refs[:6]
    kv_ref, w_ref, w2_ref, rows_ref, rows_gate_ref = refs[6:11]
    outs, rest = refs[11 : n + 11], refs[n + 11 :]
    w_all, w2_all, kv_mine, k_s, v_s, low_bias, high_bias, send_s, gate_s = rest[:9]
    office = PostOffice(sizes, rest[9:12])
    kv_send, kv_recv, kv_here, row_send, row_recv = rest[12:17]
    kv_bufs = rest[17:]
    _, ep, cp = sizes
    n_seq, my_cp = len(kv_bufs), office.my_cp
    rows = 2 * BLK
    wide = KV * HD
    office.greet(kinds)
    base = jobs_messages(kinds, *sizes)

    def begin(stage):
        if STAGES[stage]:
            office.begin(kinds, ins, outs, STAGES[stage])

    gather = office.gather(shard_ref, w_all, base, n)
    gather2 = office.gather(shard2_ref, w2_all, base + jobs_messages(["gather"], *sizes), n + 1)
    steps(gather, office.column_steps())
    begin(0)
    x = x_ref[...].astype(F32)
    x = x * lax.rsqrt(jnp.mean(x * x, axis=-1, keepdims=True) + EPS)
    steps(gather, 1)
    begin(1)
    steps(gather2, 1)
    depth = x.shape[1]
    keep_w = pltpu.make_async_copy(w_all, w_ref, kv_here.at[2 * n_seq])
    keep_w.start()

    def column(w, first):
        return w[:, :, pl.ds(first, 128)].reshape(depth, 128)

    gain = column(w_all, H * HD + 2 * wide).astype(F32).T[:1]
    a_ref[...] = (x * gain).astype(BF16)

    def project(first):
        return dot(a_ref[...], w_all[:, :, pl.ds(first, wide)].reshape(depth, wide)).astype(BF16)

    for part in range(2):
        piece = project(H * HD + part * wide)
        for s in range(n_seq):
            kv_mine[s, part] = piece[s * rows : (s + 1) * rows]
    copies = []
    for s in range(n_seq):
        group = [
            mesh_copy(
                kv_mine.at[s],
                kv_bufs[s].at[my_cp],
                (kv_send, kv_recv),
                s * (cp - 1) + m - 1,
                {"cp": plus(my_cp, m, cp)},
            )
            for m in range(1, cp)
        ]
        group.append(pltpu.make_async_copy(kv_mine.at[s], kv_bufs[s].at[my_cp], kv_here.at[s]))
        for c in group:
            c.start()
        copies.append(group)
    steps(gather2, 1)

    @pl.loop(0, H * HD // wide)
    def _(t):
        first = pl.multiple_of(t * wide, wide)
        q_ref[:, pl.ds(first, wide)] = project(first)

    steps(gather2, 1)
    keeps = []
    for s in range(n_seq):
        for c in copies[s]:
            c.wait()
        keep = pltpu.make_async_copy(kv_bufs[s], kv_ref.at[:, s], kv_here.at[n_seq + s])
        keep.start()
        keeps.append(keep)
        for b in range(2 * cp):
            at = table[s, b]
            to = pl.ds(b * BLK, BLK)
            source = pl.ds((at % 2) * BLK, BLK)
            k_s[to, :] = kv_bufs[s][at // 2, 0, source, :]
            v_s[to, :] = kv_bufs[s][at // 2, 1, source, :]
        if s == n_seq - 1:
            begin(2)
        low_bias[...], high_bias[...] = query_bias(place[s], 2 * cp)

        @pl.loop(0, KV // PACK)
        def _(g, s=s):
            head = pl.ds(pl.multiple_of(g * PACK * HD, PACK * HD), PACK * HD)
            group = PACK * GROUP * HD
            heads = pl.ds(pl.multiple_of(g * group, group), group)
            at = pl.ds(s * rows, rows)
            o_ref[at, heads] = attend_group(
                q_ref[at, heads], k_s[:, head], v_s[:, head], low_bias[...], high_bias[...]
            )

        steps(gather2, 1)

    begin(3)
    steps(gather2, office.column_steps())
    keep_w2 = pltpu.make_async_copy(w2_all, w2_ref, kv_here.at[2 * n_seq + 1])
    keep_w2.start()

    @pl.loop(0, depth // wide)
    def _(t):
        cols = pl.ds(pl.multiple_of(t * wide, wide), wide)
        out = dot(o_ref[...], w2_all[:, :, cols].reshape(H * HD, wide))
        middle_ref[:, cols] = x_ref[:, cols].astype(F32) + out

    middle = middle_ref[...]
    last = column(w2_all, depth)
    gain = last.astype(F32).T[EXPERTS : EXPERTS + 1]
    b_ref[...] = (
        middle * lax.rsqrt(jnp.mean(middle * middle, axis=-1, keepdims=True) + EPS) * gain
    ).astype(BF16)
    logits = dot(b_ref[...], last)
    lane = lax.broadcasted_iota(jnp.int32, logits.shape, 1)
    picked = [
        jnp.sum(jnp.where(lane == routes_ref[:, r : r + 1], logits, 0.0), axis=1, keepdims=True)
        for r in range(2)
    ]
    top = jnp.maximum(picked[0], picked[1])
    powers = [jnp.exp(p - top) for p in picked]
    gates = [p / (powers[0] + powers[1]) for p in powers]
    both = jnp.where(lane == 0, gates[0], jnp.where(lane == 1, gates[1], 0.0))
    gates_ref[...] = both
    gate_rows = both.T[:2]
    count = EXPERTS
    cap = send_s.shape[1]
    mine = my_cp * ep + office.my_ep

    def away(k, lane):
        to = partner(mine, k, count)
        src, dst = ((send_s, rows_ref), (gate_s, rows_gate_ref))[lane]
        return mesh_copy(
            src.at[k],
            dst.at[mine],
            (row_send, row_recv),
            2 * k + lane,
            {"cp": to // ep, "ep": lax.rem(to, ep)},
        )

    @pl.loop(0, count)
    def _(k):
        first = partner(mine, k, count) * cap
        ids = lax.broadcasted_iota(jnp.int32, (cap, slots_ref.shape[1]), 0) + first
        at = [slots_ref[r : r + 1, :] == ids for r in range(2)]
        chosen = jnp.where(at[0] | at[1], 1.0, 0.0).astype(BF16)
        send_s[k] = dot(chosen, b_ref[...]).astype(BF16)
        gate = sum(jnp.where(at[r], gate_rows[r : r + 1], 0.0) for r in range(2))
        gate_s[k] = three_parts(jnp.sum(gate, axis=1, keepdims=True))

        @pl.when(k < count - 1)
        def _():
            away(k, 0).start()
            away(k, 1).start()

    own = [
        pltpu.make_async_copy(src.at[count - 1], dst.at[mine], kv_here.at[2 * n_seq + 2 + i])
        for i, (src, dst) in enumerate(((send_s, rows_ref), (gate_s, rows_gate_ref)))
    ]
    for c in own:
        c.start()
    for c in own + keeps + [keep_w, keep_w2]:
        c.wait()
    for k in range(count - 1):
        away(k, 0).wait()
        away(k, 1).wait()
    office.end(kinds, ins, outs)


def front(collective_id, table, place, x, routes, slots, shard, shard2, *jobs):
    sizes = tuple(lax.axis_size(a) for a in DENSE)
    hi, ep, cp = sizes
    n_seq = table.shape[0]
    kinds, arrays, shapes = courier_jobs(sizes, jobs)
    rows, wide = 2 * BLK, KV * HD
    whole, whole2 = ((hi * ep * cp,) + s.shape for s in (shard, shard2))
    hbm = pl.BlockSpec(memory_space=pl.ANY)
    vmem = pl.BlockSpec(memory_space=pltpu.VMEM)
    smem = pl.BlockSpec(memory_space=pltpu.SMEM)
    keys = cp * rows
    tokens, width = x.shape
    sent = (EXPERTS, n_seq * CAP, width)
    sent_gate = (EXPERTS, n_seq * CAP, 128)

    def sems(count):
        return pltpu.SemaphoreType.DMA((count,))

    return pl.pallas_call(
        functools.partial(front_kernel, sizes, kinds),
        in_specs=[smem, smem, vmem, vmem, vmem, hbm, hbm] + [hbm] * len(jobs),
        out_specs=[vmem] * 6 + [hbm] * 5 + [hbm] * len(jobs),
        out_shape=[jax.ShapeDtypeStruct(x.shape, BF16)] * 3
        + [
            jax.ShapeDtypeStruct(x.shape, F32),
            jax.ShapeDtypeStruct(x.shape, BF16),
            jax.ShapeDtypeStruct((tokens, 128), F32),
            jax.ShapeDtypeStruct((cp, n_seq, 2, rows, wide), BF16),
            jax.ShapeDtypeStruct(whole, BF16),
            jax.ShapeDtypeStruct(whole2, BF16),
            jax.ShapeDtypeStruct(sent, BF16),
            jax.ShapeDtypeStruct(sent_gate, BF16),
        ]
        + shapes,
        scratch_shapes=[
            pltpu.VMEM(whole, BF16),
            pltpu.VMEM(whole2, BF16),
            pltpu.VMEM((n_seq, 2, rows, wide), BF16),
            pltpu.VMEM((keys, wide), BF16),
            pltpu.VMEM((keys, wide), BF16),
            pltpu.VMEM((BLK, keys // 2), F32),
            pltpu.VMEM((BLK, keys // 2), F32),
            pltpu.VMEM(sent, BF16),
            pltpu.VMEM(sent_gate, BF16),
        ]
        + post_scratch(jobs_messages(kinds + ["gather"] * 2, *sizes), len(jobs) + 2)
        + [
            sems(n_seq * (cp - 1)),
            sems(n_seq * (cp - 1)),
            sems(2 * n_seq + 4),
            sems(2 * EXPERTS),
            sems(2 * EXPERTS),
        ]
        + [pltpu.VMEM((cp, 2, rows, wide), BF16)] * n_seq,
        compiler_params=pltpu.CompilerParams(
            collective_id=collective_id, has_side_effects=True, vmem_limit_bytes=60 * 2**20
        ),
        cost_estimate=ATTENTION_COST,
    )(table, place, x, routes, slots, shard, shard2, *arrays)


def dense_sum_kernel(sizes, kinds, n_parts, slots_ref, gates_ref, returned_hbm, middle_hbm, *refs):
    n = len(kinds)
    parts, refs = refs[:n_parts], refs[n_parts:]
    widths = [p.shape[2] for p in parts]
    columns = [pl.ds(sum(widths[:j]), w) for j, w in enumerate(widths)]
    ins, out, final_ref, outs, rest = (
        refs[:n], refs[n], refs[n + 1], refs[n + 2 : 2 * n + 2], refs[2 * n + 2 :]
    )
    mine, from_core, summed, from_peers, rows_out, from_column, returned_s, middle_s = rest[:8]
    office = PostOffice(sizes, rest[8:11])
    load_sem, combine_sem = rest[11:13]
    core_sems, peer_sems, column_sems = rest[13:15], rest[15:17], rest[17:19]
    cp, columns_n = sizes[2], office.fsdp // 2
    me, my_cp = office.me, office.my_cp
    office.greet(kinds)
    core = lax.rem(me, 2)
    targets = [flip(me, 2 * k) for k in range(columns_n - 1, -1, -1)]
    loads, cores = [], []
    for i, f in enumerate(targets):
        other = flip(f, 1)
        for j, (part, where) in enumerate(zip(parts, columns)):
            c = mesh_copy(
                part.at[pl.ds(other * cp, cp)],
                from_core.at[i, :, :, where],
                core_sems,
                i * n_parts + j,
                office.at_fsdp(office.sibling),
            )
            c.start()
            cores.append(c)
            c = pltpu.make_async_copy(
                part.at[pl.ds(f * cp, cp)], mine.at[i, :, :, where], load_sem.at[i * n_parts + j]
            )
            c.start()
            loads.append(c)
    fetch = [
        pltpu.make_async_copy(src, dst, combine_sem.at[i])
        for i, (src, dst) in enumerate(((returned_hbm, returned_s), (middle_hbm, middle_s)))
    ]
    for c in fetch:
        c.start()
    office.begin(kinds, ins, outs)
    peers = []
    for i in range(columns_n):
        for c in loads[i * n_parts : (i + 1) * n_parts] + cores[i * n_parts : (i + 1) * n_parts]:
            c.wait()
        summed[i] = (mine[i].astype(F32) + from_core[i].astype(F32)).astype(BF16)
        row = []
        for m in range(1, cp):
            to = plus(my_cp, m, cp)
            c = mesh_copy(
                summed.at[i, to], from_peers.at[i, m - 1], peer_sems, i * (cp - 1) + m - 1, {"cp": to}
            )
            c.start()
            row.append(c)
        peers.append(row)
    for c in fetch:
        c.wait()
    tokens, width = middle_s.shape
    slot = lax.broadcasted_iota(jnp.int32, (tokens, returned_s.shape[0]), 1)
    takes = [(slots_ref[:, r : r + 1] == slot).astype(F32).astype(BF16) for r in range(2)]
    for d in range(0, width, 512):
        cols = slice(d, d + 512)
        final = middle_s[:, cols]
        for r in range(2):
            final = final + gates_ref[:, r : r + 1] * dot(takes[r], returned_s[:, cols])
        final_ref[:, cols] = final.astype(BF16)
    column = []
    total = None
    for i, f in enumerate(targets):
        total = summed[i, my_cp].astype(F32)
        for m, c in enumerate(peers[i], 1):
            c.wait_recv()
            total = total + from_peers[i, m - 1].astype(F32)
        if i < columns_n - 1:
            rows_out[i] = total.astype(BF16)
            c = mesh_copy(
                rows_out.at[i], from_column.at[i], column_sems, i, office.at_fsdp(f)
            )
            c.start()
            column.append(c)
    for i, c in enumerate(column):
        c.wait_recv()
        total = total + from_column[i].astype(F32)
    out[...] = total
    for c in column + [c for row in peers for c in row]:
        c.wait_send()
    office.end(kinds, ins, outs)


def dense_sum(collective_id, parts, slots, gates, returned, middle, *jobs):
    sizes = tuple(lax.axis_size(a) for a in DENSE)
    hi, ep, cp = sizes
    column = hi * ep // 2
    rows = parts[0].shape[0] // (hi * ep * cp)
    width = sum(p.shape[1] for p in parts)
    kinds, arrays, shapes = courier_jobs(sizes, jobs)
    hbm = pl.BlockSpec(memory_space=pl.ANY)
    vmem = pl.BlockSpec(memory_space=pltpu.VMEM)

    def sems(count):
        return [pltpu.SemaphoreType.DMA((count,))] * 2

    return pl.pallas_call(
        functools.partial(dense_sum_kernel, sizes, kinds, len(parts)),
        out_shape=[
            jax.ShapeDtypeStruct((rows, width), F32),
            jax.ShapeDtypeStruct(middle.shape, BF16),
        ]
        + shapes,
        in_specs=[vmem] * 2 + [hbm] * (2 + len(parts) + len(jobs)),
        out_specs=[vmem] * 2 + [hbm] * len(jobs),
        scratch_shapes=[
            pltpu.VMEM((column, cp, rows, width), BF16),
            pltpu.VMEM((column, cp, rows, width), BF16),
            pltpu.VMEM((column, cp, rows, width), BF16),
            pltpu.VMEM((column, cp - 1, rows, width), BF16),
            pltpu.VMEM((column - 1, rows, width), BF16),
            pltpu.VMEM((column - 1, rows, width), BF16),
            pltpu.VMEM(returned.shape, BF16),
            pltpu.VMEM(middle.shape, F32),
        ]
        + post_scratch(jobs_messages(kinds, *sizes), len(jobs))
        + [pltpu.SemaphoreType.DMA((column * len(parts),)), pltpu.SemaphoreType.DMA((2,))]
        + sems(column * len(parts))
        + sems(column * (cp - 1))
        + sems(column - 1),
        compiler_params=pltpu.CompilerParams(
            collective_id=collective_id, has_side_effects=True, vmem_limit_bytes=56 * 2**20
        ),
    )(slots, gates, returned, middle, *(p.reshape(-1, rows, p.shape[1]) for p in parts), *arrays)


def swap(x):
    hi = lax.axis_size("hi")
    xs = x if isinstance(x, list) else [x] * (hi - 1)
    return [
        lax.ppermute(xs[k - 1], "hi", [(i, (i + k) % hi) for i in range(hi)]) for k in range(1, hi)
    ]


def after(k):
    return lax.rem(lax.axis_index("hi") + k, lax.axis_size("hi"))


def half_rows(x):
    rows = x.shape[0] // lax.axis_size("hi")
    parts = [
        lax.dynamic_slice_in_dim(x, after(k) * rows, rows, axis=0)
        for k in range(lax.axis_size("hi"))
    ]
    return parts[0], parts[1:]


def expert_kernel(
    sizes,
    group,
    x_hbm,
    dy_hbm,
    gate_hbm,
    up_hbm,
    down_hbm,
    scale_ref,
    back_ref,
    inner_ref,
    e_ref,
    gate_out,
    up_out,
    down_out,
    x_s,
    dy_s,
    gate_w,
    up_w,
    down_w,
    hidden_s,
    dg_s,
    du_s,
    back_s,
    inner_s,
    e_s,
    load_sem,
    weight_sem,
    send,
    recv,
    out_sem,
):
    _, ep, cp = sizes
    n, cap, width = x_hbm.shape
    depth = hidden_s.shape[1]
    me = lax.axis_index("cp") * ep + lax.axis_index("ep")

    def source(k):
        return partner(me, k, n)

    def device(at):
        return {"cp": at // ep, "ep": lax.rem(at, ep)}

    barrier = pltpu.get_barrier_semaphore()
    for k in range(n - 1):
        pl.semaphore_signal(
            barrier, inc=1, device_id=device(source(k)), device_id_type=pl.DeviceIdType.MESH
        )
    weights = [
        pltpu.make_async_copy(src, dst, weight_sem.at[i])
        for i, (src, dst) in enumerate(
            ((gate_hbm, gate_w), (up_hbm, up_w), (down_hbm, down_w))
        )
    ]
    loads = []
    for c in weights[:2]:
        c.start()
    for k in range(n):
        pair = [
            pltpu.make_async_copy(src.at[source(k)], dst.at[k], load_sem.at[2 * k + i])
            for i, (src, dst) in enumerate(((x_hbm, x_s), (dy_hbm, dy_s)))
        ]
        for c in pair:
            c.start()
        loads.append(pair)
    weights[2].start()
    for pair in loads:
        for c in pair:
            c.wait()
    for c in weights:
        c.wait()
    pl.semaphore_wait(barrier, n - 1)

    def away(k, src, dst, lane):
        return pltpu.make_async_remote_copy(
            src_ref=src.at[k],
            dst_ref=dst.at[me],
            send_sem=send.at[2 * k + lane],
            recv_sem=recv.at[2 * k + lane],
            device_id=device(source(k)),
            device_id_type=pl.DeviceIdType.MESH,
        )

    def here(src, dst, lane):
        return pltpu.make_async_copy(src.at[n - 1], dst.at[me], out_sem.at[lane])

    def keep_e(k):
        return pltpu.make_async_copy(e_s.at[k], e_ref.at[source(k)], out_sem.at[2 + k])

    tile = group * cap
    chunk = min(512, depth)

    @pl.loop(0, n // group)
    def _(t):
        first = pl.multiple_of(t * tile, tile)
        at = pl.ds(first, tile)
        k0 = t * group
        x = x_s[pl.ds(k0, group)].reshape(tile, width)
        dy = dy_s[pl.ds(k0, group)].reshape(tile, width)
        inner = jnp.zeros((tile, 1), F32)
        for f in range(0, depth, chunk):
            cols = slice(f, f + chunk)
            gate_pre = dot(x, gate_w[:, cols])
            up_pre = dot(x, up_w[:, cols])
            sigmoid_gate = jax.nn.sigmoid(gate_pre)
            swish = gate_pre * sigmoid_gate
            hidden = (swish * up_pre).astype(BF16)
            hidden_s[at, cols] = hidden
            hidden_grad = dot(dy, down_w[cols, :], 1, 1)
            inner = inner + jnp.sum(hidden_grad * hidden.astype(F32), axis=1, keepdims=True)
            slope = sigmoid_gate * (1.0 + gate_pre * (1.0 - sigmoid_gate))
            dg_s[at, cols] = (hidden_grad * up_pre * slope).astype(BF16)
            du_s[at, cols] = (hidden_grad * swish).astype(BF16)
        inner_s[pl.ds(k0, group)] = three_parts(inner).reshape(group, cap, 128)
        for d in range(0, width, 512):
            cols = slice(d, d + 512)
            back = dot(dg_s[at, :], gate_w[cols, :], 1, 1) + dot(du_s[at, :], up_w[cols, :], 1, 1)
            back_s[pl.ds(k0, group), :, cols] = back.astype(BF16).reshape(group, cap, 512)
        for i in range(group):
            k = k0 + i

            @pl.when(k < n - 1)
            def _():
                away(k, back_s, back_ref, 0).start()
                away(k, inner_s, inner_ref, 1).start()

        for d in range(0, width, 512):
            cols = slice(d, d + 512)
            e = dot(hidden_s[at, :], down_w[:, cols])
            e_s[pl.ds(k0, group), :, cols] = e.astype(BF16).reshape(group, cap, 512)
        for i in range(group):
            keep_e(k0 + i).start()

    here(back_s, back_ref, 0).start()
    here(inner_s, inner_ref, 1).start()
    for k in range(n):
        lanes = lax.broadcasted_iota(jnp.int32, (cap, 128), 1)
        gate = jnp.sum(
            jnp.where(lanes < 3, scale_ref[source(k)].astype(F32), 0.0), axis=1, keepdims=True
        )
        x_s[k] = (x_s[k].astype(F32) * gate).astype(BF16)
        dy_s[k] = (dy_s[k].astype(F32) * gate).astype(BF16)

    @pl.loop(0, width // 256)
    def _(d):
        cols = pl.ds(pl.multiple_of(d * 256, 256), 256)
        x = x_s[:, :, cols].reshape(n * cap, 256)
        gate_out[cols, :] = dot(x, dg_s[...], 0, 0).astype(BF16)
        up_out[cols, :] = dot(x, du_s[...], 0, 0).astype(BF16)

    @pl.loop(0, depth // 256)
    def _(f):
        cols = pl.ds(pl.multiple_of(f * 256, 256), 256)
        down_out[cols, :] = dot(
            hidden_s[:, cols], dy_s[...].reshape(n * cap, width), 0, 0
        ).astype(BF16)

    here(back_s, back_ref, 0).wait()
    here(inner_s, inner_ref, 1).wait()
    for k in range(n):
        keep_e(k).wait()
    for k in range(n - 1):
        away(k, back_s, back_ref, 0).wait()
        away(k, inner_s, inner_ref, 1).wait()


def expert(collective_id, x, dy, gate, up, down, scale):
    sizes = tuple(lax.axis_size(a) for a in DENSE)
    n, cap, width = x.shape
    depth = gate.shape[1]
    hbm = pl.BlockSpec(memory_space=pl.ANY)
    vmem = pl.BlockSpec(memory_space=pltpu.VMEM)
    rows = pltpu.VMEM(x.shape, BF16)
    tall = pltpu.VMEM((n * cap, depth), BF16)

    def sems(count):
        return pltpu.SemaphoreType.DMA((count,))

    return pl.pallas_call(
        functools.partial(expert_kernel, sizes, 4),
        in_specs=[hbm] * 5 + [vmem],
        out_specs=[hbm] * 3 + [vmem] * 3,
        out_shape=[
            jax.ShapeDtypeStruct(x.shape, BF16),
            jax.ShapeDtypeStruct((n, cap, 128), BF16),
            jax.ShapeDtypeStruct(x.shape, BF16),
            jax.ShapeDtypeStruct(gate.shape, BF16),
            jax.ShapeDtypeStruct(up.shape, BF16),
            jax.ShapeDtypeStruct(down.shape, BF16),
        ],
        scratch_shapes=[
            rows,
            rows,
            pltpu.VMEM(gate.shape, BF16),
            pltpu.VMEM(up.shape, BF16),
            pltpu.VMEM(down.shape, BF16),
            tall,
            tall,
            tall,
            rows,
            pltpu.VMEM((n, cap, 128), BF16),
            rows,
            sems(2 * n),
            sems(3),
            sems(2 * n),
            sems(2 * n),
            sems(2 + n),
        ],
        compiler_params=pltpu.CompilerParams(
            collective_id=collective_id, has_side_effects=True, vmem_limit_bytes=62 * 2**20
        ),
        cost_estimate=ATTENTION_COST,
    )(x, dy, gate, up, down, scale)


def rms_backward(rows, scale, gain, grad_norm):
    weighted = grad_norm * gain
    inner = jnp.mean(weighted * rows, axis=-1, keepdims=True)
    grad_rows = scale * weighted - rows * scale * scale * scale * inner
    return grad_rows, jnp.sum(grad_norm * rows * scale, axis=0)


def with_extra(main, *columns):
    rows = main.shape[0]
    columns = [c.reshape(rows, -1).astype(main.dtype) for c in columns]
    used = sum(c.shape[1] for c in columns)
    return jnp.concatenate([main, *columns, jnp.zeros((rows, -used % 128), main.dtype)], axis=1)


def local(
    layer_input,
    cotangent,
    pairing,
    routes,
    first_gain,
    second_gain,
    query_weight,
    key_weight,
    value_weight,
    out_weight,
    router_weight,
    gate_weight,
    up_weight,
    down_weight,
):
    n_seq = layer_input.shape[0]
    width = layer_input.shape[-1]
    rows = 2 * BLK
    tokens = n_seq * rows
    cp = lax.axis_size("cp")
    here = lax.axis_index("cp")
    blocks = 2 * cp
    n_q, n_kv = H * HD, KV * HD
    n_slots = EXPERTS * n_seq * CAP

    first = with_extra(
        jnp.concatenate([query_weight, key_weight, value_weight], axis=1), first_gain
    )
    second = with_extra(out_weight, router_weight, second_gain)
    n_first = n_q + 2 * n_kv

    chosen = routes.reshape(tokens, 2)
    experts = jnp.arange(EXPERTS, dtype=jnp.int32)
    picks = chosen[:, :, None] == experts[None, None, :]
    named = jnp.any(picks, axis=1).astype(BF16)
    token = jnp.arange(tokens, dtype=jnp.int32)
    earlier = (token[None, :] < token[:, None]) & (token[None, :] // rows == token[:, None] // rows)
    before = dot(earlier.astype(BF16), named)
    rank = jnp.sum(jnp.where(picks, before[:, None, :], 0.0), axis=-1).astype(jnp.int32)
    slots = (chosen * n_seq + (token // rows)[:, None]) * CAP + rank
    slot = jnp.arange(n_slots, dtype=jnp.int32)
    at_slot = [slots[:, r][None, :] == slot[:, None] for r in range(2)]
    place_rows = (at_slot[0] | at_slot[1]).astype(BF16)
    take_rows = [(slots[:, r][:, None] == slot[None, :]).astype(BF16) for r in range(2)]

    def exchange(x):
        x = x.reshape(EXPERTS, n_seq * CAP, -1)
        x = lax.all_to_all(x, ("cp", "ep"), split_axis=0, concat_axis=0, tiled=True)
        return x.reshape(n_slots, -1)

    def exchange_scalar(x):
        x = x.reshape(EXPERTS, 1, n_seq * CAP)
        x = lax.all_to_all(x, ("cp", "ep"), split_axis=0, concat_axis=0, tiled=True)
        return x.reshape(n_slots)

    grad_rows = dot(place_rows, cotangent.reshape(tokens, width)).astype(BF16)
    resid = layer_input.reshape(tokens, width).astype(F32)
    scale_one = lax.rsqrt(jnp.mean(resid * resid, axis=-1, keepdims=True) + EPS)
    ids = jnp.stack([pairing, blocks - 1 - pairing], axis=2).reshape(n_seq, blocks)
    order = jnp.arange(blocks, dtype=jnp.int32)
    table = jnp.sum(jnp.where(ids[:, :, None] == order, order[None, :, None], 0), axis=1)
    place = lax.dynamic_index_in_dim(pairing, here, axis=1, keepdims=False)
    pick_f = picks.astype(F32)
    weights = [("expert", w) for w in (gate_weight, up_weight, down_weight)]
    if first.shape[0] % 16 == 0:
        (
            attn_in,
            queries,
            attn_out,
            middle,
            moe_in,
            gates,
            kv_all,
            first,
            second,
            arrived,
            arrived_gate,
            gate_matrix,
            up_matrix,
            down_matrix,
            grad_rows,
        ) = front(
            0,
            table,
            place,
            layer_input.reshape(tokens, width),
            chosen,
            slots.T,
            first,
            second,
            *weights,
            ("tokens", grad_rows.reshape(EXPERTS, n_seq * CAP, width)),
        )
        gates = gates[:, :2]
        first = first.reshape(width, -1)
        second = second.reshape(n_q, -1)
    else:
        second = lax.all_gather(second, DENSE, axis=0, tiled=True)
        first, gate_matrix, down_matrix = courier(0, ("gather", first), weights[0], weights[2])
        first = first.reshape(width, -1)
        attn_in = (resid * scale_one * first[:, n_first].astype(F32)).astype(BF16)
        qkv = dot(attn_in, first[:, :n_first]).astype(BF16)
        queries = qkv[:, :n_q]
        kv = qkv[:, n_q:].reshape(n_seq, rows, 2, n_kv).transpose(0, 2, 1, 3)
        kv_all, up_matrix = courier(1, ("peers", kv), weights[1])
        grad_rows = exchange(tie(grad_rows, kv_all))
        attn_out = tie(attend(table, place, queries, kv_all), grad_rows)
        middle = resid + dot(attn_out, second[:, :width])
        scale_two = lax.rsqrt(jnp.mean(middle * middle, axis=-1, keepdims=True) + EPS)
        moe_in = (middle * scale_two * second[:, width + EXPERTS].astype(F32)).astype(BF16)
        logits = dot(moe_in, second[:, width : width + EXPERTS])
        picked = jnp.sum(pick_f * logits[:, None, :], axis=-1)
        powers = jnp.exp(picked - jnp.max(picked, axis=-1, keepdims=True))
        gates = powers / jnp.sum(powers, axis=-1, keepdims=True)
        gate_slot = jnp.sum(
            sum(jnp.where(at_slot[r], gates[:, r][None, :], 0.0) for r in range(2)), axis=1
        )
        arrived = exchange(dot(place_rows, moe_in).astype(BF16))
        rest, lanes = exchange_scalar(tie(gate_slot, arrived)), []
        for _ in range(3):
            lanes.append(lax.reduce_precision(rest, 8, 7))
            rest = rest - lanes[-1]
        arrived_gate = jnp.pad(jnp.stack(lanes, axis=1).astype(BF16), ((0, 0), (0, 125)))
    qkv_matrix = first[:, :n_first]
    gain_one = first[:, n_first].astype(F32)
    out_matrix = second[:, :width]
    router_matrix = second[:, width : width + EXPERTS]
    gain_two = second[:, width + EXPERTS].astype(F32)
    scale_two = lax.rsqrt(jnp.mean(middle * middle, axis=-1, keepdims=True) + EPS)

    shape = (EXPERTS, n_seq * CAP, width)
    grad_returned, inner, produced, gate_part, up_part, down_part = expert(
        4,
        arrived.reshape(shape),
        grad_rows.reshape(shape),
        gate_matrix,
        up_matrix,
        down_matrix,
        arrived_gate.reshape(EXPERTS, -1, 128),
    )
    grad_returned = grad_returned.reshape(n_slots, width)
    gate_inner = jnp.sum(inner[:, :, :3].astype(F32), axis=2).reshape(n_slots)
    down_own, down_sent = half_rows(down_part)
    down_sent = swap(down_sent)

    returned = exchange(tie(produced, grad_returned))
    grad_final = cotangent.reshape(tokens, width).astype(F32)
    gate_inner = jnp.stack(
        [jnp.sum(jnp.where(a, gate_inner[:, None], 0.0), axis=0) for a in at_slot], axis=1
    )
    pair_grad = gates * (gate_inner - jnp.sum(gates * gate_inner, axis=-1, keepdims=True))
    logit_grad = jnp.sum(pick_f * pair_grad[:, :, None], axis=1)
    moe_in_grad = jnp.dot(logit_grad, router_matrix.astype(F32).T, precision=HIGH)
    for r in range(2):
        moe_in_grad = moe_in_grad + gates[:, r : r + 1] * dot(take_rows[r], grad_returned)
    router_part = jnp.dot(moe_in.astype(F32).T, logit_grad, precision=HIGH)
    middle_norm_grad, gain_two_grad = rms_backward(middle, scale_two, gain_two, moe_in_grad)
    middle_grad = grad_final + middle_norm_grad
    branch_grad = middle_grad.astype(BF16)
    out_part = dot(attn_out, branch_grad, 0, 0).astype(BF16)
    attn_out_grad = dot(branch_grad, out_matrix, 1, 1).astype(BF16)
    attn_out_grad = tie(attn_out_grad, out_part)
    query_grad, kv_grad, gate_parts = attend_back(
        2, table, ids, place, queries, kv_all, attn_out_grad, ("owners", gate_part)
    )
    kv_grad = tie(kv_grad, returned, *down_sent)
    kv_grad = jnp.sum(kv_grad.astype(F32), axis=0).astype(BF16)
    kv_grad = kv_grad.transpose(0, 2, 1, 3).reshape(tokens, 2 * n_kv)
    qkv_grad = jnp.concatenate([query_grad, kv_grad], axis=1)
    first_part = dot(attn_in, qkv_grad, 0, 0).astype(BF16)
    attn_in_grad = dot(qkv_grad, qkv_matrix, 1, 1)
    resid_norm_grad, gain_one_grad = rms_backward(resid, scale_one, gain_one, attn_in_grad)
    input_grad = middle_grad + resid_norm_grad
    down_sum = tie(down_own, query_grad, returned).astype(F32) + sum(d.astype(F32) for d in down_sent)
    down_sum = down_sum.astype(BF16).reshape(down_weight.shape)

    def own_sum(parts):
        halves = parts.reshape((-1,) + gate_weight.shape)
        return jnp.sum(halves.astype(F32), axis=0)

    small_part = jnp.concatenate(
        [router_part, gain_one_grad[:, None], gain_two_grad[:, None]], axis=1
    ).astype(BF16)
    small_part = jnp.pad(small_part, ((0, 0), (0, -small_part.shape[1] % 128)))
    dense, layer_output, up_parts, down_sum = dense_sum(
        3,
        [first_part, out_part, small_part],
        slots,
        gates,
        returned,
        middle,
        ("owners", up_part),
        ("quad", down_sum),
    )
    at_small = n_first + width
    return (
        layer_output.reshape(layer_input.shape),
        input_grad.reshape(layer_input.shape),
        dense[:, at_small + EXPERTS],
        dense[:, at_small + EXPERTS + 1],
        dense[:, :n_q],
        dense[:, n_q : n_q + n_kv],
        dense[:, n_q + n_kv : n_first],
        dense[:, n_first:at_small],
        dense[:, at_small : at_small + EXPERTS],
        own_sum(gate_parts),
        own_sum(up_parts),
        down_sum.astype(F32),
    )


def solution(mesh):
    fsdp, cp = mesh.shape["fsdp"], mesh.shape["cp"]
    ep = EXPERTS // cp
    finer = Mesh(mesh.devices.reshape(fsdp // ep, ep, cp), DENSE)
    rows = ("hi", "ep")
    block = P(rows, "cp", None, None, None)
    dense, vector, expert = P(DENSE, None), P(DENSE), P("cp", rows, None)
    in_specs = (block, block, P(rows, None), block) + (vector,) * 2 + (dense,) * 5 + (expert,) * 3
    out_specs = (block,) * 2 + (vector,) * 2 + (dense,) * 5 + (expert,) * 3
    return jax.shard_map(
        local, mesh=finer, in_specs=in_specs, out_specs=out_specs, check_vma=False
    )
```

```python
import functools

import jax
import jax.numpy as jnp
from jax import lax
from jax.experimental import pallas as pl
from jax.experimental.pallas import tpu as pltpu
from jax.sharding import Mesh, PartitionSpec as P

H = 24
KV = 8
HD = 64
EXPERTS = 16
BLK = 128
CAP = 48
EPS = 1e-05
NEG = -1e30
GROUP = H // KV
SCALE = HD ** (-0.5)
PACK = 2
HIGH = lax.Precision.HIGHEST
F32 = jnp.float32
BF16 = jnp.bfloat16
DENSE = ("hi", "ep", "cp")


def dot(a, b, ca=1, cb=0):
    return lax.dot_general(a, b, (((ca,), (cb,)), ((), ())), preferred_element_type=F32)


def sort_blocks(table, seq, src, dst, which, blocks):
    for b in range(blocks):
        at = table[seq, b]
        dst[pl.ds(b * BLK, BLK), :] = src[at // 2, 0, which, pl.ds((at % 2) * BLK, BLK), :]


def stack_heads(rows, first, scale=None):
    parts = [
        rows[half * BLK : (half + 1) * BLK, (first + i) * HD : (first + i + 1) * HD]
        for half in range(2)
        for i in range(GROUP)
    ]
    out = jnp.concatenate(parts, axis=0)
    return out if scale is None else out * jnp.asarray(scale, out.dtype)


def unstack_heads(low, high):
    rows = []
    for pieces in (low, high):
        heads = [p[i * BLK : (i + 1) * BLK] for p in pieces for i in range(GROUP)]
        rows.append(jnp.concatenate(heads, axis=1))
    return jnp.concatenate(rows, axis=0)


def attend_group(q_all, k_all, v_all, low_bias, high_bias):
    half = k_all.shape[0] // 2
    rows = GROUP * BLK
    lows, highs = [], []
    for j in range(PACK):
        k = k_all[:, j * HD : (j + 1) * HD]
        v = v_all[:, j * HD : (j + 1) * HD]
        q = stack_heads(q_all, j * GROUP, SCALE)
        s_low = dot(q[:rows], k[:half], 1, 1) + jnp.concatenate([low_bias] * GROUP, axis=0)
        peak = jnp.max(s_low, axis=-1, keepdims=True)
        e_low = jnp.exp(s_low - peak)
        total = jnp.sum(e_low, axis=-1, keepdims=True)
        lows.append((dot(e_low.astype(BF16), v[:half]) / total).astype(BF16))
        s_one = dot(q[rows:], k[:half], 1, 1)
        s_two = dot(q[rows:], k[half:], 1, 1) + jnp.concatenate([high_bias] * GROUP, axis=0)
        peak = jnp.maximum(
            jnp.max(s_one, axis=-1, keepdims=True), jnp.max(s_two, axis=-1, keepdims=True)
        )
        e_one = jnp.exp(s_one - peak)
        e_two = jnp.exp(s_two - peak)
        total = jnp.sum(e_one, axis=-1, keepdims=True) + jnp.sum(e_two, axis=-1, keepdims=True)
        mixed = dot(e_one.astype(BF16), v[:half]) + dot(e_two.astype(BF16), v[half:])
        highs.append((mixed / total).astype(BF16))
    return unstack_heads(lows, highs)


def query_bias(at, blocks):
    half = blocks * BLK // 2
    query = lax.broadcasted_iota(jnp.int32, (BLK, half), 0)
    key = lax.broadcasted_iota(jnp.int32, (BLK, half), 1)
    low = jnp.where(key <= query + at * BLK, 0.0, NEG)
    high = jnp.where(key + half <= query + (blocks - 1 - at) * BLK, 0.0, NEG)
    return low, high


def attend_kernel(table, place, q_ref, kv_ref, o_ref, k_s, v_s, low_bias, high_bias):
    seq = pl.program_id(0)
    blocks = 2 * kv_ref.shape[0]

    @pl.when(pl.program_id(1) == 0)
    def _():
        low_bias[...], high_bias[...] = query_bias(place[seq], blocks)

    sort_blocks(table, seq, kv_ref, k_s, 0, blocks)
    sort_blocks(table, seq, kv_ref, v_s, 1, blocks)
    o_ref[...] = attend_group(q_ref[...], k_s[...], v_s[...], low_bias[...], high_bias[...])


def attend_back_kernel(
    sizes, kinds, table, inverse, place, q_ref, kv_ref, g_ref, *refs
):
    n = len(kinds)
    ins, dq_ref, dkv_ref, outs = refs[:n], refs[n], refs[n + 1], refs[n + 2 : 2 * n + 2]
    k_s, v_s, low_bias, high_bias, parts = refs[2 * n + 2 : 2 * n + 7]
    post_sems = refs[2 * n + 7 : 2 * n + 10]
    step_send, step_recv, step_here = refs[2 * n + 10 :]
    cp = sizes[2]
    my_cp = lax.axis_index("cp")
    groups = KV // PACK
    step = pl.program_id(0) * groups + pl.program_id(1)
    last = pl.num_programs(0) * groups - 1
    office = PostOffice(sizes, post_sems)

    @pl.when(step == 0)
    def _():
        office.greet(kinds)
        office.begin(kinds, ins, outs)

    def step_copy(at_seq, at_group, at_step, m):
        columns = pl.ds(pl.multiple_of(at_group * PACK * HD, PACK * HD), PACK * HD)
        to = lax.rem(my_cp + m, cp)
        return mesh_copy(
            parts.at[at_step, to],
            dkv_ref.at[my_cp, at_seq, :, :, columns],
            (step_send, step_recv),
            at_step * (cp - 1) + m - 1,
            {"cp": to},
        )

    def own_copy(at_seq, at_group, at_step):
        columns = pl.ds(pl.multiple_of(at_group * PACK * HD, PACK * HD), PACK * HD)
        return pltpu.make_async_copy(
            parts.at[at_step, my_cp], dkv_ref.at[my_cp, at_seq, :, :, columns], step_here.at[at_step]
        )

    seq = pl.program_id(0)
    blocks = 2 * kv_ref.shape[0]
    half = blocks * BLK // 2
    rows = GROUP * BLK
    at = place[seq]

    @pl.when(pl.program_id(1) == 0)
    def _():
        key = lax.broadcasted_iota(jnp.int32, (half, BLK), 0)
        query = lax.broadcasted_iota(jnp.int32, (half, BLK), 1)
        low_bias[...] = jnp.where(key <= query + at * BLK, 0.0, NEG)
        high_bias[...] = jnp.where(key + half <= query + (blocks - 1 - at) * BLK, 0.0, NEG)

    sort_blocks(table, seq, kv_ref, k_s, 0, blocks)
    sort_blocks(table, seq, kv_ref, v_s, 1, blocks)
    q_all = q_ref[...]
    g_all = g_ref[...]
    lows, highs, dks, dvs = [], [], [], []
    for j in range(PACK):
        k = k_s[:, j * HD : (j + 1) * HD]
        v = v_s[:, j * HD : (j + 1) * HD]
        q = stack_heads(q_all, j * GROUP, SCALE)
        g = stack_heads(g_all, j * GROUP)

        def probs(s_parts):
            peak = jnp.max(s_parts[0], axis=0, keepdims=True)
            for s in s_parts[1:]:
                peak = jnp.maximum(peak, jnp.max(s, axis=0, keepdims=True))
            es = [jnp.exp(s - peak) for s in s_parts]
            total = jnp.sum(es[0], axis=0, keepdims=True)
            for e in es[1:]:
                total = total + jnp.sum(e, axis=0, keepdims=True)
            part = 1.0 / total
            return [e * part for e in es]

        def score_grads(ps, dps):
            inner = jnp.sum(ps[0] * dps[0], axis=0, keepdims=True)
            for p, d in zip(ps[1:], dps[1:]):
                inner = inner + jnp.sum(p * d, axis=0, keepdims=True)
            return [(p * (d - inner)).astype(BF16) for p, d in zip(ps, dps)]

        s_low = dot(k[:half], q[:rows], 1, 1) + jnp.concatenate([low_bias[...]] * GROUP, axis=1)
        (p_low,) = probs([s_low])
        (d_low,) = score_grads([p_low], [dot(v[:half], g[:rows], 1, 1)])
        dv_one = dot(p_low.astype(BF16), g[:rows])
        dk_one = dot(d_low, q[:rows])
        lows.append((dot(d_low, k[:half], 0, 0) * SCALE).astype(BF16))

        s_one = dot(k[:half], q[rows:], 1, 1)
        s_two = dot(k[half:], q[rows:], 1, 1) + jnp.concatenate([high_bias[...]] * GROUP, axis=1)
        p_one, p_two = probs([s_one, s_two])
        d_one, d_two = score_grads(
            [p_one, p_two], [dot(v[:half], g[rows:], 1, 1), dot(v[half:], g[rows:], 1, 1)]
        )
        dv_one = dv_one + dot(p_one.astype(BF16), g[rows:])
        dv_two = dot(p_two.astype(BF16), g[rows:])
        dk_one = dk_one + dot(d_one, q[rows:])
        dk_two = dot(d_two, q[rows:])
        highs.append(
            ((dot(d_one, k[:half], 0, 0) + dot(d_two, k[half:], 0, 0)) * SCALE).astype(BF16)
        )
        dks.append(jnp.concatenate([dk_one, dk_two], axis=0).astype(BF16))
        dvs.append(jnp.concatenate([dv_one, dv_two], axis=0).astype(BF16))
    dq_ref[...] = unstack_heads(lows, highs)
    k_s[...] = jnp.concatenate(dks, axis=1)
    v_s[...] = jnp.concatenate(dvs, axis=1)
    for c in range(cp):
        for h in range(2):
            at_b = pl.ds(inverse[seq, 2 * c + h] * BLK, BLK)
            parts[step, c, 0, h * BLK : (h + 1) * BLK, :] = k_s[at_b, :]
            parts[step, c, 1, h * BLK : (h + 1) * BLK, :] = v_s[at_b, :]
    for m in range(1, cp):
        step_copy(seq, pl.program_id(1), step, m).start()
    own_copy(seq, pl.program_id(1), step).start()

    @pl.when(step == last)
    def _():
        @pl.loop(0, last + 1)
        def _(i):
            at_seq, at_group = i // groups, lax.rem(i, groups)
            for m in range(1, cp):
                step_copy(at_seq, at_group, i, m).wait()
            own_copy(at_seq, at_group, i).wait()

        office.end(kinds, ins, outs)


ATTENTION_COST = pl.CostEstimate(flops=2**34, bytes_accessed=2**24, transcendentals=2**24)


def attention_specs(kv):
    cp, n_seq = kv.shape[:2]
    row = pl.BlockSpec((2 * BLK, PACK * GROUP * HD), lambda s, g, *_: (s, g))
    whole = pl.BlockSpec((cp, 1, 2, 2 * BLK, PACK * HD), lambda s, g, *_: (0, s, 0, 0, g))
    return row, whole, (n_seq, KV // PACK), cp * 2 * BLK


def attend(table, place, q, kv):
    row, whole, grid, keys = attention_specs(kv)
    return pl.pallas_call(
        attend_kernel,
        grid_spec=pltpu.PrefetchScalarGridSpec(
            num_scalar_prefetch=2,
            grid=grid,
            in_specs=[row, whole],
            out_specs=row,
            scratch_shapes=[pltpu.VMEM((keys, PACK * HD), BF16)] * 2
            + [pltpu.VMEM((BLK, keys // 2), F32)] * 2,
        ),
        out_shape=jax.ShapeDtypeStruct(q.shape, BF16),
        compiler_params=pltpu.CompilerParams(
            dimension_semantics=("arbitrary", "arbitrary"), vmem_limit_bytes=56 * 2**20
        ),
        cost_estimate=ATTENTION_COST,
    )(table, place, q, kv)


def attend_back(collective_id, table, inverse, place, q, kv, grad, *jobs):
    row, whole, grid, keys = attention_specs(kv)
    sizes = tuple(lax.axis_size(a) for a in DENSE)
    cp = sizes[2]
    steps = grid[0] * grid[1]
    kinds, arrays, shapes = courier_jobs(sizes, jobs)
    smem = pl.BlockSpec(memory_space=pltpu.SMEM)
    hbm = pl.BlockSpec(memory_space=pl.ANY)
    n = jobs_messages(kinds, *sizes)
    return pl.pallas_call(
        functools.partial(attend_back_kernel, sizes, kinds),
        grid=grid,
        in_specs=[smem, smem, smem, row, whole, row] + [hbm] * len(jobs),
        out_specs=[row, hbm] + [hbm] * len(jobs),
        out_shape=[
            jax.ShapeDtypeStruct(q.shape, BF16),
            jax.ShapeDtypeStruct(kv.shape, BF16),
        ]
        + shapes,
        scratch_shapes=[pltpu.VMEM((keys, PACK * HD), BF16)] * 2
        + [pltpu.VMEM((keys // 2, BLK), F32)] * 2
        + [pltpu.VMEM((steps, cp, 2, 2 * BLK, PACK * HD), BF16)]
        + post_scratch(n, len(jobs))
        + [
            pltpu.SemaphoreType.DMA((steps * (cp - 1),)),
            pltpu.SemaphoreType.DMA((steps * (cp - 1),)),
            pltpu.SemaphoreType.DMA((steps,)),
        ],
        compiler_params=pltpu.CompilerParams(
            dimension_semantics=("arbitrary", "arbitrary"),
            vmem_limit_bytes=56 * 2**20,
            collective_id=collective_id,
            has_side_effects=True,
        ),
        cost_estimate=ATTENTION_COST,
    )(table, inverse, place, q, kv, grad, *arrays)


def tie(x, *others):
    return lax.optimization_barrier((x,) + others)[0]


def mesh_copy(src, dst, sems, at, device):
    send, recv = sems
    return pltpu.make_async_remote_copy(
        src_ref=src, dst_ref=dst, send_sem=send.at[at], recv_sem=recv.at[at],
        device_id=device, device_id_type=pl.DeviceIdType.MESH,
    )


def jobs_messages(kinds, hi, ep, cp):
    f, e = hi * ep, ep * cp
    counts = {
        "gather": f // 2 - 1 + (f // 2) * (cp - 1) + (f // 2) * cp,
        "expert": f - 1, "owners": f - 1, "tokens": e - 1, "peers": cp - 1, "quad": ep - 1,
    }
    return sum(counts[k] for k in kinds)


def post_scratch(n, jobs):
    return [
        pltpu.SemaphoreType.DMA((max(n, 1),)),
        pltpu.SemaphoreType.DMA((max(n, 1),)),
        pltpu.SemaphoreType.DMA((max(jobs, 1),)),
    ]


def plus(a, b, size):
    return lax.rem(a + b, size)


def flip(a, bits):
    out = a
    for bit in range(bits.bit_length()):
        if bits >> bit & 1:
            out = out + (1 << bit) - (1 << (bit + 1)) * lax.rem(a // (1 << bit), 2)
    return out


def partner(me, k, n):
    return lax.rem(me + lax.rem((k + 1) * 5, n), n)


class PostOffice:
    def __init__(self, sizes, sems):
        self.hi, self.ep, self.cp = sizes
        self.fsdp = self.hi * self.ep
        self.send, self.recv, self.here = sems
        self.my_ep, self.my_cp = lax.axis_index("ep"), lax.axis_index("cp")
        self.me = lax.axis_index("hi") * self.ep + self.my_ep
        self.sibling = flip(self.me, 1)

    def at_fsdp(self, f):
        return {"hi": f // self.ep, "ep": lax.rem(f, self.ep)}

    def greet(self, kinds):
        barrier = pltpu.get_barrier_semaphore()
        partners = [self.at_fsdp(plus(self.me, k, self.fsdp)) for k in range(1, self.fsdp)]
        partners += [{"cp": plus(self.my_cp, k, self.cp)} for k in range(1, self.cp)]
        if "tokens" in kinds:
            partners += [
                {"ep": plus(self.my_ep, a, self.ep), "cp": plus(self.my_cp, b, self.cp)}
                for a in range(1, self.ep)
                for b in range(1, self.cp)
            ]
        for p in partners:
            pl.semaphore_signal(barrier, inc=1, device_id=p, device_id_type=pl.DeviceIdType.MESH)
        pl.semaphore_wait(barrier, len(partners))

    def copies(self, kinds, ins, outs, only=None):
        me, my_ep, my_cp, ep, cp, fsdp = (
            self.me, self.my_ep, self.my_cp, self.ep, self.cp, self.fsdp
        )
        away, local, count = [], [], {"away": 0, "here": 0}

        def post(src, dst, device):
            if only is None or job in only:
                away.append(mesh_copy(src, dst, (self.send, self.recv), count["away"], device))
            count["away"] += 1

        def keep(src, dst):
            if only is None or job in only:
                local.append(pltpu.make_async_copy(src, dst, self.here.at[count["here"]]))
            count["here"] += 1

        for job, (kind, x, out) in enumerate(zip(kinds, ins, outs)):
            if kind == "expert":
                rows = x.shape[1]
                at = pl.ds(pl.multiple_of(me * rows, rows), rows)
                for k in range(1, fsdp):
                    to = plus(me, 5 * k % fsdp, fsdp)
                    post(x.at[lax.rem(to, ep)], out.at[at], self.at_fsdp(to))
                keep(x.at[my_ep], out.at[at])
            elif kind == "owners":
                rows = out.shape[1]
                for k in range(1, fsdp):
                    to = plus(me, 5 * k % fsdp, fsdp)
                    src = x.at[pl.ds(pl.multiple_of(to * rows, rows), rows)]
                    post(src, out.at[me], self.at_fsdp(to))
                keep(x.at[pl.ds(pl.multiple_of(me * rows, rows), rows)], out.at[me])
            elif kind == "quad":
                for k in range(1, ep):
                    to = plus(my_ep, k, ep)
                    post(x.at[to], out.at[my_ep], {"ep": to})
                keep(x.at[my_ep], out.at[my_ep])
            elif kind == "peers":
                for m in range(1, cp):
                    post(x, out.at[my_cp], {"cp": plus(my_cp, m, cp)})
                keep(x, out.at[my_cp])
            elif kind == "tokens":
                mine = my_cp * ep + my_ep
                for k in range(ep * cp - 1):
                    to = partner(mine, k, ep * cp)
                    post(x.at[to], out.at[mine], {"ep": lax.rem(to, ep), "cp": to // ep})
                keep(x.at[my_cp * ep + my_ep], out.at[my_cp * ep + my_ep])
        return away, local

    def begin(self, *jobs):
        for group in self.copies(*jobs):
            for c in group:
                c.start()

    def end(self, *jobs):
        for group in self.copies(*jobs):
            for c in group:
                c.wait()

    def gather(self, x, out, first, here):
        me, my_cp, cp, fsdp = self.me, self.my_cp, self.cp, self.fsdp
        sent, across, mirrored = [], [], []

        def post(src, dst, device):
            c = mesh_copy(src, dst, (self.send, self.recv), first + len(sent), device)
            c.start()
            sent.append(c)
            return c

        def row(f, c):
            return out.at[f * cp + c]

        def share(f, src):
            for m in range(1, cp):
                across.append((f, m, post(src, row(f, my_cp), {"cp": plus(my_cp, m, cp)})))
            mirrored.append(post(src, row(f, my_cp), self.at_fsdp(self.sibling)))

        z = post(x, row(me, my_cp), self.at_fsdp(flip(me, 2)))
        own = pltpu.make_async_copy(x, row(me, my_cp), self.here.at[here])
        own.start()
        share(me, x)
        for k in range(1, fsdp // 2):
            yield
            z.wait_recv()
            if k + 1 < fsdp // 2:
                z = post(x, row(me, my_cp), self.at_fsdp(flip(me, 2 * k + 2)))
            f = flip(me, 2 * k)
            share(f, row(f, my_cp))
        yield
        for f, m, c in across:
            c.wait_recv()
            got = row(f, plus(my_cp, cp - m, cp))
            mirrored.append(post(got, got, self.at_fsdp(self.sibling)))
        for c in mirrored:
            c.wait_recv()
        for c in sent:
            c.wait_send()
        own.wait()

    def column_steps(self):
        return self.fsdp // 2


def steps(generator, count):
    for _ in range(count):
        next(generator, None)


def courier_jobs(sizes, jobs):
    hi, ep, cp = sizes
    shapes = []
    for kind, x in jobs:
        if kind == "gather":
            shape = (hi * ep * cp,) + x.shape
        elif kind == "expert":
            shape = (hi * ep * x.shape[1],) + x.shape[2:]
        elif kind == "owners":
            shape = (hi * ep, x.shape[0] // (hi * ep)) + x.shape[1:]
        elif kind == "peers":
            shape = (cp,) + x.shape
        else:
            shape = x.shape
        shapes.append(jax.ShapeDtypeStruct(shape, x.dtype))
    return [k for k, _ in jobs], [x for _, x in jobs], shapes


def courier_kernel(sizes, kinds, *refs):
    n = len(kinds)
    ins, outs = refs[:n], refs[n : 2 * n]
    office = PostOffice(sizes, refs[2 * n :])
    office.greet(kinds)
    first, here, gathers = jobs_messages([k for k in kinds if k != "gather"], *sizes), 0, []
    here = len([k for k in kinds if k != "gather"])
    for kind, x, out in zip(kinds, ins, outs):
        if kind == "gather":
            gathers.append(office.gather(x, out, first, here))
            first, here = first + jobs_messages(["gather"], *sizes), here + 1
            steps(gathers[-1], office.column_steps())
    office.begin(kinds, ins, outs)
    for g in gathers:
        steps(g, 1)
    office.end(kinds, ins, outs)


def courier(collective_id, *jobs):
    sizes = tuple(lax.axis_size(a) for a in DENSE)
    kinds, arrays, shapes = courier_jobs(sizes, jobs)
    hbm = pl.BlockSpec(memory_space=pl.ANY)
    return pl.pallas_call(
        functools.partial(courier_kernel, sizes, kinds),
        out_shape=shapes,
        in_specs=[hbm] * len(jobs),
        out_specs=[hbm] * len(jobs),
        scratch_shapes=post_scratch(jobs_messages(kinds, *sizes), len(jobs)),
        compiler_params=pltpu.CompilerParams(collective_id=collective_id, has_side_effects=True),
    )(*arrays)


def three_parts(x):
    high = x.astype(BF16).astype(F32)
    middle = (x - high).astype(BF16).astype(F32)
    low = x - high - middle
    lane = lax.broadcasted_iota(jnp.int32, (x.shape[0], 128), 1)
    out = jnp.where(lane == 0, high, jnp.where(lane == 1, middle, jnp.where(lane == 2, low, 0.0)))
    return out.astype(BF16)


STAGES = ((0, 3), (), (1, 2), ())


def front_kernel(sizes, kinds, table, place, x_ref, routes_ref, slots_ref, shard_ref, shard2_ref, *refs):
    n = len(kinds)
    ins, refs = refs[:n], refs[n:]
    a_ref, q_ref, o_ref, middle_ref, b_ref, gates_ref = refs[:6]
    kv_ref, w_ref, w2_ref, rows_ref, rows_gate_ref = refs[6:11]
    outs, rest = refs[11 : n + 11], refs[n + 11 :]
    w_all, w2_all, kv_mine, k_s, v_s, low_bias, high_bias, send_s, gate_s = rest[:9]
    office = PostOffice(sizes, rest[9:12])
    kv_send, kv_recv, kv_here, row_send, row_recv = rest[12:17]
    kv_bufs = rest[17:]
    _, ep, cp = sizes
    n_seq, my_cp = len(kv_bufs), office.my_cp
    rows = 2 * BLK
    wide = KV * HD
    office.greet(kinds)
    base = jobs_messages(kinds, *sizes)

    def begin(stage):
        if STAGES[stage]:
            office.begin(kinds, ins, outs, STAGES[stage])

    gather = office.gather(shard_ref, w_all, base, n)
    gather2 = office.gather(shard2_ref, w2_all, base + jobs_messages(["gather"], *sizes), n + 1)
    steps(gather, office.column_steps())
    begin(0)
    x = x_ref[...].astype(F32)
    x = x * lax.rsqrt(jnp.mean(x * x, axis=-1, keepdims=True) + EPS)
    steps(gather, 1)
    begin(1)
    steps(gather2, 1)
    depth = x.shape[1]
    keep_w = pltpu.make_async_copy(w_all, w_ref, kv_here.at[2 * n_seq])
    keep_w.start()

    def column(w, first):
        return w[:, :, pl.ds(first, 128)].reshape(depth, 128)

    gain = column(w_all, H * HD + 2 * wide).astype(F32).T[:1]
    a_ref[...] = (x * gain).astype(BF16)

    def project(first):
        return dot(a_ref[...], w_all[:, :, pl.ds(first, wide)].reshape(depth, wide)).astype(BF16)

    for part in range(2):
        piece = project(H * HD + part * wide)
        for s in range(n_seq):
            kv_mine[s, part] = piece[s * rows : (s + 1) * rows]
    copies = []
    for s in range(n_seq):
        group = [
            mesh_copy(
                kv_mine.at[s],
                kv_bufs[s].at[my_cp],
                (kv_send, kv_recv),
                s * (cp - 1) + m - 1,
                {"cp": plus(my_cp, m, cp)},
            )
            for m in range(1, cp)
        ]
        group.append(pltpu.make_async_copy(kv_mine.at[s], kv_bufs[s].at[my_cp], kv_here.at[s]))
        for c in group:
            c.start()
        copies.append(group)
    steps(gather2, 1)

    @pl.loop(0, H * HD // wide)
    def _(t):
        first = pl.multiple_of(t * wide, wide)
        q_ref[:, pl.ds(first, wide)] = project(first)

    steps(gather2, 1)
    keeps = []
    for s in range(n_seq):
        for c in copies[s]:
            c.wait()
        keep = pltpu.make_async_copy(kv_bufs[s], kv_ref.at[:, s], kv_here.at[n_seq + s])
        keep.start()
        keeps.append(keep)
        for b in range(2 * cp):
            at = table[s, b]
            to = pl.ds(b * BLK, BLK)
            source = pl.ds((at % 2) * BLK, BLK)
            k_s[to, :] = kv_bufs[s][at // 2, 0, source, :]
            v_s[to, :] = kv_bufs[s][at // 2, 1, source, :]
        if s == n_seq - 1:
            begin(2)
        low_bias[...], high_bias[...] = query_bias(place[s], 2 * cp)

        @pl.loop(0, KV // PACK)
        def _(g, s=s):
            head = pl.ds(pl.multiple_of(g * PACK * HD, PACK * HD), PACK * HD)
            group = PACK * GROUP * HD
            heads = pl.ds(pl.multiple_of(g * group, group), group)
            at = pl.ds(s * rows, rows)
            o_ref[at, heads] = attend_group(
                q_ref[at, heads], k_s[:, head], v_s[:, head], low_bias[...], high_bias[...]
            )

        steps(gather2, 1)

    begin(3)
    steps(gather2, office.column_steps())
    keep_w2 = pltpu.make_async_copy(w2_all, w2_ref, kv_here.at[2 * n_seq + 1])
    keep_w2.start()

    @pl.loop(0, depth // wide)
    def _(t):
        cols = pl.ds(pl.multiple_of(t * wide, wide), wide)
        out = dot(o_ref[...], w2_all[:, :, cols].reshape(H * HD, wide))
        middle_ref[:, cols] = x_ref[:, cols].astype(F32) + out

    middle = middle_ref[...]
    last = column(w2_all, depth)
    gain = last.astype(F32).T[EXPERTS : EXPERTS + 1]
    b_ref[...] = (
        middle * lax.rsqrt(jnp.mean(middle * middle, axis=-1, keepdims=True) + EPS) * gain
    ).astype(BF16)
    logits = dot(b_ref[...], last)
    lane = lax.broadcasted_iota(jnp.int32, logits.shape, 1)
    picked = [
        jnp.sum(jnp.where(lane == routes_ref[:, r : r + 1], logits, 0.0), axis=1, keepdims=True)
        for r in range(2)
    ]
    top = jnp.maximum(picked[0], picked[1])
    powers = [jnp.exp(p - top) for p in picked]
    gates = [p / (powers[0] + powers[1]) for p in powers]
    both = jnp.where(lane == 0, gates[0], jnp.where(lane == 1, gates[1], 0.0))
    gates_ref[...] = both
    gate_rows = both.T[:2]
    count = EXPERTS
    cap = send_s.shape[1]
    mine = my_cp * ep + office.my_ep

    def away(k, lane):
        to = partner(mine, k, count)
        src, dst = ((send_s, rows_ref), (gate_s, rows_gate_ref))[lane]
        return mesh_copy(
            src.at[k],
            dst.at[mine],
            (row_send, row_recv),
            2 * k + lane,
            {"cp": to // ep, "ep": lax.rem(to, ep)},
        )

    @pl.loop(0, count)
    def _(k):
        first = partner(mine, k, count) * cap
        ids = lax.broadcasted_iota(jnp.int32, (cap, slots_ref.shape[1]), 0) + first
        at = [slots_ref[r : r + 1, :] == ids for r in range(2)]
        chosen = jnp.where(at[0] | at[1], 1.0, 0.0).astype(BF16)
        send_s[k] = dot(chosen, b_ref[...]).astype(BF16)
        gate = sum(jnp.where(at[r], gate_rows[r : r + 1], 0.0) for r in range(2))
        gate_s[k] = three_parts(jnp.sum(gate, axis=1, keepdims=True))

        @pl.when(k < count - 1)
        def _():
            away(k, 0).start()
            away(k, 1).start()

    own = [
        pltpu.make_async_copy(src.at[count - 1], dst.at[mine], kv_here.at[2 * n_seq + 2 + i])
        for i, (src, dst) in enumerate(((send_s, rows_ref), (gate_s, rows_gate_ref)))
    ]
    for c in own:
        c.start()
    for c in own + keeps + [keep_w, keep_w2]:
        c.wait()
    for k in range(count - 1):
        away(k, 0).wait()
        away(k, 1).wait()
    office.end(kinds, ins, outs)


def front(collective_id, table, place, x, routes, slots, shard, shard2, *jobs):
    sizes = tuple(lax.axis_size(a) for a in DENSE)
    hi, ep, cp = sizes
    n_seq = table.shape[0]
    kinds, arrays, shapes = courier_jobs(sizes, jobs)
    rows, wide = 2 * BLK, KV * HD
    whole, whole2 = ((hi * ep * cp,) + s.shape for s in (shard, shard2))
    hbm = pl.BlockSpec(memory_space=pl.ANY)
    vmem = pl.BlockSpec(memory_space=pltpu.VMEM)
    smem = pl.BlockSpec(memory_space=pltpu.SMEM)
    keys = cp * rows
    tokens, width = x.shape
    sent = (EXPERTS, n_seq * CAP, width)
    sent_gate = (EXPERTS, n_seq * CAP, 128)

    def sems(count):
        return pltpu.SemaphoreType.DMA((count,))

    return pl.pallas_call(
        functools.partial(front_kernel, sizes, kinds),
        in_specs=[smem, smem, vmem, vmem, vmem, hbm, hbm] + [hbm] * len(jobs),
        out_specs=[vmem] * 6 + [hbm] * 5 + [hbm] * len(jobs),
        out_shape=[jax.ShapeDtypeStruct(x.shape, BF16)] * 3
        + [
            jax.ShapeDtypeStruct(x.shape, F32),
            jax.ShapeDtypeStruct(x.shape, BF16),
            jax.ShapeDtypeStruct((tokens, 128), F32),
            jax.ShapeDtypeStruct((cp, n_seq, 2, rows, wide), BF16),
            jax.ShapeDtypeStruct(whole, BF16),
            jax.ShapeDtypeStruct(whole2, BF16),
            jax.ShapeDtypeStruct(sent, BF16),
            jax.ShapeDtypeStruct(sent_gate, BF16),
        ]
        + shapes,
        scratch_shapes=[
            pltpu.VMEM(whole, BF16),
            pltpu.VMEM(whole2, BF16),
            pltpu.VMEM((n_seq, 2, rows, wide), BF16),
            pltpu.VMEM((keys, wide), BF16),
            pltpu.VMEM((keys, wide), BF16),
            pltpu.VMEM((BLK, keys // 2), F32),
            pltpu.VMEM((BLK, keys // 2), F32),
            pltpu.VMEM(sent, BF16),
            pltpu.VMEM(sent_gate, BF16),
        ]
        + post_scratch(jobs_messages(kinds + ["gather"] * 2, *sizes), len(jobs) + 2)
        + [
            sems(n_seq * (cp - 1)),
            sems(n_seq * (cp - 1)),
            sems(2 * n_seq + 4),
            sems(2 * EXPERTS),
            sems(2 * EXPERTS),
        ]
        + [pltpu.VMEM((cp, 2, rows, wide), BF16)] * n_seq,
        compiler_params=pltpu.CompilerParams(
            collective_id=collective_id, has_side_effects=True, vmem_limit_bytes=60 * 2**20
        ),
        cost_estimate=ATTENTION_COST,
    )(table, place, x, routes, slots, shard, shard2, *arrays)


def dense_sum_kernel(sizes, kinds, n_parts, slots_ref, gates_ref, returned_hbm, middle_hbm, *refs):
    n = len(kinds)
    parts, refs = refs[:n_parts], refs[n_parts:]
    widths = [p.shape[2] for p in parts]
    columns = [pl.ds(sum(widths[:j]), w) for j, w in enumerate(widths)]
    ins, out, final_ref, outs, rest = (
        refs[:n], refs[n], refs[n + 1], refs[n + 2 : 2 * n + 2], refs[2 * n + 2 :]
    )
    mine, from_core, summed, from_peers, rows_out, from_column, returned_s, middle_s = rest[:8]
    office = PostOffice(sizes, rest[8:11])
    load_sem, combine_sem = rest[11:13]
    core_sems, peer_sems, column_sems = rest[13:15], rest[15:17], rest[17:19]
    cp, columns_n = sizes[2], office.fsdp // 2
    me, my_cp = office.me, office.my_cp
    office.greet(kinds)
    core = lax.rem(me, 2)
    targets = [flip(me, 2 * k) for k in range(columns_n - 1, -1, -1)]
    loads, cores = [], []
    for i, f in enumerate(targets):
        other = flip(f, 1)
        for j, (part, where) in enumerate(zip(parts, columns)):
            c = mesh_copy(
                part.at[pl.ds(other * cp, cp)],
                from_core.at[i, :, :, where],
                core_sems,
                i * n_parts + j,
                office.at_fsdp(office.sibling),
            )
            c.start()
            cores.append(c)
            c = pltpu.make_async_copy(
                part.at[pl.ds(f * cp, cp)], mine.at[i, :, :, where], load_sem.at[i * n_parts + j]
            )
            c.start()
            loads.append(c)
    fetch = [
        pltpu.make_async_copy(src, dst, combine_sem.at[i])
        for i, (src, dst) in enumerate(((returned_hbm, returned_s), (middle_hbm, middle_s)))
    ]
    for c in fetch:
        c.start()
    office.begin(kinds, ins, outs)
    peers = []
    for i in range(columns_n):
        for c in loads[i * n_parts : (i + 1) * n_parts] + cores[i * n_parts : (i + 1) * n_parts]:
            c.wait()
        summed[i] = (mine[i].astype(F32) + from_core[i].astype(F32)).astype(BF16)
        row = []
        for m in range(1, cp):
            to = plus(my_cp, m, cp)
            c = mesh_copy(
                summed.at[i, to], from_peers.at[i, m - 1], peer_sems, i * (cp - 1) + m - 1, {"cp": to}
            )
            c.start()
            row.append(c)
        peers.append(row)
    for c in fetch:
        c.wait()
    tokens, width = middle_s.shape
    slot = lax.broadcasted_iota(jnp.int32, (tokens, returned_s.shape[0]), 1)
    takes = [(slots_ref[:, r : r + 1] == slot).astype(F32).astype(BF16) for r in range(2)]
    for d in range(0, width, 512):
        cols = slice(d, d + 512)
        final = middle_s[:, cols]
        for r in range(2):
            final = final + gates_ref[:, r : r + 1] * dot(takes[r], returned_s[:, cols])
        final_ref[:, cols] = final.astype(BF16)
    column = []
    total = None
    for i, f in enumerate(targets):
        total = summed[i, my_cp].astype(F32)
        for m, c in enumerate(peers[i], 1):
            c.wait_recv()
            total = total + from_peers[i, m - 1].astype(F32)
        if i < columns_n - 1:
            rows_out[i] = total.astype(BF16)
            c = mesh_copy(
                rows_out.at[i], from_column.at[i], column_sems, i, office.at_fsdp(f)
            )
            c.start()
            column.append(c)
    for i, c in enumerate(column):
        c.wait_recv()
        total = total + from_column[i].astype(F32)
    out[...] = total
    for c in column + [c for row in peers for c in row]:
        c.wait_send()
    office.end(kinds, ins, outs)


def dense_sum(collective_id, parts, slots, gates, returned, middle, *jobs):
    sizes = tuple(lax.axis_size(a) for a in DENSE)
    hi, ep, cp = sizes
    column = hi * ep // 2
    rows = parts[0].shape[0] // (hi * ep * cp)
    width = sum(p.shape[1] for p in parts)
    kinds, arrays, shapes = courier_jobs(sizes, jobs)
    hbm = pl.BlockSpec(memory_space=pl.ANY)
    vmem = pl.BlockSpec(memory_space=pltpu.VMEM)

    def sems(count):
        return [pltpu.SemaphoreType.DMA((count,))] * 2

    return pl.pallas_call(
        functools.partial(dense_sum_kernel, sizes, kinds, len(parts)),
        out_shape=[
            jax.ShapeDtypeStruct((rows, width), F32),
            jax.ShapeDtypeStruct(middle.shape, BF16),
        ]
        + shapes,
        in_specs=[vmem] * 2 + [hbm] * (2 + len(parts) + len(jobs)),
        out_specs=[vmem] * 2 + [hbm] * len(jobs),
        scratch_shapes=[
            pltpu.VMEM((column, cp, rows, width), BF16),
            pltpu.VMEM((column, cp, rows, width), BF16),
            pltpu.VMEM((column, cp, rows, width), BF16),
            pltpu.VMEM((column, cp - 1, rows, width), BF16),
            pltpu.VMEM((column - 1, rows, width), BF16),
            pltpu.VMEM((column - 1, rows, width), BF16),
            pltpu.VMEM(returned.shape, BF16),
            pltpu.VMEM(middle.shape, F32),
        ]
        + post_scratch(jobs_messages(kinds, *sizes), len(jobs))
        + [pltpu.SemaphoreType.DMA((column * len(parts),)), pltpu.SemaphoreType.DMA((2,))]
        + sems(column * len(parts))
        + sems(column * (cp - 1))
        + sems(column - 1),
        compiler_params=pltpu.CompilerParams(
            collective_id=collective_id, has_side_effects=True, vmem_limit_bytes=56 * 2**20
        ),
    )(slots, gates, returned, middle, *(p.reshape(-1, rows, p.shape[1]) for p in parts), *arrays)


def swap(x):
    hi = lax.axis_size("hi")
    xs = x if isinstance(x, list) else [x] * (hi - 1)
    return [
        lax.ppermute(xs[k - 1], "hi", [(i, (i + k) % hi) for i in range(hi)]) for k in range(1, hi)
    ]


def after(k):
    return lax.rem(lax.axis_index("hi") + k, lax.axis_size("hi"))


def half_rows(x):
    rows = x.shape[0] // lax.axis_size("hi")
    parts = [
        lax.dynamic_slice_in_dim(x, after(k) * rows, rows, axis=0)
        for k in range(lax.axis_size("hi"))
    ]
    return parts[0], parts[1:]


def expert_kernel(
    sizes,
    group,
    x_hbm,
    dy_hbm,
    gate_hbm,
    up_hbm,
    down_hbm,
    scale_ref,
    back_ref,
    inner_ref,
    e_ref,
    gate_out,
    up_out,
    down_out,
    x_s,
    dy_s,
    gate_w,
    up_w,
    down_w,
    hidden_s,
    dg_s,
    du_s,
    back_s,
    inner_s,
    e_s,
    load_sem,
    weight_sem,
    send,
    recv,
    out_sem,
):
    _, ep, cp = sizes
    n, cap, width = x_hbm.shape
    depth = hidden_s.shape[1]
    me = lax.axis_index("cp") * ep + lax.axis_index("ep")

    def source(k):
        return partner(me, k, n)

    def device(at):
        return {"cp": at // ep, "ep": lax.rem(at, ep)}

    barrier = pltpu.get_barrier_semaphore()
    for k in range(n - 1):
        pl.semaphore_signal(
            barrier, inc=1, device_id=device(source(k)), device_id_type=pl.DeviceIdType.MESH
        )
    weights = [
        pltpu.make_async_copy(src, dst, weight_sem.at[i])
        for i, (src, dst) in enumerate(
            ((gate_hbm, gate_w), (up_hbm, up_w), (down_hbm, down_w))
        )
    ]
    loads = []
    for c in weights[:2]:
        c.start()
    for k in range(n):
        pair = [
            pltpu.make_async_copy(src.at[source(k)], dst.at[k], load_sem.at[2 * k + i])
            for i, (src, dst) in enumerate(((x_hbm, x_s), (dy_hbm, dy_s)))
        ]
        for c in pair:
            c.start()
        loads.append(pair)
    weights[2].start()
    for pair in loads:
        for c in pair:
            c.wait()
    for c in weights:
        c.wait()
    pl.semaphore_wait(barrier, n - 1)

    def away(k, src, dst, lane):
        return pltpu.make_async_remote_copy(
            src_ref=src.at[k],
            dst_ref=dst.at[me],
            send_sem=send.at[2 * k + lane],
            recv_sem=recv.at[2 * k + lane],
            device_id=device(source(k)),
            device_id_type=pl.DeviceIdType.MESH,
        )

    def here(src, dst, lane):
        return pltpu.make_async_copy(src.at[n - 1], dst.at[me], out_sem.at[lane])

    def keep_e(k):
        return pltpu.make_async_copy(e_s.at[k], e_ref.at[source(k)], out_sem.at[2 + k])

    tile = group * cap
    chunk = min(512, depth)

    @pl.loop(0, n // group)
    def _(t):
        first = pl.multiple_of(t * tile, tile)
        at = pl.ds(first, tile)
        k0 = t * group
        x = x_s[pl.ds(k0, group)].reshape(tile, width)
        dy = dy_s[pl.ds(k0, group)].reshape(tile, width)
        inner = jnp.zeros((tile, 1), F32)
        for f in range(0, depth, chunk):
            cols = slice(f, f + chunk)
            gate_pre = dot(x, gate_w[:, cols])
            up_pre = dot(x, up_w[:, cols])
            sigmoid_gate = jax.nn.sigmoid(gate_pre)
            swish = gate_pre * sigmoid_gate
            hidden = (swish * up_pre).astype(BF16)
            hidden_s[at, cols] = hidden
            hidden_grad = dot(dy, down_w[cols, :], 1, 1)
            inner = inner + jnp.sum(hidden_grad * hidden.astype(F32), axis=1, keepdims=True)
            slope = sigmoid_gate * (1.0 + gate_pre * (1.0 - sigmoid_gate))
            dg_s[at, cols] = (hidden_grad * up_pre * slope).astype(BF16)
            du_s[at, cols] = (hidden_grad * swish).astype(BF16)
        inner_s[pl.ds(k0, group)] = three_parts(inner).reshape(group, cap, 128)
        for d in range(0, width, 512):
            cols = slice(d, d + 512)
            back = dot(dg_s[at, :], gate_w[cols, :], 1, 1) + dot(du_s[at, :], up_w[cols, :], 1, 1)
            back_s[pl.ds(k0, group), :, cols] = back.astype(BF16).reshape(group, cap, 512)
        for i in range(group):
            k = k0 + i

            @pl.when(k < n - 1)
            def _():
                away(k, back_s, back_ref, 0).start()
                away(k, inner_s, inner_ref, 1).start()

        for d in range(0, width, 512):
            cols = slice(d, d + 512)
            e = dot(hidden_s[at, :], down_w[:, cols])
            e_s[pl.ds(k0, group), :, cols] = e.astype(BF16).reshape(group, cap, 512)
        for i in range(group):
            keep_e(k0 + i).start()

    here(back_s, back_ref, 0).start()
    here(inner_s, inner_ref, 1).start()
    for k in range(n):
        lanes = lax.broadcasted_iota(jnp.int32, (cap, 128), 1)
        gate = jnp.sum(
            jnp.where(lanes < 3, scale_ref[source(k)].astype(F32), 0.0), axis=1, keepdims=True
        )
        x_s[k] = (x_s[k].astype(F32) * gate).astype(BF16)
        dy_s[k] = (dy_s[k].astype(F32) * gate).astype(BF16)

    @pl.loop(0, width // 256)
    def _(d):
        cols = pl.ds(pl.multiple_of(d * 256, 256), 256)
        x = x_s[:, :, cols].reshape(n * cap, 256)
        gate_out[cols, :] = dot(x, dg_s[...], 0, 0).astype(BF16)
        up_out[cols, :] = dot(x, du_s[...], 0, 0).astype(BF16)

    @pl.loop(0, depth // 256)
    def _(f):
        cols = pl.ds(pl.multiple_of(f * 256, 256), 256)
        down_out[cols, :] = dot(
            hidden_s[:, cols], dy_s[...].reshape(n * cap, width), 0, 0
        ).astype(BF16)

    here(back_s, back_ref, 0).wait()
    here(inner_s, inner_ref, 1).wait()
    for k in range(n):
        keep_e(k).wait()
    for k in range(n - 1):
        away(k, back_s, back_ref, 0).wait()
        away(k, inner_s, inner_ref, 1).wait()


def expert(collective_id, x, dy, gate, up, down, scale):
    sizes = tuple(lax.axis_size(a) for a in DENSE)
    n, cap, width = x.shape
    depth = gate.shape[1]
    hbm = pl.BlockSpec(memory_space=pl.ANY)
    vmem = pl.BlockSpec(memory_space=pltpu.VMEM)
    rows = pltpu.VMEM(x.shape, BF16)
    tall = pltpu.VMEM((n * cap, depth), BF16)

    def sems(count):
        return pltpu.SemaphoreType.DMA((count,))

    return pl.pallas_call(
        functools.partial(expert_kernel, sizes, 4),
        in_specs=[hbm] * 5 + [vmem],
        out_specs=[hbm] * 3 + [vmem] * 3,
        out_shape=[
            jax.ShapeDtypeStruct(x.shape, BF16),
            jax.ShapeDtypeStruct((n, cap, 128), BF16),
            jax.ShapeDtypeStruct(x.shape, BF16),
            jax.ShapeDtypeStruct(gate.shape, BF16),
            jax.ShapeDtypeStruct(up.shape, BF16),
            jax.ShapeDtypeStruct(down.shape, BF16),
        ],
        scratch_shapes=[
            rows,
            rows,
            pltpu.VMEM(gate.shape, BF16),
            pltpu.VMEM(up.shape, BF16),
            pltpu.VMEM(down.shape, BF16),
            tall,
            tall,
            tall,
            rows,
            pltpu.VMEM((n, cap, 128), BF16),
            rows,
            sems(2 * n),
            sems(3),
            sems(2 * n),
            sems(2 * n),
            sems(2 + n),
        ],
        compiler_params=pltpu.CompilerParams(
            collective_id=collective_id, has_side_effects=True, vmem_limit_bytes=62 * 2**20
        ),
        cost_estimate=ATTENTION_COST,
    )(x, dy, gate, up, down, scale)


def rms_backward(rows, scale, gain, grad_norm):
    weighted = grad_norm * gain
    inner = jnp.mean(weighted * rows, axis=-1, keepdims=True)
    grad_rows = scale * weighted - rows * scale * scale * scale * inner
    return grad_rows, jnp.sum(grad_norm * rows * scale, axis=0)


def with_extra(main, *columns):
    rows = main.shape[0]
    columns = [c.reshape(rows, -1).astype(main.dtype) for c in columns]
    used = sum(c.shape[1] for c in columns)
    return jnp.concatenate([main, *columns, jnp.zeros((rows, -used % 128), main.dtype)], axis=1)


def local(
    layer_input,
    cotangent,
    pairing,
    routes,
    first_gain,
    second_gain,
    query_weight,
    key_weight,
    value_weight,
    out_weight,
    router_weight,
    gate_weight,
    up_weight,
    down_weight,
):
    n_seq = layer_input.shape[0]
    width = layer_input.shape[-1]
    rows = 2 * BLK
    tokens = n_seq * rows
    cp = lax.axis_size("cp")
    here = lax.axis_index("cp")
    blocks = 2 * cp
    n_q, n_kv = H * HD, KV * HD
    n_slots = EXPERTS * n_seq * CAP

    first = with_extra(
        jnp.concatenate([query_weight, key_weight, value_weight], axis=1), first_gain
    )
    second = with_extra(out_weight, router_weight, second_gain)
    n_first = n_q + 2 * n_kv

    chosen = routes.reshape(tokens, 2)
    experts = jnp.arange(EXPERTS, dtype=jnp.int32)
    picks = chosen[:, :, None] == experts[None, None, :]
    named = jnp.any(picks, axis=1).astype(BF16)
    token = jnp.arange(tokens, dtype=jnp.int32)
    earlier = (token[None, :] < token[:, None]) & (token[None, :] // rows == token[:, None] // rows)
    before = dot(earlier.astype(BF16), named)
    rank = jnp.sum(jnp.where(picks, before[:, None, :], 0.0), axis=-1).astype(jnp.int32)
    slots = (chosen * n_seq + (token // rows)[:, None]) * CAP + rank
    slot = jnp.arange(n_slots, dtype=jnp.int32)
    at_slot = [slots[:, r][None, :] == slot[:, None] for r in range(2)]
    place_rows = (at_slot[0] | at_slot[1]).astype(BF16)
    take_rows = [(slots[:, r][:, None] == slot[None, :]).astype(BF16) for r in range(2)]

    def exchange(x):
        x = x.reshape(EXPERTS, n_seq * CAP, -1)
        x = lax.all_to_all(x, ("cp", "ep"), split_axis=0, concat_axis=0, tiled=True)
        return x.reshape(n_slots, -1)

    def exchange_scalar(x):
        x = x.reshape(EXPERTS, 1, n_seq * CAP)
        x = lax.all_to_all(x, ("cp", "ep"), split_axis=0, concat_axis=0, tiled=True)
        return x.reshape(n_slots)

    grad_rows = dot(place_rows, cotangent.reshape(tokens, width)).astype(BF16)
    resid = layer_input.reshape(tokens, width).astype(F32)
    scale_one = lax.rsqrt(jnp.mean(resid * resid, axis=-1, keepdims=True) + EPS)
    ids = jnp.stack([pairing, blocks - 1 - pairing], axis=2).reshape(n_seq, blocks)
    order = jnp.arange(blocks, dtype=jnp.int32)
    table = jnp.sum(jnp.where(ids[:, :, None] == order, order[None, :, None], 0), axis=1)
    place = lax.dynamic_index_in_dim(pairing, here, axis=1, keepdims=False)
    pick_f = picks.astype(F32)
    weights = [("expert", w) for w in (gate_weight, up_weight, down_weight)]
    if first.shape[0] % 16 == 0:
        (
            attn_in,
            queries,
            attn_out,
            middle,
            moe_in,
            gates,
            kv_all,
            first,
            second,
            arrived,
            arrived_gate,
            gate_matrix,
            up_matrix,
            down_matrix,
            grad_rows,
        ) = front(
            0,
            table,
            place,
            layer_input.reshape(tokens, width),
            chosen,
            slots.T,
            first,
            second,
            *weights,
            ("tokens", grad_rows.reshape(EXPERTS, n_seq * CAP, width)),
        )
        gates = gates[:, :2]
        first = first.reshape(width, -1)
        second = second.reshape(n_q, -1)
    else:
        second = lax.all_gather(second, DENSE, axis=0, tiled=True)
        first, gate_matrix, down_matrix = courier(0, ("gather", first), weights[0], weights[2])
        first = first.reshape(width, -1)
        attn_in = (resid * scale_one * first[:, n_first].astype(F32)).astype(BF16)
        qkv = dot(attn_in, first[:, :n_first]).astype(BF16)
        queries = qkv[:, :n_q]
        kv = qkv[:, n_q:].reshape(n_seq, rows, 2, n_kv).transpose(0, 2, 1, 3)
        kv_all, up_matrix = courier(1, ("peers", kv), weights[1])
        grad_rows = exchange(tie(grad_rows, kv_all))
        attn_out = tie(attend(table, place, queries, kv_all), grad_rows)
        middle = resid + dot(attn_out, second[:, :width])
        scale_two = lax.rsqrt(jnp.mean(middle * middle, axis=-1, keepdims=True) + EPS)
        moe_in = (middle * scale_two * second[:, width + EXPERTS].astype(F32)).astype(BF16)
        logits = dot(moe_in, second[:, width : width + EXPERTS])
        picked = jnp.sum(pick_f * logits[:, None, :], axis=-1)
        powers = jnp.exp(picked - jnp.max(picked, axis=-1, keepdims=True))
        gates = powers / jnp.sum(powers, axis=-1, keepdims=True)
        gate_slot = jnp.sum(
            sum(jnp.where(at_slot[r], gates[:, r][None, :], 0.0) for r in range(2)), axis=1
        )
        arrived = exchange(dot(place_rows, moe_in).astype(BF16))
        rest, lanes = exchange_scalar(tie(gate_slot, arrived)), []
        for _ in range(3):
            lanes.append(lax.reduce_precision(rest, 8, 7))
            rest = rest - lanes[-1]
        arrived_gate = jnp.pad(jnp.stack(lanes, axis=1).astype(BF16), ((0, 0), (0, 125)))
    qkv_matrix = first[:, :n_first]
    gain_one = first[:, n_first].astype(F32)
    out_matrix = second[:, :width]
    router_matrix = second[:, width : width + EXPERTS]
    gain_two = second[:, width + EXPERTS].astype(F32)
    scale_two = lax.rsqrt(jnp.mean(middle * middle, axis=-1, keepdims=True) + EPS)

    shape = (EXPERTS, n_seq * CAP, width)
    grad_returned, inner, produced, gate_part, up_part, down_part = expert(
        4,
        arrived.reshape(shape),
        grad_rows.reshape(shape),
        gate_matrix,
        up_matrix,
        down_matrix,
        arrived_gate.reshape(EXPERTS, -1, 128),
    )
    grad_returned = grad_returned.reshape(n_slots, width)
    gate_inner = jnp.sum(inner[:, :, :3].astype(F32), axis=2).reshape(n_slots)
    down_own, down_sent = half_rows(down_part)
    down_sent = swap(down_sent)

    returned = exchange(tie(produced, grad_returned))
    grad_final = cotangent.reshape(tokens, width).astype(F32)
    gate_inner = jnp.stack(
        [jnp.sum(jnp.where(a, gate_inner[:, None], 0.0), axis=0) for a in at_slot], axis=1
    )
    pair_grad = gates * (gate_inner - jnp.sum(gates * gate_inner, axis=-1, keepdims=True))
    logit_grad = jnp.sum(pick_f * pair_grad[:, :, None], axis=1)
    moe_in_grad = jnp.dot(logit_grad, router_matrix.astype(F32).T, precision=HIGH)
    for r in range(2):
        moe_in_grad = moe_in_grad + gates[:, r : r + 1] * dot(take_rows[r], grad_returned)
    router_part = jnp.dot(moe_in.astype(F32).T, logit_grad, precision=HIGH)
    middle_norm_grad, gain_two_grad = rms_backward(middle, scale_two, gain_two, moe_in_grad)
    middle_grad = grad_final + middle_norm_grad
    branch_grad = middle_grad.astype(BF16)
    out_part = dot(attn_out, branch_grad, 0, 0).astype(BF16)
    attn_out_grad = dot(branch_grad, out_matrix, 1, 1).astype(BF16)
    attn_out_grad = tie(attn_out_grad, out_part)
    query_grad, kv_grad, gate_parts = attend_back(
        2, table, ids, place, queries, kv_all, attn_out_grad, ("owners", gate_part)
    )
    kv_grad = tie(kv_grad, returned, *down_sent)
    kv_grad = jnp.sum(kv_grad.astype(F32), axis=0).astype(BF16)
    kv_grad = kv_grad.transpose(0, 2, 1, 3).reshape(tokens, 2 * n_kv)
    qkv_grad = jnp.concatenate([query_grad, kv_grad], axis=1)
    first_part = dot(attn_in, qkv_grad, 0, 0).astype(BF16)
    attn_in_grad = dot(qkv_grad, qkv_matrix, 1, 1)
    resid_norm_grad, gain_one_grad = rms_backward(resid, scale_one, gain_one, attn_in_grad)
    input_grad = middle_grad + resid_norm_grad
    down_sum = tie(down_own, query_grad, returned).astype(F32) + sum(d.astype(F32) for d in down_sent)
    down_sum = down_sum.astype(BF16).reshape(down_weight.shape)

    def own_sum(parts):
        halves = parts.reshape((-1,) + gate_weight.shape)
        return jnp.sum(halves.astype(F32), axis=0)

    small_part = jnp.concatenate(
        [router_part, gain_one_grad[:, None], gain_two_grad[:, None]], axis=1
    ).astype(BF16)
    small_part = jnp.pad(small_part, ((0, 0), (0, -small_part.shape[1] % 128)))
    dense, layer_output, up_parts, down_sum = dense_sum(
        3,
        [first_part, out_part, small_part],
        slots,
        gates,
        returned,
        middle,
        ("owners", up_part),
        ("quad", down_sum),
    )
    at_small = n_first + width
    return (
        layer_output.reshape(layer_input.shape),
        input_grad.reshape(layer_input.shape),
        dense[:, at_small + EXPERTS],
        dense[:, at_small + EXPERTS + 1],
        dense[:, :n_q],
        dense[:, n_q : n_q + n_kv],
        dense[:, n_q + n_kv : n_first],
        dense[:, n_first:at_small],
        dense[:, at_small : at_small + EXPERTS],
        own_sum(gate_parts),
        own_sum(up_parts),
        down_sum.astype(F32),
    )


def solution(mesh):
    fsdp, cp = mesh.shape["fsdp"], mesh.shape["cp"]
    ep = EXPERTS // cp
    finer = Mesh(mesh.devices.reshape(fsdp // ep, ep, cp), DENSE)
    rows = ("hi", "ep")
    block = P(rows, "cp", None, None, None)
    dense, vector, expert = P(DENSE, None), P(DENSE), P("cp", rows, None)
    in_specs = (block, block, P(rows, None), block) + (vector,) * 2 + (dense,) * 5 + (expert,) * 3
    out_specs = (block,) * 2 + (vector,) * 2 + (dense,) * 5 + (expert,) * 3
    return jax.shard_map(
        local, mesh=finer, in_specs=in_specs, out_specs=out_specs, check_vma=False
    )
```
